32 devices in a mesh: fsdp: 2 (over x), ctx: 4 (over z), tp: 4 (over y, core).
Axes of the slice: x: 2, y: 2, z: 4, core: 2. Of those that a mesh axis runs over, the one named last changes fastest.
Arguments:
- tokens: bfloat16 [3072, 512], P(('fsdp', 'ctx'), 'tp'), may hold values from -62 to 62
- first_expand: bfloat16 [512, 2048], P(('fsdp', 'ctx'), 'tp'), may hold values from -0.25 to 0.25
- first_shrink: bfloat16 [2048, 512], P('tp', ('fsdp', 'ctx')), may hold values from -0.25 to 0.25
- attend_input: bfloat16 [512, 3, 512], P(('fsdp', 'ctx'), None, 'tp'), may hold values from -0.25 to 0.25
- position_map: bfloat16 [512, 512], P(('fsdp', 'ctx'), 'tp'), may hold values from -0.25 to 0.25
- position_bias: float32 [2, 8, 64], P(None, 'tp'), may hold values from -4 to 4
- attend_output: bfloat16 [512, 512], P('tp', ('fsdp', 'ctx')), may hold values from -2.5 to 2.5
- gating_map: bfloat16 [512, 2, 512], P(('fsdp', 'ctx'), None, 'tp'), may hold values from -0.25 to 0.25
- depth_kernel: float32 [31, 512], P(None, 'tp'), may hold values from -1 to 1
- batch_scale: float32 [512], P('tp'), may hold values from 0.1 to 1.9
- batch_shift: float32 [512], P('tp'), may hold values from -3 to 3
- mixing_map: bfloat16 [512, 512], P('tp', ('fsdp', 'ctx')), may hold values from -0.25 to 0.25
- second_expand: bfloat16 [512, 2048], P(('fsdp', 'ctx'), 'tp'), may hold values from -0.25 to 0.25
- second_shrink: bfloat16 [2048, 512], P('tp', ('fsdp', 'ctx')), may hold values from -0.25 to 0.25
- layer_gains: float32 [5, 512], P(None, 'tp'), may hold values from 0.1 to 1.9
- cotangent: bfloat16 [3072, 512], P(('fsdp', 'ctx'), 'tp'), may hold values from -6 to 6
Outputs:
- outputs: bfloat16 [3072, 512], P(('fsdp', 'ctx'), 'tp')
- tokens_grad: float32 [3072, 512], P(('fsdp', 'ctx'), 'tp')
- first_expand_grad: float32 [512, 2048], P(('fsdp', 'ctx'), 'tp')
- first_shrink_grad: float32 [2048, 512], P('tp', ('fsdp', 'ctx'))
- attend_input_grad: float32 [512, 3, 512], P(('fsdp', 'ctx'), None, 'tp')
- position_map_grad: float32 [512, 512], P(('fsdp', 'ctx'), 'tp')
- position_bias_grad: float32 [2, 8, 64], P(None, 'tp')
- attend_output_grad: float32 [512, 512], P('tp', ('fsdp', 'ctx'))
- gating_map_grad: float32 [512, 2, 512], P(('fsdp', 'ctx'), None, 'tp')
- depth_kernel_grad: float32 [31, 512], P(None, 'tp')
- batch_scale_grad: float32 [512], P('tp')
- batch_shift_grad: float32 [512], P('tp')
- mixing_map_grad: float32 [512, 512], P('tp', ('fsdp', 'ctx'))
- second_expand_grad: float32 [512, 2048], P(('fsdp', 'ctx'), 'tp')
- second_shrink_grad: float32 [2048, 512], P('tp', ('fsdp', 'ctx'))
- layer_gains_grad: float32 [5, 512], P(None, 'tp')
The draws below stay inside these ranges and needn't reach their ends.
All inputs are finite; a program needn't handle non-finite values.
Results may differ from the reference program's by a relative error of at most 0.04.
Values may be sent and summed in bfloat16 or wider, within the bound.
No kernel may reach another device: no remote copies, remote signals or barrier semaphores. Data moves between devices by JAX's collectives and lax.ppermute only.
A program may use at most 128 MiB of HBM per device.

```python
import math
import jax
import jax.numpy as jnp
from jax import lax

D = 512
H = 8
HD = 64
FF = 2048
KW = 31
FR_DEV = 384
LENGTH = 1536
TOKENS = 3072


def draw_tokens(key, part):
    key = jax.random.fold_in(key, 11)
    noise_key, column_key, row_key = jax.random.split(key, 3)
    place = jnp.arange(TOKENS, dtype=jnp.float32) / (TOKENS - 1)
    feature = jnp.arange(D, dtype=jnp.float32) / (D - 1)
    common = 1.0 + 2.0 * feature
    column = jnp.exp(jax.random.uniform(column_key, (D,), jnp.float32, -1.15, 1.15))
    row_scale = jnp.exp(jax.random.uniform(row_key, (TOKENS, 1), jnp.float32, -1.15, 1.15))
    noise = jnp.clip(jax.random.normal(noise_key, (TOKENS, D), jnp.float32), -5.0, 5.0)
    lift = 0.3 + 0.9 * place
    return (row_scale * (column[None, :] * noise + lift[:, None] * common[None, :])).astype(jnp.bfloat16)


def block_levels(key, extent, cuts, low, largest):
    factor_of, own = 1.0, jax.random.fold_in(key, 6)
    for axis_at, parts in cuts:
        steps = jnp.exp(jax.random.uniform(jax.random.fold_in(own, axis_at), (parts,), jnp.float32, low / len(cuts), largest / len(cuts)))
        factor_of = factor_of * jnp.repeat(steps, extent[axis_at] // parts).reshape([-1 if axis == axis_at else 1 for axis in range(len(extent))])
    return factor_of


def normal_values(stream_key, shape, spread, most, shards=(), held_as=jnp.bfloat16):
    values = spread * jax.random.normal(stream_key, shape, jnp.float32)
    if shards:
        values = values * block_levels(stream_key, shape, shards, -0.22, 0.18)
    return jnp.clip(values, -most, most).astype(held_as)


def setup_inputs(seed: int = 0) -> dict:
    key_list = jax.random.split(jax.random.key(seed), 17)
    return {
        "tokens": draw_tokens(jax.random.fold_in(key_list[16], 71), 0),
        "first_expand": normal_values(key_list[1], (D, FF), D ** -0.5, 0.25, ((0, 8), (1, 4))),
        "first_shrink": normal_values(key_list[2], (FF, D), (FF // 4) ** -0.5, 0.25, ((0, 4), (1, 8))),
        "attend_input": normal_values(key_list[3], (D, 3, D), D ** -0.5, 0.25, ((0, 8), (2, 4))),
        "position_map": normal_values(key_list[4], (D, D), D ** -0.5, 0.25, ((0, 8), (1, 4))),
        "position_bias": normal_values(key_list[5], (2, H, HD), 1.0, 4.0, ((1, 4),), jnp.float32),
        "attend_output": normal_values(key_list[6], (D, D), (max(1, D * 16 // LENGTH)) ** -0.5, 2.5, ((0, 4), (1, 8))),
        "gating_map": normal_values(key_list[7], (D, 2, D), D ** -0.5, 0.25, ((0, 8), (2, 4))),
        "depth_kernel": normal_values(key_list[8], (KW, D), KW ** -0.5, 1.0, ((1, 4),), jnp.float32),
        "batch_scale": jnp.clip(1.0 + 0.18 * jax.random.normal(key_list[9], (D,), jnp.float32), 0.1, 1.9),
        "batch_shift": normal_values(key_list[10], (D,), 0.5, 3.0, ((0, 4),), jnp.float32),
        "mixing_map": normal_values(key_list[11], (D, D), D ** -0.5, 0.25, ((0, 4), (1, 8))),
        "second_expand": normal_values(key_list[12], (D, FF), D ** -0.5, 0.25, ((0, 8), (1, 4))),
        "second_shrink": normal_values(key_list[13], (FF, D), (FF // 4) ** -0.5, 0.25, ((0, 4), (1, 8))),
        "layer_gains": jnp.clip(1.0 + 0.18 * jax.random.normal(key_list[14], (5, D), jnp.float32), 0.1, 1.9),
        "cotangent": normal_values(key_list[15], (TOKENS, D), 1.0, 6.0, ((0, 8), (1, 4))),
    }


@jax.custom_vjp
def low(v):
    return lax.optimization_barrier(v.astype(jnp.bfloat16)).astype(jnp.float32)

@jax.custom_vjp
def low_back(v):
    return v

def low_keep(v):
    return (low(v), None)

def low_pass(kept, grad):
    return (grad,)

def back_keep(v):
    return (v, None)

def back_low(kept, grad):
    return (low(grad),)
low.defvjp(low_keep, low_pass)
low_back.defvjp(back_keep, back_low)
EPSILON = 1e-05
HIGHEST = lax.Precision.HIGHEST

def swished(value):
    return value * jax.nn.sigmoid(value)

def layer_norm(stream, gain):
    centre = lax.optimization_barrier(jnp.mean(stream, axis=1, keepdims=True))
    centred = stream - centre
    variance = lax.optimization_barrier(jnp.mean(centred * centred, axis=1, keepdims=True))
    return centred * lax.rsqrt(variance + EPSILON) * gain

def sinusoid(places, width):
    half = jnp.arange(width // 2, dtype=jnp.float32)
    rates = jnp.exp(half * (-2.0 * math.log(10000.0) / width))
    angles = places[:, None] * rates[None, :]
    return jnp.stack([jnp.sin(angles), jnp.cos(angles)], axis=2).reshape(places.shape[0], width)

def diagonal_shift(wide, key_count):
    heads, rows, width = wide.shape
    flat = jnp.pad(wide, ((0, 0), (0, 0), (0, 1))).reshape(heads, rows * (width + 1))
    flat = lax.slice_in_dim(flat, rows - 1, rows - 1 + rows * width, axis=1)
    return flat.reshape(heads, rows, width)[:, :, :key_count]

def feed(stream, gain, expand, shrink):
    normed = low(layer_norm(stream, gain))
    inner = low_back(jnp.dot(normed, expand, precision=HIGHEST))
    hidden = low(swished(inner))
    return low_back(jnp.dot(hidden, shrink, precision=HIGHEST))

def attend_block(block_a, block_b, start, seq_keys, seq_values, position_map):
    rows = block_a.shape[0]
    length = seq_keys.shape[0]
    places = (start + rows - 1 - jnp.arange(rows + length - 1, dtype=jnp.int32)).astype(jnp.float32)
    embed = low(sinusoid(places, D))
    relative = low(low_back(jnp.dot(embed, position_map, precision=HIGHEST))).reshape(-1, H, HD)
    content = jnp.einsum('rhe,khe->hrk', block_a, seq_keys, precision=HIGHEST)
    wide = jnp.einsum('rhe,whe->hrw', block_b, relative, precision=HIGHEST)
    scores = low_back((content + diagonal_shift(wide, length)) * HD ** (-0.5))
    weights = jax.nn.softmax(scores, axis=2)
    return jnp.einsum('hrk,khe->rhe', low(weights), seq_values, precision=HIGHEST)

def forward(tokens, first_expand, first_shrink, attend_input, position_map, position_bias, attend_output, gating_map, depth_kernel, batch_scale, batch_shift, mixing_map, second_expand, second_shrink, layer_gains):
    count = tokens.shape[0] // LENGTH
    blocks = LENGTH // FR_DEV
    stream = tokens + 0.5 * feed(tokens, layer_gains[0], first_expand, first_shrink)
    normed = low(layer_norm(stream, layer_gains[1]))
    project = low_back(jnp.dot(normed, attend_input.reshape(D, 3 * D), precision=HIGHEST)).reshape(-1, 3, H, HD)
    query = project[:, 0]
    keys = low(project[:, 1])
    values = low(project[:, 2])
    query_a = low(query + position_bias[0])
    query_b = low(query + position_bias[1])
    starts = jnp.arange(blocks, dtype=jnp.int32) * FR_DEV

    def per_sequence(items):
        seq_a, seq_b, seq_keys, seq_values = items

        def per_block(inner):
            block_a, block_b, start = inner
            return attend_block(block_a, block_b, start, seq_keys, seq_values, position_map)
        return lax.map(jax.checkpoint(per_block), (seq_a.reshape(blocks, FR_DEV, H, HD), seq_b.reshape(blocks, FR_DEV, H, HD), starts))
    attended = lax.map(per_sequence, (query_a.reshape(count, LENGTH, H, HD), query_b.reshape(count, LENGTH, H, HD), keys.reshape(count, LENGTH, H, HD), values.reshape(count, LENGTH, H, HD)))
    mixed = low(low_back(attended.reshape(-1, D)))
    stream = stream + low_back(jnp.dot(mixed, attend_output, precision=HIGHEST))
    normed = low(layer_norm(stream, layer_gains[2]))
    paired = low_back(jnp.dot(normed, gating_map.reshape(D, 2 * D), precision=HIGHEST)).reshape(-1, 2, D)
    gated = low(paired[:, 0] * jax.nn.sigmoid(paired[:, 1]))
    halo = (KW - 1) // 2
    padded = jnp.pad(gated.reshape(count, LENGTH, D), ((0, 0), (halo, halo), (0, 0)))
    convolved = jnp.zeros((count, LENGTH, D), jnp.float32)
    for offset in range(KW):
        convolved = convolved + depth_kernel[offset] * padded[:, offset:offset + LENGTH]
    convolved = low_back(convolved.reshape(-1, D))
    centre = lax.optimization_barrier(jnp.mean(convolved, axis=0))
    centred = convolved - centre
    variance = lax.optimization_barrier(jnp.mean(centred * centred, axis=0))
    normal = centred * lax.rsqrt(variance + EPSILON)
    active = low(swished(normal * batch_scale + batch_shift))
    stream = stream + low_back(jnp.dot(active, mixing_map, precision=HIGHEST))
    stream = stream + 0.5 * feed(stream, layer_gains[3], second_expand, second_shrink)
    return layer_norm(stream, layer_gains[4])

def reference(tokens, first_expand, first_shrink, attend_input, position_map, position_bias, attend_output, gating_map, depth_kernel, batch_scale, batch_shift, mixing_map, second_expand, second_shrink, layer_gains, cotangent):
    result, pullback = jax.vjp(forward, tokens.astype(jnp.float32), first_expand.astype(jnp.float32), first_shrink.astype(jnp.float32), attend_input.astype(jnp.float32), position_map.astype(jnp.float32), position_bias.astype(jnp.float32), attend_output.astype(jnp.float32), gating_map.astype(jnp.float32), depth_kernel.astype(jnp.float32), batch_scale.astype(jnp.float32), batch_shift.astype(jnp.float32), mixing_map.astype(jnp.float32), second_expand.astype(jnp.float32), second_shrink.astype(jnp.float32), layer_gains.astype(jnp.float32))
    grads = pullback(cotangent.astype(jnp.float32))
    return (result.astype(jnp.bfloat16), grads[0], grads[1], grads[2], grads[3], grads[4], grads[5], grads[6], grads[7], grads[8], grads[9], grads[10], grads[11], grads[12], grads[13], grads[14])
```

```python
import functools
import math

import jax
import jax.numpy as jnp
from jax import lax
from jax.experimental import pallas as pl
from jax.experimental.pallas import tpu as pltpu
from jax.sharding import PartitionSpec as P

F32 = jnp.float32
BF16 = jnp.bfloat16
EPSILON = 1e-05
HALO = 16
BLOCK = 128
VMEM_BYTES = 40 * 1024 * 1024


def call(body, outs, *args, scratch=(), flops=0, vmem=VMEM_BYTES):
    outs = [jax.ShapeDtypeStruct(shape, dtype) for shape, dtype in outs]
    moved = sum(a.size * a.dtype.itemsize for a in list(args[1:]) + outs)
    return pl.pallas_call(
        body,
        out_shape=outs,
        in_specs=[pl.BlockSpec(memory_space=pltpu.SMEM)]
        + [pl.BlockSpec(memory_space=pltpu.VMEM)] * (len(args) - 1),
        out_specs=[pl.BlockSpec(memory_space=pltpu.VMEM)] * len(outs),
        scratch_shapes=list(scratch),
        compiler_params=pltpu.CompilerParams(vmem_limit_bytes=vmem),
        cost_estimate=pl.CostEstimate(
            flops=int(flops), bytes_accessed=int(moved), transcendentals=0
        ),
    )(*args)


def dot(left, right):
    return jnp.dot(left, right, preferred_element_type=F32)


def dot_cols(left, right):
    return lax.dot_general(left, right, (((1,), (1,)), ((), ())), preferred_element_type=F32)


def dot_rows(left, right):
    return lax.dot_general(left, right, (((0,), (0,)), ((), ())), preferred_element_type=F32)


def normalized(stream):
    centred = stream - jnp.mean(stream, axis=1, keepdims=True)
    spread = lax.rsqrt(jnp.mean(centred * centred, axis=1, keepdims=True) + EPSILON)
    return centred * spread, spread


def norm_pullback(grad, stream, gain):
    normal, spread = normalized(stream)
    scaled = grad * gain
    first = jnp.mean(scaled, axis=1, keepdims=True)
    second = jnp.mean(scaled * normal, axis=1, keepdims=True)
    return spread * (scaled - first - normal * second), jnp.sum(
        grad * normal, axis=0, keepdims=True
    )


def swish_slope(value, logistic):
    return logistic * (1.0 + value * (1.0 - logistic))


def halves(idx, rows):
    half = rows // 2
    mine = pl.multiple_of(idx[1] * half, half)
    theirs = pl.multiple_of((1 - idx[1]) * half, half)
    return pl.ds(mine, half), pl.ds(theirs, half)


def split(idx, whole, keep, send):
    mine, theirs = halves(idx, whole.shape[0])
    keep[...] = whole[mine, :].astype(BF16)
    send[...] = whole[theirs, :].astype(BF16)


def join(idx, t_mine, t_theirs, whole):
    mine, theirs = halves(idx, whole.shape[0])
    whole[mine, :] = t_mine[...].astype(F32)
    whole[theirs, :] = t_theirs[...].astype(F32)


def xor_pairs(count, step):
    return [(i, i ^ step) for i in range(count)]


def swap(value, axis, step):
    return lax.ppermute(value, axis, xor_pairs(lax.axis_size(axis), step))


def added(left, right):
    return (left.astype(F32) + right.astype(F32)).astype(BF16)


def tp_sum(keep, send):
    count = lax.axis_size("tp")
    total = added(keep, swap(send, "tp", 1))
    step = 2
    while step < count:
        total = added(total, swap(total, "tp", step))
        step *= 2
    return total, swap(total, "tp", 1)


def place_body(idx, *refs):
    out = refs[-1]
    blocks = refs[:-1]
    ctx = len(blocks) // 2
    rows = blocks[0].shape[0]
    for at in range(2 * ctx):
        half = idx[2] if at < ctx else 1 - idx[2]
        target = half * ctx + jnp.bitwise_xor(idx[3], at % ctx)
        out[pl.ds(pl.multiple_of(target * rows, rows), rows), :] = blocks[at][...]


def wgrad_body(pairs, ordered, ctx, idx, *refs):
    out, scratch = refs[2 * pairs], refs[2 * pairs + 1]
    column = 0
    for at in range(pairs):
        left, right = refs[2 * at], refs[2 * at + 1]
        width = right.shape[1]
        product = dot_rows(left[...], right[...]).astype(BF16)
        if ordered:
            out[:, column : column + width] = product
        else:
            scratch[:, column : column + width] = product
        column += width
    if not ordered:
        rows = out.shape[0] // (2 * ctx)
        for at in range(2 * ctx):
            half = idx[2] if at < ctx else 1 - idx[2]
            source = half * ctx + jnp.bitwise_xor(idx[3], at % ctx)
            out[at * rows : (at + 1) * rows, :] = scratch[
                pl.ds(pl.multiple_of(source * rows, rows), rows), :
            ]


def feed_body(gain_at, base, joined, idx, *refs):
    if joined:
        x_ref, t1, t2, gains, weights, x_out, z_out, u_out, h_out, keep, send, work = refs
        join(idx, t1, t2, work)
        x = x_ref[...] + work[...]
        x_out[...] = x
    else:
        x_ref, gains, weights, z_out, u_out, h_out, keep, send, work = refs
        x = x_ref[...].astype(F32)
    hidden = u_out.shape[1]
    normal, unused = normalized(x)
    z = (normal * gains[gain_at : gain_at + 1, :]).astype(BF16)
    z_out[...] = z
    u = dot(z, weights[:, base : base + hidden])
    u_out[...] = u
    h = (u * jax.nn.sigmoid(u)).astype(BF16)
    h_out[...] = h
    work[...] = dot_cols(h, weights[:, base + hidden : base + 2 * hidden])
    split(idx, work, keep, send)


def attend_in_body(idx, x_ref, t1, t2, gains, weights, bias, x_out, z_out, qa, qb, kv, work):
    join(idx, t1, t2, work)
    x = x_ref[...].astype(F32) + 0.5 * work[...]
    x_out[...] = x
    normal, unused = normalized(x)
    z = (normal * gains[1:2, :]).astype(BF16)
    z_out[...] = z
    local = bias.shape[1]
    project = dot(z, weights[:, : 3 * local])
    query = project[:, :local]
    qa[...] = (query + bias[0:1, :]).astype(BF16)
    qb[...] = (query + bias[1:2, :]).astype(BF16)
    kv[...] = project[:, local:].astype(BF16)


def relative_body(base, idx, near_p, near_q, far_c, far_s, weights, embed, relative):
    step = far_c.shape[0]
    cos, sin = far_c[...], far_s[...]
    for at in range(embed.shape[0] // step):
        value = near_p[at : at + 1, :] * cos + near_q[at : at + 1, :] * sin
        embed[at * step : (at + 1) * step, :] = value.astype(BF16)
    relative[...] = dot(embed[...], weights[:, base : base + relative.shape[1]]).astype(BF16)


def position_body(heads, idx, qb, relative, out):
    rows, local = qb.shape
    size = local // heads
    length = out.shape[2]
    width = length + BLOCK
    for head in range(heads):
        columns = slice(head * size, (head + 1) * size)
        for at in range(rows // BLOCK):
            frames = slice(at * BLOCK, (at + 1) * BLOCK)
            first = rows - BLOCK * (at + 1)
            wide = dot_cols(qb[frames, columns], relative[first : first + width, columns])
            turned = pltpu.roll(wide, width - (BLOCK - 1), 1, stride=1, stride_axis=0)
            out[head, frames, :] = turned[:, :length]


def fill_pairs(idx, blocks, whole):
    rows = blocks[0].shape[0]
    for at, block in enumerate(blocks):
        target = jnp.bitwise_xor(idx[3], at)
        whole[pl.ds(pl.multiple_of(target * rows, rows), rows), :] = block[...]


def attend_body(heads, ctx, base, idx, qa, *refs):
    blocks = refs[:ctx]
    position, weights, p_out, mixed, keep, send, pairs, work = refs[ctx:]
    fill_pairs(idx, blocks, pairs)
    rows, local = qa.shape
    size = local // heads
    scale = size**-0.5
    for head in range(heads):
        columns = slice(head * size, (head + 1) * size)
        values = slice(local + head * size, local + (head + 1) * size)
        for at in range(rows // BLOCK):
            frames = slice(at * BLOCK, (at + 1) * BLOCK)
            scores = (dot_cols(qa[frames, columns], pairs[:, columns]) + position[head, frames, :]) * scale
            raised = jnp.exp(scores - jnp.max(scores, axis=1, keepdims=True))
            share = (raised / jnp.sum(raised, axis=1, keepdims=True)).astype(BF16)
            p_out[head, frames, :] = share
            mixed[frames, columns] = dot(share, pairs[:, values]).astype(BF16)
    work[...] = dot_cols(mixed[...], weights[:, base : base + local])
    split(idx, work, keep, send)


def conv_in_body(idx, x_ref, t1, t2, gains, weights, x_out, z_out, g_out, glu, first, last, work):
    join(idx, t1, t2, work)
    x = x_ref[...] + work[...]
    x_out[...] = x
    normal, unused = normalized(x)
    z = (normal * gains[2:3, :]).astype(BF16)
    z_out[...] = z
    rows, channels = glu.shape
    paired = dot(z, weights[:, : 2 * channels])
    g_out[...] = paired
    gated = (paired[:, :channels] * jax.nn.sigmoid(paired[:, channels:])).astype(BF16)
    glu[...] = gated
    first[...] = gated[:HALO, :]
    last[...] = gated[rows - HALO :, :]


def fill_padded(low, own, high, padded):
    rows = own.shape[0]
    padded[:HALO, :] = low[...].astype(F32)
    padded[HALO : HALO + rows, :] = own[...].astype(F32)
    padded[HALO + rows :, :] = high[...].astype(F32)


def conv_body(idx, glu, low, high, kernel, c_out, stats, padded):
    fill_padded(low, glu, high, padded)
    rows = glu.shape[0]
    taps = kernel.shape[0]
    shift = HALO - (taps - 1) // 2
    total = kernel[0:1, :] * padded[shift : shift + rows, :]
    for tap in range(1, taps):
        total = total + kernel[tap : tap + 1, :] * padded[shift + tap : shift + tap + rows, :]
    c_out[...] = total
    mean = jnp.mean(total, axis=0, keepdims=True)
    centred = total - mean
    stats[0:1, :] = mean
    stats[1:2, :] = jnp.sum(centred * centred, axis=0, keepdims=True)
    stats[2:, :] = jnp.zeros((stats.shape[0] - 2, stats.shape[1]), F32)


def batch_body(base, idx, c, stats, params, weights, q_out, act_out, keep, send, work):
    spread = stats[1:2, :]
    q = (c[...] - stats[0:1, :]) * spread
    q_out[...] = q
    a = q * params[0:1, :] + params[1:2, :]
    act = (a * jax.nn.sigmoid(a)).astype(BF16)
    act_out[...] = act
    work[...] = dot_cols(act, weights[:, base : base + act.shape[1]])
    split(idx, work, keep, send)


def feed_pullback(idx, grad, u, weights, base, f_out, du_out, keep, send, work):
    hidden = u.shape[1]
    f = (0.5 * grad).astype(BF16)
    f_out[...] = f
    value = u[...]
    logistic = jax.nn.sigmoid(value)
    back = dot(f, weights[:, base + hidden : base + 2 * hidden])
    du = (back * swish_slope(value, logistic)).astype(BF16)
    du_out[...] = du
    work[...] = dot_cols(du, weights[:, base : base + hidden])
    split(idx, work, keep, send)


def final_body(base, idx, x_ref, t1, t2, gains, cot, u, weights, y_out, d_out, gain_out, f_out, du_out, keep, send, work):
    join(idx, t1, t2, work)
    x = x_ref[...] + 0.5 * work[...]
    normal, unused = normalized(x)
    gain = gains[4:5, :]
    work[...] = normal * gain
    width = y_out.shape[1]
    y_out[...] = work[:, pl.ds(pl.multiple_of(idx[0] * width, width), width)].astype(BF16)
    grad, gain_grad = norm_pullback(cot[...].astype(F32), x, gain)
    gain_out[...] = gain_grad
    d_out[...] = grad
    feed_pullback(idx, grad, u, weights, base, f_out, du_out, keep, send, work)


def conv_back_body(base, idx, x_ref, d_ref, t1, t2, gains, q, params, weights, d_out, f_out, da_out, sums, first, last, gain_out, work):
    join(idx, t1, t2, work)
    grad, gain_grad = norm_pullback(work[...], x_ref[...], gains[3:4, :])
    gain_out[...] = gain_grad
    grad = d_ref[...] + grad
    d_out[...] = grad
    f = grad.astype(BF16)
    f_out[...] = f
    rows, channels = q.shape
    value = q[...]
    a = value * params[0:1, :] + params[1:2, :]
    da = dot(f, weights[:, base : base + channels]) * swish_slope(a, jax.nn.sigmoid(a))
    da_out[...] = da
    sums[0:1, :] = jnp.sum(da * value, axis=0, keepdims=True)
    sums[1:2, :] = jnp.sum(da, axis=0, keepdims=True)
    sums[2:, :] = jnp.zeros((sums.shape[0] - 2, channels), F32)
    first[:HALO, :] = da[:HALO, :]
    first[HALO:, :] = value[:HALO, :]
    last[:HALO, :] = da[rows - HALO :, :]
    last[HALO:, :] = value[rows - HALO :, :]


def gate_back_body(ctx, counted, idx, da, q, low, high, sums, stats, params, kernel, paired, weights, dc_out, dg_out, keep, send, padded, work):
    rows, channels = q.shape
    factor = stats[1:2, :] * params[0:1, :]
    mean_scale = sums[0:1, :] / counted
    mean_shift = sums[1:2, :] / counted

    def centred(grad, normal):
        return (factor * (grad - mean_shift - normal * mean_scale)).astype(BF16)

    dc = centred(da[...], q[...])
    dc_out[...] = dc
    before = (idx[3] > 0).astype(F32)
    after = (idx[3] < ctx - 1).astype(F32)
    padded[:HALO, :] = centred(low[:HALO, :], low[HALO:, :]).astype(F32) * before
    padded[HALO : HALO + rows, :] = dc.astype(F32)
    padded[HALO + rows :, :] = centred(high[:HALO, :], high[HALO:, :]).astype(F32) * after
    taps = kernel.shape[0]
    top = HALO + (taps - 1) // 2
    total = kernel[0:1, :] * padded[top : top + rows, :]
    for tap in range(1, taps):
        total = total + kernel[tap : tap + 1, :] * padded[top - tap : top - tap + rows, :]
    logistic = jax.nn.sigmoid(paired[:, channels:])
    through = total * logistic
    dg_out[:, :channels] = through.astype(BF16)
    dg_out[:, channels:] = (through * paired[:, :channels] * (1.0 - logistic)).astype(BF16)
    work[...] = dot_cols(dg_out[...], weights[:, : 2 * channels])
    split(idx, work, keep, send)


def taps_body(idx, glu, low, high, dc, out, padded):
    fill_padded(low, glu, high, padded)
    rows = glu.shape[0]
    grad = dc[...].astype(F32)
    shift = HALO - (out.shape[0] - 1) // 2
    for tap in range(out.shape[0]):
        out[tap : tap + 1, :] = jnp.sum(
            grad * padded[shift + tap : shift + tap + rows, :], axis=0, keepdims=True
        )


def attend_back_body(heads, ctx, base, idx, x_ref, d_ref, t1, t2, gains, weights, p, qa, *refs):
    blocks = refs[:ctx]
    d_out, f_out, gain_out, ds_out, dqa = refs[ctx : ctx + 5]
    out_blocks = refs[ctx + 5 : 2 * ctx + 5]
    pairs, grads, do, work = refs[2 * ctx + 5 :]
    fill_pairs(idx, blocks, pairs)
    join(idx, t1, t2, work)
    grad, gain_grad = norm_pullback(work[...], x_ref[...], gains[2:3, :])
    gain_out[...] = gain_grad
    grad = d_ref[...] + grad
    d_out[...] = grad
    f = grad.astype(BF16)
    f_out[...] = f
    rows, local = qa.shape
    size = local // heads
    scale = size**-0.5
    do[...] = dot(f, weights[:, base : base + local]).astype(BF16)
    for head in range(heads):
        columns = slice(head * size, (head + 1) * size)
        values = slice(local + head * size, local + (head + 1) * size)
        for at in range(rows // BLOCK):
            frames = slice(at * BLOCK, (at + 1) * BLOCK)
            dp = dot_cols(do[frames, columns], pairs[:, values])
            share = p[head, frames, :].astype(F32)
            balance = jnp.sum(share * dp, axis=1, keepdims=True)
            ds = (share * (dp - balance)).astype(BF16)
            ds_out[head, frames, :] = ds
            dqa[frames, columns] = dot(ds, pairs[:, columns]) * scale
        grads[:, columns] = (dot_rows(ds_out[head], qa[:, columns]) * scale).astype(BF16)
        grads[:, values] = dot_rows(p[head], do[:, columns]).astype(BF16)
    for at, block in enumerate(out_blocks):
        source = jnp.bitwise_xor(idx[3], at)
        block[...] = grads[pl.ds(pl.multiple_of(source * rows, rows), rows), :]


def position_back_body(heads, idx, ds, qb, relative, dqb, dr_out, wide, total):
    rows, local = qb.shape
    size = local // heads
    length = ds.shape[2]
    width = length + BLOCK
    scale = size**-0.5
    down = lax.broadcasted_iota(jnp.int32, (BLOCK, BLOCK), 0)
    across = lax.broadcasted_iota(jnp.int32, (BLOCK, BLOCK), 1)
    flip = (down + across == BLOCK - 1).astype(BF16)
    total[...] = jnp.zeros(total.shape, F32)
    wide[:, length:] = jnp.zeros((BLOCK, BLOCK), F32)
    for head in range(heads):
        columns = slice(head * size, (head + 1) * size)
        for at in range(rows // BLOCK):
            frames = slice(at * BLOCK, (at + 1) * BLOCK)
            first = rows - BLOCK * (at + 1)
            wide[:, :length] = dot(flip, ds[head, frames, :])
            turned = pltpu.roll(wide[...], 0, 1, stride=1, stride_axis=0).astype(BF16)
            turned_b = dot(turned, relative[first : first + width, columns]) * scale
            dqb[frames, columns] = jnp.dot(
                flip.astype(F32), turned_b, precision=lax.Precision.HIGHEST, preferred_element_type=F32
            )
            flipped = dot(flip, qb[frames, columns]).astype(BF16)
            total[first : first + width, columns] += dot_rows(turned, flipped)
    dr_out[...] = (total[...] * scale).astype(BF16)


def attend_out_body(ctx, idx, dqa, dqb, *refs):
    blocks = refs[:ctx]
    weights, dp_out, bias_out, keep, send, work = refs[ctx:]
    local = dqa.shape[1]
    bias_out[0:1, :] = jnp.sum(dqa[...], axis=0, keepdims=True)
    bias_out[1:2, :] = jnp.sum(dqb[...], axis=0, keepdims=True)
    dp_out[:, :local] = (dqa[...] + dqb[...]).astype(BF16)
    total = blocks[0][...].astype(F32)
    for block in blocks[1:]:
        total = total + block[...].astype(F32)
    dp_out[:, local:] = total.astype(BF16)
    work[...] = dot_cols(dp_out[...], weights[:, : 3 * local])
    split(idx, work, keep, send)


def feed_back_body(idx, x_ref, d_ref, t1, t2, gains, u, x0, weights, d_out, f_out, du_out, gain_out, last_gain, keep, send, work):
    join(idx, t1, t2, work)
    grad, gain_grad = norm_pullback(work[...], x_ref[...], gains[1:2, :])
    gain_out[...] = gain_grad
    grad = d_ref[...] + grad
    d_out[...] = grad
    feed_pullback(idx, grad, u, weights, 0, f_out, du_out, keep, send, work)
    normal, unused = normalized(x0[...].astype(F32))
    last_gain[...] = jnp.sum(work[...] * normal, axis=0, keepdims=True)


def last_body(idx, x_ref, d_ref, t1, t2, gains, out, work):
    join(idx, t1, t2, work)
    grad, unused = norm_pullback(work[...], x_ref[...].astype(F32), gains[0:1, :])
    work[...] = d_ref[...] + grad
    width = out.shape[1]
    out[...] = work[:, pl.ds(pl.multiple_of(idx[0] * width, width), width)]


FRAMES = ("fsdp", "ctx")


def paired_mesh():
    return lax.axis_size("fsdp") == 2


def gathered(idx, shard):
    if not paired_mesh():
        return lax.all_gather(shard, FRAMES, axis=0, tiled=True)
    ctx = lax.axis_size("ctx")
    mine = [shard] + [swap(shard, "ctx", step) for step in range(1, ctx)]
    theirs = [swap(block, "fsdp", 1) for block in mine]
    rows, width = shard.shape
    return call(place_body, [((2 * ctx * rows, width), BF16)], idx, *mine, *theirs)[0]


def weight_grads(idx, pairs, ordered):
    depth = pairs[0][0].shape[1]
    width = sum(right.shape[1] for unused, right in pairs)
    flat = [array for pair in pairs for array in pair]
    ctx = lax.axis_size("ctx")
    flops = sum(2 * left.shape[0] * depth * right.shape[1] for left, right in pairs)
    return call(
        functools.partial(wgrad_body, len(pairs), ordered, ctx),
        [((depth, width), BF16)],
        idx,
        *flat,
        scratch=[pltpu.VMEM((8, 128) if ordered else (depth, width), BF16)],
        flops=flops,
    )[0]


def scattered(idx, pairs, direct):
    direct = direct and paired_mesh()
    grads = weight_grads(idx, pairs, not direct)
    if not direct:
        return lax.psum_scatter(grads, FRAMES, scatter_dimension=0, tiled=True).astype(F32)
    ctx = lax.axis_size("ctx")
    half = grads.shape[0] // 2
    rows = half // ctx
    total = added(grads[:half], swap(grads[half:], "fsdp", 1))
    parts = [total[:rows]]
    for step in range(1, ctx):
        parts.append(swap(total[step * rows : (step + 1) * rows], "ctx", step))
    return sum(part.astype(F32) for part in parts)


def over_frames(value, merge):
    for axis in ("fsdp", "ctx"):
        step = 1
        while step < lax.axis_size(axis):
            value = merge(value, swap(value, axis, step))
            step *= 2
    return value


def summed(value):
    return over_frames(value, lambda left, right: left + right)


def pooled(stats, rows):
    count = [rows]

    def merge(left, right):
        gap = left[0:1] - right[0:1]
        mean = 0.5 * (left[0:1] + right[0:1])
        squares = left[1:2] + right[1:2] + gap * gap * (0.5 * count[0])
        count[0] *= 2
        return jnp.concatenate([mean, squares, left[2:]], axis=0)

    stats = over_frames(stats, merge)
    spread = lax.rsqrt(stats[1:2] / count[0] + EPSILON)
    return jnp.concatenate([stats[0:1], spread, stats[2:]], axis=0)


def neighbours(first, last):
    count = lax.axis_size("ctx")
    up = [(i, i + 1) for i in range(count - 1)]
    down = [(i + 1, i) for i in range(count - 1)]
    return lax.ppermute(last, "ctx", up), lax.ppermute(first, "ctx", down)


def angle_tables(start, rows, width, features):
    step = 64
    column = jnp.arange(features, dtype=jnp.int32)
    rates = jnp.exp((column // 2).astype(F32) * (-2.0 * math.log(10000.0) / features))
    even = (column % 2 == 0)[None, :]
    near = (start + rows - 1 - step * jnp.arange(width // step, dtype=jnp.int32)).astype(F32)
    near = near[:, None] * rates[None, :]
    far = jnp.arange(step, dtype=jnp.int32).astype(F32)[:, None] * rates[None, :]
    sine, cosine = jnp.sin(near), jnp.cos(near)
    return (
        jnp.where(even, sine, cosine),
        jnp.where(even, -cosine, sine),
        jnp.cos(far),
        jnp.sin(far),
    )


def shards(
    tokens,
    first_expand,
    first_shrink,
    attend_input,
    position_map,
    position_bias,
    attend_output,
    gating_map,
    depth_kernel,
    batch_scale,
    batch_shift,
    mixing_map,
    second_expand,
    second_shrink,
    layer_gains,
    cotangent,
):
    rows, part = tokens.shape
    tp, ctx = lax.axis_size("tp"), lax.axis_size("ctx")
    features = part * tp
    shard = first_expand.shape[0]
    hidden = first_expand.shape[1]
    heads, size = position_bias.shape[1:]
    local = heads * size
    channels = depth_kernel.shape[1]
    length = rows * ctx
    width = length + rows
    tp_at = lax.axis_index("tp")
    ctx_at = lax.axis_index("ctx")
    idx = jnp.stack(
        [tp_at, tp_at % 2, lax.axis_index("fsdp"), ctx_at]
    ).astype(jnp.int32)

    one = gathered(idx, jnp.concatenate([first_expand, first_shrink.T], axis=1))
    gains = lax.all_gather(layer_gains, "tp", axis=1, tiled=True)
    frames = lax.all_gather(
        jnp.concatenate([tokens, cotangent], axis=0), "tp", axis=1, tiled=True
    )
    x0, cot = frames[:rows], frames[rows:]
    bias = position_bias.reshape(2, local)
    params = jnp.stack([batch_scale, batch_shift])
    tables = angle_tables(ctx_at * rows, rows, width, features)
    two = gathered(
        idx,
        jnp.concatenate(
            [attend_input.reshape(shard, 3 * local), position_map, attend_output.T], axis=1
        ),
    )
    three = gathered(
        idx,
        jnp.concatenate(
            [
                gating_map.reshape(shard, 2 * channels),
                mixing_map.T,
                second_expand,
                second_shrink.T,
            ],
            axis=1,
        ),
    )
    at_pos, at_out = 3 * local, 4 * local
    at_mix, at_two = 2 * channels, 3 * channels

    stream = ((rows, features), F32)
    packed = ((rows, features), BF16)
    piece = ((rows // 2, features), BF16)
    gain_row = ((1, features), F32)
    work = pltpu.VMEM((rows, features), F32)
    feed_flops = 4 * rows * features * hidden

    feed_outs = [packed, ((rows, hidden), F32), ((rows, hidden), BF16), piece, piece]
    z1, u1, h1, keep, send = call(
        functools.partial(feed_body, 0, 0, False),
        feed_outs,
        idx,
        x0,
        gains,
        one,
        scratch=[work],
        flops=feed_flops,
    )
    t1, t2 = tp_sum(keep, send)
    embed, relative = call(
        functools.partial(relative_body, at_pos),
        [((width, features), BF16), ((width, local), BF16)],
        idx,
        *tables,
        two,
        flops=2 * width * features * local,
    )
    per_head = ((rows, local), BF16)
    x1, z2, qa, qb, kv = call(
        attend_in_body,
        [stream, packed, per_head, per_head, ((rows, 2 * local), BF16)],
        idx,
        x0,
        t1,
        t2,
        gains,
        two,
        bias,
        scratch=[work],
        flops=6 * rows * features * local,
    )
    pairs = [kv] + [swap(kv, "ctx", step) for step in range(1, ctx)]
    position = call(
        functools.partial(position_body, heads),
        [((heads, rows, length), F32)],
        idx,
        qb,
        relative,
        flops=2 * rows * (length + BLOCK) * local * 8,
    )[0]
    whole_pairs = pltpu.VMEM((length, 2 * local), BF16)
    p, mixed, keep, send = call(
        functools.partial(attend_body, heads, ctx, at_out),
        [((heads, rows, length), BF16), per_head, piece, piece],
        idx,
        qa,
        *pairs,
        position,
        two,
        scratch=[whole_pairs, work],
        flops=4 * rows * length * local * 8,
    )
    t1, t2 = tp_sum(keep, send)
    edge = ((HALO, channels), BF16)
    x2, z3, paired, glu, first, last = call(
        conv_in_body,
        [stream, packed, ((rows, 2 * channels), F32), ((rows, channels), BF16), edge, edge],
        idx,
        x1,
        t1,
        t2,
        gains,
        three,
        scratch=[work],
        flops=4 * rows * features * channels,
    )
    low, high = neighbours(first, last)
    padded = pltpu.VMEM((rows + 2 * HALO, channels), F32)
    c, stats = call(
        conv_body,
        [((rows, channels), F32), ((8, channels), F32)],
        idx,
        glu,
        low,
        high,
        depth_kernel,
        scratch=[padded],
    )
    stats = pooled(stats, rows)
    q, act, keep, send = call(
        functools.partial(batch_body, at_mix),
        [((rows, channels), F32), ((rows, channels), BF16), piece, piece],
        idx,
        c,
        stats,
        params,
        three,
        scratch=[work],
        flops=2 * rows * features * channels,
    )
    t1, t2 = tp_sum(keep, send)
    x3, z4, u2, h2, keep, send = call(
        functools.partial(feed_body, 3, at_two, True),
        [stream] + feed_outs,
        idx,
        x2,
        t1,
        t2,
        gains,
        three,
        scratch=[work],
        flops=feed_flops,
    )
    t1, t2 = tp_sum(keep, send)
    outputs, d4, gain_five, f4, du2, keep, send = call(
        functools.partial(final_body, at_two),
        [((rows, part), BF16), stream, gain_row, packed, ((rows, hidden), BF16), piece, piece],
        idx,
        x3,
        t1,
        t2,
        gains,
        cot,
        u2,
        three,
        scratch=[work],
        flops=feed_flops,
    )
    t1, t2 = tp_sum(keep, send)
    rear = scattered(idx, [(z4, du2), (f4, h2)], False)
    edge = ((2 * HALO, channels), F32)
    d3, f3, da, sums, first, last, gain_four = call(
        functools.partial(conv_back_body, at_mix),
        [stream, packed, ((rows, channels), F32), ((8, channels), F32), edge, edge, gain_row],
        idx,
        x3,
        d4,
        t1,
        t2,
        gains,
        q,
        params,
        three,
        scratch=[work],
        flops=2 * rows * features * channels,
    )
    low_back, high_back = neighbours(first, last)
    sums = summed(sums)
    counted = rows * lax.axis_size(FRAMES)
    dc, dg, keep, send = call(
        functools.partial(gate_back_body, ctx, counted),
        [((rows, channels), BF16), ((rows, 2 * channels), BF16), piece, piece],
        idx,
        da,
        q,
        low_back,
        high_back,
        sums,
        stats,
        params,
        depth_kernel,
        paired,
        three,
        scratch=[padded, work],
        flops=4 * rows * features * channels,
    )
    t1, t2 = tp_sum(keep, send)
    kernel_grad = call(
        taps_body,
        [(depth_kernel.shape, F32)],
        idx,
        glu,
        low,
        high,
        dc,
        scratch=[padded],
    )[0]
    middle = scattered(idx, [(z3, dg), (f3, act)], False)
    pair_block = ((rows, 2 * local), BF16)
    results = call(
        functools.partial(attend_back_body, heads, ctx, at_out),
        [stream, packed, gain_row, ((heads, rows, length), BF16), ((rows, local), F32)]
        + [pair_block] * ctx,
        idx,
        x2,
        d3,
        t1,
        t2,
        gains,
        two,
        p,
        qa,
        *pairs,
        scratch=[whole_pairs, whole_pairs, pltpu.VMEM((rows, local), BF16), work],
        flops=8 * rows * length * local * 4,
    )
    d2, f2, gain_three, ds, dqa = results[:5]
    pair_grads = [results[5]] + [
        swap(block, "ctx", step + 1) for step, block in enumerate(results[6:])
    ]
    dqb, dr = call(
        functools.partial(position_back_body, heads),
        [((rows, local), F32), ((width, local), BF16)],
        idx,
        ds,
        qb,
        relative,
        scratch=[pltpu.VMEM((BLOCK, length + BLOCK), F32), pltpu.VMEM((width, local), F32)],
        flops=4 * rows * (length + BLOCK) * local * 8,
    )
    dp, bias_grad, keep, send = call(
        functools.partial(attend_out_body, ctx),
        [((rows, 3 * local), BF16), ((2, local), F32), piece, piece],
        idx,
        dqa,
        dqb,
        *pair_grads,
        two,
        scratch=[work],
        flops=6 * rows * features * local,
    )
    t1, t2 = tp_sum(keep, send)
    inner = scattered(idx, [(z2, dp), (embed, dr), (f2, mixed)], False)
    d1, f1, du1, gain_two, gain_one, keep, send = call(
        feed_back_body,
        [stream, packed, ((rows, hidden), BF16), gain_row, gain_row, piece, piece],
        idx,
        x1,
        d2,
        t1,
        t2,
        gains,
        u1,
        x0,
        one,
        scratch=[work],
        flops=feed_flops,
    )
    t1, t2 = tp_sum(keep, send)
    front_b = scattered(idx, [(f1, h1)], True)
    front_a = scattered(idx, [(z1, du1)], True)
    step = 1
    while step < tp:
        gain_one = gain_one + swap(gain_one, "tp", step)
        step *= 2
    rows_grad = lax.dynamic_slice_in_dim(
        jnp.concatenate([gain_one, gain_two, gain_three, gain_four, gain_five], axis=0),
        tp_at * part,
        part,
        axis=1,
    )
    small = summed(jnp.concatenate([rows_grad, bias_grad, kernel_grad], axis=0))
    taps = depth_kernel.shape[0]
    tokens_grad = call(
        last_body,
        [((rows, part), F32)],
        idx,
        x0,
        d1,
        t1,
        t2,
        gains,
        scratch=[work],
    )[0]
    return (
        outputs,
        tokens_grad,
        front_a,
        front_b.T,
        inner[:, :at_pos].reshape(shard, 3, local),
        inner[:, at_pos:at_out],
        small[5:7].reshape(2, heads, size),
        inner[:, at_out:].T,
        middle[:, :at_mix].reshape(shard, 2, channels),
        small[7 : 7 + taps],
        sums[0],
        sums[1],
        middle[:, at_mix:].T,
        rear[:, :hidden],
        rear[:, hidden:].T,
        small[:5],
    )


def solution(mesh):
    frames = ("fsdp", "ctx")
    rows, columns = P(frames, "tp"), P("tp", frames)
    three_dims, last_only, one_dim = P(frames, None, "tp"), P(None, "tp"), P("tp")
    heads = P(None, "tp", None)
    return jax.shard_map(
        shards,
        mesh=mesh,
        in_specs=(
            rows,
            rows,
            columns,
            three_dims,
            rows,
            heads,
            columns,
            three_dims,
            last_only,
            one_dim,
            one_dim,
            columns,
            rows,
            columns,
            last_only,
            rows,
        ),
        out_specs=(
            rows,
            rows,
            rows,
            columns,
            three_dims,
            rows,
            heads,
            columns,
            three_dims,
            last_only,
            one_dim,
            one_dim,
            columns,
            rows,
            columns,
            last_only,
        ),
        check_vma=False,
    )
```

```python
import functools
import math

import jax
import jax.numpy as jnp
from jax import lax
from jax.experimental import pallas as pl
from jax.experimental.pallas import tpu as pltpu
from jax.sharding import PartitionSpec as P

F32 = jnp.float32
BF16 = jnp.bfloat16
EPSILON = 1e-05
HALO = 16
BLOCK = 128
VMEM_BYTES = 12 * 1024 * 1024


def call(body, outs, *args, scratch=(), flops=0, vmem=VMEM_BYTES):
    outs = [jax.ShapeDtypeStruct(shape, dtype) for shape, dtype in outs]
    moved = sum(a.size * a.dtype.itemsize for a in list(args[1:]) + outs)
    return pl.pallas_call(
        body,
        out_shape=outs,
        in_specs=[pl.BlockSpec(memory_space=pltpu.SMEM)]
        + [pl.BlockSpec(memory_space=pltpu.VMEM)] * (len(args) - 1),
        out_specs=[pl.BlockSpec(memory_space=pltpu.VMEM)] * len(outs),
        scratch_shapes=list(scratch),
        compiler_params=pltpu.CompilerParams(vmem_limit_bytes=vmem),
        cost_estimate=pl.CostEstimate(
            flops=int(flops), bytes_accessed=int(moved), transcendentals=0
        ),
    )(*args)


def dot(left, right):
    return jnp.dot(left, right, preferred_element_type=F32)


def dot_cols(left, right):
    return lax.dot_general(left, right, (((1,), (1,)), ((), ())), preferred_element_type=F32)


def dot_rows(left, right):
    return lax.dot_general(left, right, (((0,), (0,)), ((), ())), preferred_element_type=F32)


def normalized(stream):
    centred = stream - jnp.mean(stream, axis=1, keepdims=True)
    spread = lax.rsqrt(jnp.mean(centred * centred, axis=1, keepdims=True) + EPSILON)
    return centred * spread, spread


def norm_pullback(grad, stream, gain):
    normal, spread = normalized(stream)
    scaled = grad * gain
    first = jnp.mean(scaled, axis=1, keepdims=True)
    second = jnp.mean(scaled * normal, axis=1, keepdims=True)
    return spread * (scaled - first - normal * second), jnp.sum(
        grad * normal, axis=0, keepdims=True
    )


def swish_slope(value, logistic):
    return logistic * (1.0 + value * (1.0 - logistic))


def halves(idx, rows):
    half = rows // 2
    mine = pl.multiple_of(idx[1] * half, half)
    theirs = pl.multiple_of((1 - idx[1]) * half, half)
    return pl.ds(mine, half), pl.ds(theirs, half)


def split(idx, whole, keep, send):
    mine, theirs = halves(idx, whole.shape[0])
    keep[...] = whole[mine, :].astype(BF16)
    send[...] = whole[theirs, :].astype(BF16)


def join(idx, t_mine, t_theirs, whole):
    mine, theirs = halves(idx, whole.shape[0])
    whole[mine, :] = t_mine[...].astype(F32)
    whole[theirs, :] = t_theirs[...].astype(F32)


def xor_pairs(count, step):
    return [(i, i ^ step) for i in range(count)]


def swap(value, axis, step):
    return lax.ppermute(value, axis, xor_pairs(lax.axis_size(axis), step))


def added(left, right):
    return (left.astype(F32) + right.astype(F32)).astype(BF16)


def tp_sum(keep, send):
    count = lax.axis_size("tp")
    total = added(keep, swap(send, "tp", 1))
    step = 2
    while step < count:
        total = added(total, swap(total, "tp", step))
        step *= 2
    return total, swap(total, "tp", 1)


def place_body(ctx, later, idx, *refs):
    blocks = refs[: ctx + 2]
    out = refs[ctx + 2 + later]
    if later:
        refs[-1][...] = refs[ctx + 2][...]
    rows = blocks[0].shape[0]
    for at in range(2 * ctx):
        half = idx[2] if at < ctx else 1 - idx[2]
        target = half * ctx + jnp.bitwise_xor(idx[3], at % ctx)
        if at <= ctx:
            block = blocks[at][...]
        else:
            block = blocks[ctx + 1][(at - ctx - 1) * rows : (at - ctx) * rows, :]
        out[pl.ds(pl.multiple_of(target * rows, rows), rows), :] = block


def features_body(idx, *refs):
    blocks, gain_blocks = refs[:4], refs[4:8]
    x_out, cot_out, gains_out = refs[8:]
    rows, features = x_out.shape
    part = features // 4
    for at in range(4):
        target = jnp.bitwise_xor(idx[0], at)
        columns = pl.ds(pl.multiple_of(target * part, part), part)
        x_out[:, columns] = blocks[at][:rows, :]
        cot_out[:, columns] = blocks[at][rows:, :]
        gains_out[:, columns] = gain_blocks[at][...]


def wgrad_body(pairs, ordered, ctx, idx, *refs):
    out, scratch = refs[2 * pairs], refs[2 * pairs + 1]
    column = 0
    for at in range(pairs):
        left, right = refs[2 * at], refs[2 * at + 1]
        width = right.shape[1]
        product = dot_rows(left[...], right[...]).astype(BF16)
        if ordered:
            out[:, column : column + width] = product
        else:
            scratch[:, column : column + width] = product
        column += width
    if not ordered:
        rows = out.shape[0] // (2 * ctx)
        for at in range(2 * ctx):
            half = idx[2] if at < ctx else 1 - idx[2]
            source = half * ctx + jnp.bitwise_xor(idx[3], at % ctx)
            out[at * rows : (at + 1) * rows, :] = scratch[
                pl.ds(pl.multiple_of(source * rows, rows), rows), :
            ]


def feed_body(gain_at, base, joined, idx, *refs):
    if joined:
        x_ref, t1, t2, gains, weights, x_out, z_out, u_out, h_out, keep, send, work = refs
        join(idx, t1, t2, work)
        x = x_ref[...] + work[...]
        x_out[...] = x
    else:
        x_ref, gains, weights, z_out, u_out, h_out, keep, send, work = refs
        x = x_ref[...].astype(F32)
    hidden = u_out.shape[1]
    normal, unused = normalized(x)
    z = (normal * gains[gain_at : gain_at + 1, :]).astype(BF16)
    z_out[...] = z
    u = dot(z, weights[:, base : base + hidden])
    u_out[...] = u
    h = (u * jax.nn.sigmoid(u)).astype(BF16)
    h_out[...] = h
    work[...] = dot_cols(h, weights[:, base + hidden : base + 2 * hidden])
    split(idx, work, keep, send)


def attend_in_body(idx, x_ref, t1, t2, gains, weights, bias, x_out, z_out, qa, qb, kv, work):
    join(idx, t1, t2, work)
    x = x_ref[...].astype(F32) + 0.5 * work[...]
    x_out[...] = x
    normal, unused = normalized(x)
    z = (normal * gains[1:2, :]).astype(BF16)
    z_out[...] = z
    local = bias.shape[1]
    project = dot(z, weights[:, : 3 * local])
    query = project[:, :local]
    qa[...] = (query + bias[0:1, :]).astype(BF16)
    qb[...] = (query + bias[1:2, :]).astype(BF16)
    kv[...] = project[:, local:].astype(BF16)


def relative_body(base, idx, near_p, near_q, far_c, far_s, weights, embed, relative):
    step = far_c.shape[0]
    cos, sin = far_c[...], far_s[...]
    for at in range(embed.shape[0] // step):
        value = near_p[at : at + 1, :] * cos + near_q[at : at + 1, :] * sin
        embed[at * step : (at + 1) * step, :] = value.astype(BF16)
    relative[...] = dot(embed[...], weights[:, base : base + relative.shape[1]]).astype(BF16)


def position_body(heads, idx, qb, relative, out):
    rows, local = qb.shape
    size = local // heads
    length = out.shape[2]
    width = length + BLOCK
    for head in range(heads):
        columns = slice(head * size, (head + 1) * size)
        for at in range(rows // BLOCK):
            frames = slice(at * BLOCK, (at + 1) * BLOCK)
            first = rows - BLOCK * (at + 1)
            wide = dot_cols(qb[frames, columns], relative[first : first + width, columns])
            turned = pltpu.roll(wide, width - (BLOCK - 1), 1, stride=1, stride_axis=0)
            out[head, frames, :] = turned[:, :length]


def fill_pairs(idx, blocks, whole):
    rows = blocks[0].shape[0]
    for at, block in enumerate(blocks):
        target = jnp.bitwise_xor(idx[3], at)
        whole[pl.ds(pl.multiple_of(target * rows, rows), rows), :] = block[...]


def attend_body(heads, ctx, base, idx, qa, *refs):
    blocks = refs[:ctx]
    position, weights, p_out, mixed, keep, send, pairs, work = refs[ctx:]
    fill_pairs(idx, blocks, pairs)
    rows, local = qa.shape
    size = local // heads
    scale = size**-0.5
    for head in range(heads):
        columns = slice(head * size, (head + 1) * size)
        values = slice(local + head * size, local + (head + 1) * size)
        for at in range(rows // BLOCK):
            frames = slice(at * BLOCK, (at + 1) * BLOCK)
            scores = (dot_cols(qa[frames, columns], pairs[:, columns]) + position[head, frames, :]) * scale
            raised = jnp.exp(scores - jnp.max(scores, axis=1, keepdims=True))
            share = (raised / jnp.sum(raised, axis=1, keepdims=True)).astype(BF16)
            p_out[head, frames, :] = share
            mixed[frames, columns] = dot(share, pairs[:, values]).astype(BF16)
    work[...] = dot_cols(mixed[...], weights[:, base : base + local])
    split(idx, work, keep, send)


def conv_in_body(idx, x_ref, t1, t2, gains, weights, x_out, z_out, g_out, glu, first, last, work):
    join(idx, t1, t2, work)
    x = x_ref[...] + work[...]
    x_out[...] = x
    normal, unused = normalized(x)
    z = (normal * gains[2:3, :]).astype(BF16)
    z_out[...] = z
    rows, channels = glu.shape
    paired = dot(z, weights[:, : 2 * channels])
    g_out[...] = paired
    gated = (paired[:, :channels] * jax.nn.sigmoid(paired[:, channels:])).astype(BF16)
    glu[...] = gated
    first[...] = gated[:HALO, :]
    last[...] = gated[rows - HALO :, :]


def fill_padded(low, own, high, padded):
    rows = own.shape[0]
    padded[:HALO, :] = low[...].astype(F32)
    padded[HALO : HALO + rows, :] = own[...].astype(F32)
    padded[HALO + rows :, :] = high[...].astype(F32)


def conv_body(idx, glu, low, high, kernel, c_out, stats, padded):
    fill_padded(low, glu, high, padded)
    rows = glu.shape[0]
    taps = kernel.shape[0]
    shift = HALO - (taps - 1) // 2
    total = kernel[0:1, :] * padded[shift : shift + rows, :]
    for tap in range(1, taps):
        total = total + kernel[tap : tap + 1, :] * padded[shift + tap : shift + tap + rows, :]
    c_out[...] = total
    mean = jnp.mean(total, axis=0, keepdims=True)
    centred = total - mean
    stats[0:1, :] = mean
    stats[1:2, :] = jnp.sum(centred * centred, axis=0, keepdims=True)
    stats[2:, :] = jnp.zeros((stats.shape[0] - 2, stats.shape[1]), F32)


def batch_body(base, idx, c, stats, params, weights, q_out, act_out, keep, send, work):
    spread = stats[1:2, :]
    q = (c[...] - stats[0:1, :]) * spread
    q_out[...] = q
    a = q * params[0:1, :] + params[1:2, :]
    act = (a * jax.nn.sigmoid(a)).astype(BF16)
    act_out[...] = act
    work[...] = dot_cols(act, weights[:, base : base + act.shape[1]])
    split(idx, work, keep, send)


def feed_pullback(idx, grad, u, weights, base, f_out, du_out, keep, send, work):
    hidden = u.shape[1]
    f = (0.5 * grad).astype(BF16)
    f_out[...] = f
    value = u[...]
    logistic = jax.nn.sigmoid(value)
    back = dot(f, weights[:, base + hidden : base + 2 * hidden])
    du = (back * swish_slope(value, logistic)).astype(BF16)
    du_out[...] = du
    work[...] = dot_cols(du, weights[:, base : base + hidden])
    split(idx, work, keep, send)


def final_body(base, idx, x_ref, t1, t2, gains, cot, u, weights, y_out, d_out, gain_out, f_out, du_out, keep, send, work):
    join(idx, t1, t2, work)
    x = x_ref[...] + 0.5 * work[...]
    normal, unused = normalized(x)
    gain = gains[4:5, :]
    work[...] = normal * gain
    width = y_out.shape[1]
    y_out[...] = work[:, pl.ds(pl.multiple_of(idx[0] * width, width), width)].astype(BF16)
    grad, gain_grad = norm_pullback(cot[...].astype(F32), x, gain)
    gain_out[...] = gain_grad
    d_out[...] = grad
    feed_pullback(idx, grad, u, weights, base, f_out, du_out, keep, send, work)


def conv_back_body(base, idx, x_ref, d_ref, t1, t2, gains, q, params, weights, d_out, f_out, da_out, edges, gain_out, work):
    join(idx, t1, t2, work)
    grad, gain_grad = norm_pullback(work[...], x_ref[...], gains[3:4, :])
    gain_out[...] = gain_grad
    grad = d_ref[...] + grad
    d_out[...] = grad
    f = grad.astype(BF16)
    f_out[...] = f
    rows, channels = q.shape
    value = q[...]
    a = value * params[0:1, :] + params[1:2, :]
    da = dot(f, weights[:, base : base + channels]) * swish_slope(a, jax.nn.sigmoid(a))
    da_out[...] = da
    edges[0:1, :] = jnp.sum(da * value, axis=0, keepdims=True)
    edges[1:2, :] = jnp.sum(da, axis=0, keepdims=True)
    edges[2:8, :] = jnp.zeros((6, channels), F32)
    for at, part in enumerate((da[:HALO], value[:HALO], da[rows - HALO :], value[rows - HALO :])):
        edges[8 + at * HALO : 8 + (at + 1) * HALO, :] = part


def gate_back_body(ctx, counted, idx, da, q, own, near, far, stats, params, kernel, paired, weights, sums, dc_out, dg_out, keep, send, padded, work):
    rows, channels = q.shape
    sums[...] = own[:8, :] + far[:8, :]
    odd = idx[3] % 2 == 1
    low = jnp.where(odd, near[8 + 2 * HALO :, :], far[8 + 2 * HALO :, :])
    high = jnp.where(odd, far[8 : 8 + 2 * HALO, :], near[8 : 8 + 2 * HALO, :])
    factor = stats[1:2, :] * params[0:1, :]
    mean_scale = sums[0:1, :] / counted
    mean_shift = sums[1:2, :] / counted

    def centred(grad, normal):
        return (factor * (grad - mean_shift - normal * mean_scale)).astype(BF16)

    dc = centred(da[...], q[...])
    dc_out[...] = dc
    before = (idx[3] > 0).astype(F32)
    after = (idx[3] < ctx - 1).astype(F32)
    padded[:HALO, :] = centred(low[:HALO, :], low[HALO:, :]).astype(F32) * before
    padded[HALO : HALO + rows, :] = dc.astype(F32)
    padded[HALO + rows :, :] = centred(high[:HALO, :], high[HALO:, :]).astype(F32) * after
    taps = kernel.shape[0]
    top = HALO + (taps - 1) // 2
    total = kernel[0:1, :] * padded[top : top + rows, :]
    for tap in range(1, taps):
        total = total + kernel[tap : tap + 1, :] * padded[top - tap : top - tap + rows, :]
    logistic = jax.nn.sigmoid(paired[:, channels:])
    through = total * logistic
    dg_out[:, :channels] = through.astype(BF16)
    dg_out[:, channels:] = (through * paired[:, :channels] * (1.0 - logistic)).astype(BF16)
    work[...] = dot_cols(dg_out[...], weights[:, : 2 * channels])
    split(idx, work, keep, send)


def taps_body(idx, glu, low, high, dc, out, padded):
    fill_padded(low, glu, high, padded)
    rows = glu.shape[0]
    grad = dc[...].astype(F32)
    shift = HALO - (out.shape[0] - 1) // 2
    for tap in range(out.shape[0]):
        out[tap : tap + 1, :] = jnp.sum(
            grad * padded[shift + tap : shift + tap + rows, :], axis=0, keepdims=True
        )


def attend_back_body(heads, ctx, base, idx, x_ref, d_ref, t1, t2, gains, weights, p, qa, *refs):
    blocks = refs[:ctx]
    d_out, f_out, gain_out, ds_out, dqa = refs[ctx : ctx + 5]
    out_blocks = refs[ctx + 5 : 2 * ctx + 5]
    pairs, grads, do, work = refs[2 * ctx + 5 :]
    fill_pairs(idx, blocks, pairs)
    join(idx, t1, t2, work)
    grad, gain_grad = norm_pullback(work[...], x_ref[...], gains[2:3, :])
    gain_out[...] = gain_grad
    grad = d_ref[...] + grad
    d_out[...] = grad
    f = grad.astype(BF16)
    f_out[...] = f
    rows, local = qa.shape
    size = local // heads
    scale = size**-0.5
    do[...] = dot(f, weights[:, base : base + local]).astype(BF16)
    for head in range(heads):
        columns = slice(head * size, (head + 1) * size)
        values = slice(local + head * size, local + (head + 1) * size)
        for at in range(rows // BLOCK):
            frames = slice(at * BLOCK, (at + 1) * BLOCK)
            dp = dot_cols(do[frames, columns], pairs[:, values])
            share = p[head, frames, :].astype(F32)
            balance = jnp.sum(share * dp, axis=1, keepdims=True)
            ds = (share * (dp - balance)).astype(BF16)
            ds_out[head, frames, :] = ds
            dqa[frames, columns] = dot(ds, pairs[:, columns]) * scale
        grads[:, columns] = (dot_rows(ds_out[head], qa[:, columns]) * scale).astype(BF16)
        grads[:, values] = dot_rows(p[head], do[:, columns]).astype(BF16)
    for at, block in enumerate(out_blocks):
        source = jnp.bitwise_xor(idx[3], at)
        block[...] = grads[pl.ds(pl.multiple_of(source * rows, rows), rows), :]


def position_back_body(heads, idx, ds, qb, relative, dqb, dr_out, wide, total):
    rows, local = qb.shape
    size = local // heads
    length = ds.shape[2]
    width = length + BLOCK
    scale = size**-0.5
    down = lax.broadcasted_iota(jnp.int32, (BLOCK, BLOCK), 0)
    across = lax.broadcasted_iota(jnp.int32, (BLOCK, BLOCK), 1)
    flip = (down + across == BLOCK - 1).astype(BF16)
    total[...] = jnp.zeros(total.shape, F32)
    wide[:, length:] = jnp.zeros((BLOCK, BLOCK), F32)
    for head in range(heads):
        columns = slice(head * size, (head + 1) * size)
        for at in range(rows // BLOCK):
            frames = slice(at * BLOCK, (at + 1) * BLOCK)
            first = rows - BLOCK * (at + 1)
            wide[:, :length] = dot(flip, ds[head, frames, :])
            turned = pltpu.roll(wide[...], 0, 1, stride=1, stride_axis=0).astype(BF16)
            turned_b = dot(turned, relative[first : first + width, columns]) * scale
            dqb[frames, columns] = jnp.dot(
                flip.astype(F32), turned_b, precision=lax.Precision.HIGHEST, preferred_element_type=F32
            )
            flipped = dot(flip, qb[frames, columns]).astype(BF16)
            total[first : first + width, columns] += dot_rows(turned, flipped)
    dr_out[...] = (total[...] * scale).astype(BF16)


def attend_out_body(ctx, idx, dqa, dqb, *refs):
    blocks = refs[:ctx]
    weights, dp_out, bias_out, keep, send, work = refs[ctx:]
    local = dqa.shape[1]
    bias_out[0:1, :] = jnp.sum(dqa[...], axis=0, keepdims=True)
    bias_out[1:2, :] = jnp.sum(dqb[...], axis=0, keepdims=True)
    dp_out[:, :local] = (dqa[...] + dqb[...]).astype(BF16)
    total = blocks[0][...].astype(F32)
    for block in blocks[1:]:
        total = total + block[...].astype(F32)
    dp_out[:, local:] = total.astype(BF16)
    work[...] = dot_cols(dp_out[...], weights[:, : 3 * local])
    split(idx, work, keep, send)


def feed_back_body(idx, x_ref, d_ref, t1, t2, gains, u, x0, weights, d_out, f_out, du_out, gain_out, last_gain, keep, send, work):
    join(idx, t1, t2, work)
    grad, gain_grad = norm_pullback(work[...], x_ref[...], gains[1:2, :])
    gain_out[...] = gain_grad
    grad = d_ref[...] + grad
    d_out[...] = grad
    feed_pullback(idx, grad, u, weights, 0, f_out, du_out, keep, send, work)
    normal, unused = normalized(x0[...].astype(F32))
    last_gain[...] = jnp.sum(work[...] * normal, axis=0, keepdims=True)


def last_body(idx, x_ref, d_ref, t1, t2, gains, out, work):
    join(idx, t1, t2, work)
    grad, unused = norm_pullback(work[...], x_ref[...].astype(F32), gains[0:1, :])
    work[...] = d_ref[...] + grad
    width = out.shape[1]
    out[...] = work[:, pl.ds(pl.multiple_of(idx[0] * width, width), width)]


FRAMES = ("fsdp", "ctx")


def paired_mesh():
    return lax.axis_size("fsdp") == 2


def gathered(idx, shard, later=None):
    if not paired_mesh():
        whole = lax.all_gather(shard, FRAMES, axis=0, tiled=True)
        return whole if later is None else (whole, later)
    ctx = lax.axis_size("ctx")
    mine = [shard] + [swap(shard, "ctx", step) for step in range(1, ctx)]
    theirs = [swap(shard, "fsdp", 1), swap(jnp.concatenate(mine[1:], axis=0), "fsdp", 1)]
    rows, width = shard.shape
    outs = [((2 * ctx * rows, width), BF16)]
    handed = [] if later is None else [later]
    outs += [(later.shape, later.dtype)] if handed else []
    results = call(
        functools.partial(place_body, ctx, len(handed)), outs, idx, *mine, *theirs, *handed
    )
    return results if handed else results[0]


def features_whole(value):
    far = swap(value, "tp", 2)
    return [value, swap(value, "tp", 1), far, swap(far, "tp", 1)]


def weight_grads(idx, pairs, ordered):
    depth = pairs[0][0].shape[1]
    width = sum(right.shape[1] for unused, right in pairs)
    flat = [array for pair in pairs for array in pair]
    ctx = lax.axis_size("ctx")
    flops = sum(2 * left.shape[0] * depth * right.shape[1] for left, right in pairs)
    return call(
        functools.partial(wgrad_body, len(pairs), ordered, ctx),
        [((depth, width), BF16)],
        idx,
        *flat,
        scratch=[pltpu.VMEM((8, 128) if ordered else (depth, width), BF16)],
        flops=flops,
    )[0]


def scattered(idx, pairs, direct):
    direct = direct and paired_mesh()
    grads = weight_grads(idx, pairs, not direct)
    if not direct:
        return lax.psum_scatter(grads, FRAMES, scatter_dimension=0, tiled=True).astype(F32)
    ctx = lax.axis_size("ctx")
    half = grads.shape[0] // 2
    rows = half // ctx
    total = added(grads[:half], swap(grads[half:], "fsdp", 1))
    parts = [total[:rows]]
    for step in range(1, ctx):
        parts.append(swap(total[step * rows : (step + 1) * rows], "ctx", step))
    return sum(part.astype(F32) for part in parts)


def over_frames(value, merge):
    for axis in ("fsdp", "ctx"):
        step = 1
        while step < lax.axis_size(axis):
            value = merge(value, swap(value, axis, step))
            step *= 2
    return value


def summed(value):
    return over_frames(value, lambda left, right: left + right)


def pooled(stats, rows):
    count = [rows]

    def merge(left, right):
        gap = left[0:1] - right[0:1]
        mean = 0.5 * (left[0:1] + right[0:1])
        squares = left[1:2] + right[1:2] + gap * gap * (0.5 * count[0])
        count[0] *= 2
        return jnp.concatenate([mean, squares, left[2:]], axis=0)

    stats = over_frames(stats, merge)
    spread = lax.rsqrt(stats[1:2] / count[0] + EPSILON)
    return jnp.concatenate([stats[0:1], spread, stats[2:]], axis=0)


def edges_summed(edges):
    step = 1
    while step < lax.axis_size("fsdp"):
        edges = jnp.concatenate([edges[:8] + swap(edges[:8], "fsdp", step), edges[8:]], axis=0)
        step *= 2
    near = swap(edges, "ctx", 1)
    own = jnp.concatenate([edges[:8] + near[:8], edges[8:]], axis=0)
    return own, near, swap(own, "ctx", 3)


def neighbours(first, last):
    count = lax.axis_size("ctx")
    up = [(i, i + 1) for i in range(count - 1)]
    down = [(i + 1, i) for i in range(count - 1)]
    return lax.ppermute(last, "ctx", up), lax.ppermute(first, "ctx", down)


def angle_tables(start, rows, width, features):
    step = 64
    column = jnp.arange(features, dtype=jnp.int32)
    rates = jnp.exp((column // 2).astype(F32) * (-2.0 * math.log(10000.0) / features))
    even = (column % 2 == 0)[None, :]
    near = (start + rows - 1 - step * jnp.arange(width // step, dtype=jnp.int32)).astype(F32)
    near = near[:, None] * rates[None, :]
    far = jnp.arange(step, dtype=jnp.int32).astype(F32)[:, None] * rates[None, :]
    sine, cosine = jnp.sin(near), jnp.cos(near)
    return (
        jnp.where(even, sine, cosine),
        jnp.where(even, -cosine, sine),
        jnp.cos(far),
        jnp.sin(far),
    )


def shards(
    tokens,
    first_expand,
    first_shrink,
    attend_input,
    position_map,
    position_bias,
    attend_output,
    gating_map,
    depth_kernel,
    batch_scale,
    batch_shift,
    mixing_map,
    second_expand,
    second_shrink,
    layer_gains,
    cotangent,
):
    rows, part = tokens.shape
    tp, ctx = lax.axis_size("tp"), lax.axis_size("ctx")
    features = part * tp
    shard = first_expand.shape[0]
    hidden = first_expand.shape[1]
    heads, size = position_bias.shape[1:]
    local = heads * size
    channels = depth_kernel.shape[1]
    length = rows * ctx
    width = length + rows
    tp_at = lax.axis_index("tp")
    ctx_at = lax.axis_index("ctx")
    idx = jnp.stack(
        [tp_at, tp_at % 2, lax.axis_index("fsdp"), ctx_at]
    ).astype(jnp.int32)

    last_shard = jnp.concatenate(
        [
            gating_map.reshape(shard, 2 * channels),
            mixing_map.T,
            second_expand,
            second_shrink.T,
        ],
        axis=1,
    )
    one, last_shard = gathered(
        idx, jnp.concatenate([first_expand, first_shrink.T], axis=1), last_shard
    )
    x0, cot, gains = call(
        features_body,
        [((rows, features), BF16), ((rows, features), BF16), ((5, features), F32)],
        idx,
        *features_whole(jnp.concatenate([tokens, cotangent], axis=0)),
        *features_whole(layer_gains),
    )
    bias = position_bias.reshape(2, local)
    params = jnp.stack([batch_scale, batch_shift])
    tables = angle_tables(ctx_at * rows, rows, width, features)
    two = gathered(
        idx,
        jnp.concatenate(
            [attend_input.reshape(shard, 3 * local), position_map, attend_output.T], axis=1
        ),
    )
    three = lax.all_gather(last_shard, FRAMES, axis=0, tiled=True)
    at_pos, at_out = 3 * local, 4 * local
    at_mix, at_two = 2 * channels, 3 * channels

    stream = ((rows, features), F32)
    packed = ((rows, features), BF16)
    piece = ((rows // 2, features), BF16)
    gain_row = ((1, features), F32)
    work = pltpu.VMEM((rows, features), F32)
    feed_flops = 4 * rows * features * hidden

    feed_outs = [packed, ((rows, hidden), F32), ((rows, hidden), BF16), piece, piece]
    z1, u1, h1, keep, send = call(
        functools.partial(feed_body, 0, 0, False),
        feed_outs,
        idx,
        x0,
        gains,
        one,
        scratch=[work],
        flops=feed_flops,
    )
    t1, t2 = tp_sum(keep, send)
    embed, relative = call(
        functools.partial(relative_body, at_pos),
        [((width, features), BF16), ((width, local), BF16)],
        idx,
        *tables,
        two,
        flops=2 * width * features * local,
    )
    per_head = ((rows, local), BF16)
    x1, z2, qa, qb, kv = call(
        attend_in_body,
        [stream, packed, per_head, per_head, ((rows, 2 * local), BF16)],
        idx,
        x0,
        t1,
        t2,
        gains,
        two,
        bias,
        scratch=[work],
        flops=6 * rows * features * local,
    )
    pairs = [kv] + [swap(kv, "ctx", step) for step in range(1, ctx)]
    position = call(
        functools.partial(position_body, heads),
        [((heads, rows, length), F32)],
        idx,
        qb,
        relative,
        flops=2 * rows * (length + BLOCK) * local * 8,
    )[0]
    whole_pairs = pltpu.VMEM((length, 2 * local), BF16)
    p, mixed, keep, send = call(
        functools.partial(attend_body, heads, ctx, at_out),
        [((heads, rows, length), BF16), per_head, piece, piece],
        idx,
        qa,
        *pairs,
        position,
        two,
        scratch=[whole_pairs, work],
        flops=4 * rows * length * local * 8,
    )
    t1, t2 = tp_sum(keep, send)
    edge = ((HALO, channels), BF16)
    x2, z3, paired, glu, first, last = call(
        conv_in_body,
        [stream, packed, ((rows, 2 * channels), F32), ((rows, channels), BF16), edge, edge],
        idx,
        x1,
        t1,
        t2,
        gains,
        three,
        scratch=[work],
        flops=4 * rows * features * channels,
    )
    low, high = neighbours(first, last)
    padded = pltpu.VMEM((rows + 2 * HALO, channels), F32)
    c, stats = call(
        conv_body,
        [((rows, channels), F32), ((8, channels), F32)],
        idx,
        glu,
        low,
        high,
        depth_kernel,
        scratch=[padded],
    )
    stats = pooled(stats, rows)
    q, act, keep, send = call(
        functools.partial(batch_body, at_mix),
        [((rows, channels), F32), ((rows, channels), BF16), piece, piece],
        idx,
        c,
        stats,
        params,
        three,
        scratch=[work],
        flops=2 * rows * features * channels,
    )
    t1, t2 = tp_sum(keep, send)
    x3, z4, u2, h2, keep, send = call(
        functools.partial(feed_body, 3, at_two, True),
        [stream] + feed_outs,
        idx,
        x2,
        t1,
        t2,
        gains,
        three,
        scratch=[work],
        flops=feed_flops,
    )
    t1, t2 = tp_sum(keep, send)
    outputs, d4, gain_five, f4, du2, keep, send = call(
        functools.partial(final_body, at_two),
        [((rows, part), BF16), stream, gain_row, packed, ((rows, hidden), BF16), piece, piece],
        idx,
        x3,
        t1,
        t2,
        gains,
        cot,
        u2,
        three,
        scratch=[work],
        flops=feed_flops,
    )
    t1, t2 = tp_sum(keep, send)
    d3, f3, da, edges, gain_four = call(
        functools.partial(conv_back_body, at_mix),
        [stream, packed, ((rows, channels), F32), ((8 + 4 * HALO, channels), F32), gain_row],
        idx,
        x3,
        d4,
        t1,
        t2,
        gains,
        q,
        params,
        three,
        scratch=[work],
        flops=2 * rows * features * channels,
    )
    own, near, far = edges_summed(edges)
    counted = rows * lax.axis_size(FRAMES)
    sums, dc, dg, keep, send = call(
        functools.partial(gate_back_body, ctx, counted),
        [((8, channels), F32), ((rows, channels), BF16), ((rows, 2 * channels), BF16), piece, piece],
        idx,
        da,
        q,
        own,
        near,
        far,
        stats,
        params,
        depth_kernel,
        paired,
        three,
        scratch=[padded, work],
        flops=4 * rows * features * channels,
    )
    t1, t2 = tp_sum(keep, send)
    kernel_grad = call(
        taps_body,
        [(depth_kernel.shape, F32)],
        idx,
        glu,
        low,
        high,
        dc,
        scratch=[padded],
    )[0]
    middle = scattered(idx, [(z3, dg), (f3, act), (z4, du2), (f4, h2)], False)
    pair_block = ((rows, 2 * local), BF16)
    results = call(
        functools.partial(attend_back_body, heads, ctx, at_out),
        [stream, packed, gain_row, ((heads, rows, length), BF16), ((rows, local), F32)]
        + [pair_block] * ctx,
        idx,
        x2,
        d3,
        t1,
        t2,
        gains,
        two,
        p,
        qa,
        *pairs,
        scratch=[whole_pairs, whole_pairs, pltpu.VMEM((rows, local), BF16), work],
        flops=8 * rows * length * local * 4,
    )
    d2, f2, gain_three, ds, dqa = results[:5]
    pair_grads = [results[5]] + [
        swap(block, "ctx", step + 1) for step, block in enumerate(results[6:])
    ]
    dqb, dr = call(
        functools.partial(position_back_body, heads),
        [((rows, local), F32), ((width, local), BF16)],
        idx,
        ds,
        qb,
        relative,
        scratch=[pltpu.VMEM((BLOCK, length + BLOCK), F32), pltpu.VMEM((width, local), F32)],
        flops=4 * rows * (length + BLOCK) * local * 8,
    )
    dp, bias_grad, keep, send = call(
        functools.partial(attend_out_body, ctx),
        [((rows, 3 * local), BF16), ((2, local), F32), piece, piece],
        idx,
        dqa,
        dqb,
        *pair_grads,
        two,
        scratch=[work],
        flops=6 * rows * features * local,
    )
    t1, t2 = tp_sum(keep, send)
    inner = scattered(idx, [(z2, dp), (embed, dr), (f2, mixed)], True)
    d1, f1, du1, gain_two, gain_one, keep, send = call(
        feed_back_body,
        [stream, packed, ((rows, hidden), BF16), gain_row, gain_row, piece, piece],
        idx,
        x1,
        d2,
        t1,
        t2,
        gains,
        u1,
        x0,
        one,
        scratch=[work],
        flops=feed_flops,
    )
    t1, t2 = tp_sum(keep, send)
    front_b = scattered(idx, [(f1, h1)], True)
    front_a = scattered(idx, [(z1, du1)], True)
    step = 1
    while step < tp:
        gain_one = gain_one + swap(gain_one, "tp", step)
        step *= 2
    rows_grad = lax.dynamic_slice_in_dim(
        jnp.concatenate([gain_one, gain_two, gain_three, gain_four, gain_five], axis=0),
        tp_at * part,
        part,
        axis=1,
    )
    small = summed(jnp.concatenate([rows_grad, bias_grad, kernel_grad], axis=0))
    taps = depth_kernel.shape[0]
    tokens_grad = call(
        last_body,
        [((rows, part), F32)],
        idx,
        x0,
        d1,
        t1,
        t2,
        gains,
        scratch=[work],
    )[0]
    return (
        outputs,
        tokens_grad,
        front_a,
        front_b.T,
        inner[:, :at_pos].reshape(shard, 3, local),
        inner[:, at_pos:at_out],
        small[5:7].reshape(2, heads, size),
        inner[:, at_out:].T,
        middle[:, :at_mix].reshape(shard, 2, channels),
        small[7 : 7 + taps],
        sums[0],
        sums[1],
        middle[:, at_mix:at_two].T,
        middle[:, at_two : at_two + hidden],
        middle[:, at_two + hidden :].T,
        small[:5],
    )


def solution(mesh):
    frames = ("fsdp", "ctx")
    rows, columns = P(frames, "tp"), P("tp", frames)
    three_dims, last_only, one_dim = P(frames, None, "tp"), P(None, "tp"), P("tp")
    heads = P(None, "tp", None)
    return jax.shard_map(
        shards,
        mesh=mesh,
        in_specs=(
            rows,
            rows,
            columns,
            three_dims,
            rows,
            heads,
            columns,
            three_dims,
            last_only,
            one_dim,
            one_dim,
            columns,
            rows,
            columns,
            last_only,
            rows,
        ),
        out_specs=(
            rows,
            rows,
            rows,
            columns,
            three_dims,
            rows,
            heads,
            columns,
            three_dims,
            last_only,
            one_dim,
            one_dim,
            columns,
            rows,
            columns,
            last_only,
        ),
        check_vma=False,
    )
```

```python
import functools
import math

import jax
import jax.numpy as jnp
from jax import lax
from jax.experimental import pallas as pl
from jax.experimental.pallas import tpu as pltpu
from jax.sharding import PartitionSpec as P

F32 = jnp.float32
BF16 = jnp.bfloat16
EPSILON = 1e-05
HALO = 16
BLOCK = 128
VMEM_BYTES = 16 * 1024 * 1024
COST = 1


def call(body, outs, *args, after=(), scratch=(), results=False, vmem=VMEM_BYTES):
    first, extra = len(args), len(after)

    def kernel(*refs):
        body(*refs[:first], *refs[first + extra :])

    return pl.pallas_call(
        kernel,
        out_shape=[jax.ShapeDtypeStruct(*out) for out in outs],
        in_specs=[pl.BlockSpec(memory_space=pltpu.SMEM)]
        + [pl.BlockSpec(memory_space=pltpu.VMEM)] * (first - 1)
        + [pl.BlockSpec(memory_space=pl.ANY)] * extra,
        out_specs=[pl.BlockSpec() if results else pl.BlockSpec(memory_space=pltpu.VMEM)]
        * len(outs),
        scratch_shapes=list(scratch),
        compiler_params=pltpu.CompilerParams(vmem_limit_bytes=vmem),
        cost_estimate=pl.CostEstimate(flops=COST, bytes_accessed=COST, transcendentals=0),
    )(*args, *after)


def dot(left, right):
    return jnp.dot(left, right, preferred_element_type=F32)


def dot_cols(left, right):
    return lax.dot_general(left, right, (((1,), (1,)), ((), ())), preferred_element_type=F32)


def dot_rows(left, right):
    return lax.dot_general(left, right, (((0,), (0,)), ((), ())), preferred_element_type=F32)


def normalized(stream):
    centred = stream - jnp.mean(stream, axis=1, keepdims=True)
    spread = lax.rsqrt(jnp.mean(centred * centred, axis=1, keepdims=True) + EPSILON)
    return centred * spread, spread


def norm_pullback(grad, stream, gain):
    normal, spread = normalized(stream)
    scaled = grad * gain
    first = jnp.mean(scaled, axis=1, keepdims=True)
    second = jnp.mean(scaled * normal, axis=1, keepdims=True)
    return spread * (scaled - first - normal * second), jnp.sum(
        grad * normal, axis=0, keepdims=True
    )


def swish_slope(value, logistic):
    return logistic * (1.0 + value * (1.0 - logistic))


def halves(idx, rows):
    half = rows // 2
    mine = pl.multiple_of(idx[1] * half, half)
    theirs = pl.multiple_of((1 - idx[1]) * half, half)
    return pl.ds(mine, half), pl.ds(theirs, half)


def split(idx, whole, keep, send):
    mine, theirs = halves(idx, whole.shape[0])
    keep[...] = whole[mine, :].astype(BF16)
    send[...] = whole[theirs, :].astype(BF16)


def join(idx, t_mine, t_theirs, whole):
    mine, theirs = halves(idx, whole.shape[0])
    whole[mine, :] = t_mine[...].astype(F32)
    whole[theirs, :] = t_theirs[...].astype(F32)


def xor_pairs(count, step):
    return [(i, i ^ step) for i in range(count)]


def swap(value, axis, step):
    return lax.ppermute(value, axis, xor_pairs(lax.axis_size(axis), step))


def added(left, right):
    return (left.astype(F32) + right.astype(F32)).astype(BF16)


def added_body(idx, left, right, out):
    out[...] = (left[...].astype(F32) + right[...].astype(F32)).astype(BF16)


def added_after(idx, left, right, after):
    return call(added_body, [(left.shape, left.dtype)], idx, left, right, after=after)[0]


def tp_begin(keep, send, idx=None, after=()):
    other = swap(send, "tp", 1)
    return added_after(idx, keep, other, after) if after else added(keep, other)


def tp_end(idx, total, after=()):
    other = swap(total, "tp", 2)
    total = added_after(idx, total, other, after) if after else added(total, other)
    return total, swap(total, "tp", 1)


def tp_sum(keep, send):
    return tp_end(None, tp_begin(keep, send))


def place_body(ctx, idx, *refs):
    out = refs[-1]
    rows = refs[0].shape[0]
    blocks = []
    for ref in refs[:-1]:
        for at in range(ref.shape[0] // rows):
            blocks.append(ref[at * rows : (at + 1) * rows, :])
    for at, block in enumerate(blocks):
        half = idx[2] if at < ctx else 1 - idx[2]
        target = half * ctx + jnp.bitwise_xor(idx[3], at % ctx)
        out[pl.ds(pl.multiple_of(target * rows, rows), rows), :] = block


def pack_body(idx, tokens, cot, gains, out):
    rows = tokens.shape[0]
    out[:rows, :] = tokens[...]
    out[rows : 2 * rows, :] = cot[...]
    rest = gains[...]
    pieces = []
    for unused in range(3):
        piece = rest.astype(BF16).astype(F32)
        pieces.append(piece)
        rest = rest - piece
    pieces.append(jnp.zeros((1, rest.shape[1]), F32))
    out[2 * rows :, :] = jnp.concatenate(pieces, axis=0).astype(BF16)


def features_body(idx, *refs):
    blocks = refs[:4]
    x_out, cot_out, gains_out = refs[4:]
    rows, features = x_out.shape
    part = features // 4
    for at in range(4):
        target = jnp.bitwise_xor(idx[0], at)
        columns = pl.ds(pl.multiple_of(target * part, part), part)
        x_out[:, columns] = blocks[at][:rows, :]
        cot_out[:, columns] = blocks[at][rows : 2 * rows, :]
        pieces = blocks[at][2 * rows :, :].astype(F32)
        gains_out[:, columns] = (pieces[0:5] + pieces[5:10]) + pieces[10:15]


def finish_body(layout, parts, idx, *refs):
    total = refs[0][...].astype(F32)
    for ref in refs[1:parts]:
        total = total + ref[...].astype(F32)
    column = 0
    for (kind, width), out in zip(layout, refs[parts:]):
        if kind == "middle":
            count = out.shape[0]
            each = width // count
            for at in range(count):
                out[at] = total[:, column + at * each : column + (at + 1) * each]
        else:
            out[...] = total[:, column : column + width]
        column += width


def finish_small_body(idx, left, right, gains_out, bias_out, kernel_out):
    total = left[...] + right[...]
    gains_out[...] = total[:5]
    heads, size = bias_out.shape[1:]
    for head in range(heads):
        bias_out[:, head, :] = total[5:7, head * size : (head + 1) * size]
    kernel_out[...] = total[7 : 7 + kernel_out.shape[0]]


def wgrad_body(pairs, ordered, ctx, idx, *refs):
    out, scratch = refs[2 * pairs], refs[2 * pairs + 1]
    column = 0
    for at in range(pairs):
        left, right = refs[2 * at], refs[2 * at + 1]
        width = right.shape[1]
        product = dot_rows(left[...], right[...]).astype(BF16)
        if ordered:
            out[:, column : column + width] = product
        else:
            scratch[:, column : column + width] = product
        column += width
    if not ordered:
        rows = out.shape[0] // (2 * ctx)
        for at in range(2 * ctx):
            half = idx[2] if at < ctx else 1 - idx[2]
            source = half * ctx + jnp.bitwise_xor(idx[3], at % ctx)
            out[at * rows : (at + 1) * rows, :] = scratch[
                pl.ds(pl.multiple_of(source * rows, rows), rows), :
            ]


def feed_body(gain_at, base, joined, idx, *refs):
    if joined:
        x_ref, t1, t2, gains, weights, x_out, z_out, u_out, h_out, keep, send, work = refs
        join(idx, t1, t2, work)
        x = x_ref[...] + work[...]
        x_out[...] = x
    else:
        x_ref, gains, weights, z_out, u_out, h_out, keep, send, work = refs
        x = x_ref[...].astype(F32)
    hidden = u_out.shape[1]
    normal, unused = normalized(x)
    z = (normal * gains[gain_at : gain_at + 1, :]).astype(BF16)
    z_out[...] = z
    u = dot(z, weights[:, base : base + hidden])
    u_out[...] = u
    h = (u * jax.nn.sigmoid(u)).astype(BF16)
    h_out[...] = h
    work[...] = dot_cols(h, weights[:, base + hidden : base + 2 * hidden])
    split(idx, work, keep, send)


def attend_in_body(idx, x_ref, t1, t2, gains, weights, bias, x_out, z_out, qa, qb, kv, work):
    join(idx, t1, t2, work)
    x = x_ref[...].astype(F32) + 0.5 * work[...]
    x_out[...] = x
    normal, unused = normalized(x)
    z = (normal * gains[1:2, :]).astype(BF16)
    z_out[...] = z
    local = bias.shape[1]
    project = dot(z, weights[:, : 3 * local])
    query = project[:, :local]
    qa[...] = (query + bias[0:1, :]).astype(BF16)
    qb[...] = (query + bias[1:2, :]).astype(BF16)
    kv[...] = project[:, local:].astype(BF16)


def relative_body(base, idx, near_p, near_q, far_c, far_s, weights, embed, relative):
    step = far_c.shape[0]
    cos, sin = far_c[...], far_s[...]
    for at in range(embed.shape[0] // step):
        value = near_p[at : at + 1, :] * cos + near_q[at : at + 1, :] * sin
        embed[at * step : (at + 1) * step, :] = value.astype(BF16)
    relative[...] = dot(embed[...], weights[:, base : base + relative.shape[1]]).astype(BF16)


def position_body(heads, idx, qb, relative, out):
    rows, local = qb.shape
    size = local // heads
    length = out.shape[2]
    width = length + BLOCK
    for head in range(heads):
        columns = slice(head * size, (head + 1) * size)
        for at in range(rows // BLOCK):
            frames = slice(at * BLOCK, (at + 1) * BLOCK)
            first = rows - BLOCK * (at + 1)
            wide = dot_cols(qb[frames, columns], relative[first : first + width, columns])
            turned = pltpu.roll(wide, width - (BLOCK - 1), 1, stride=1, stride_axis=0)
            out[head, frames, :] = turned[:, :length]


def fill_pairs(idx, blocks, whole):
    rows = blocks[0].shape[0]
    for at, block in enumerate(blocks):
        target = jnp.bitwise_xor(idx[3], at)
        whole[pl.ds(pl.multiple_of(target * rows, rows), rows), :] = block[...]


def attend_body(heads, ctx, base, idx, qa, *refs):
    blocks = refs[:ctx]
    position, weights, p_out, mixed, keep, send, pairs, work = refs[ctx:]
    fill_pairs(idx, blocks, pairs)
    rows, local = qa.shape
    size = local // heads
    scale = size**-0.5
    for head in range(heads):
        columns = slice(head * size, (head + 1) * size)
        values = slice(local + head * size, local + (head + 1) * size)
        for at in range(rows // BLOCK):
            frames = slice(at * BLOCK, (at + 1) * BLOCK)
            scores = (dot_cols(qa[frames, columns], pairs[:, columns]) + position[head, frames, :]) * scale
            raised = jnp.exp(scores - jnp.max(scores, axis=1, keepdims=True))
            share = (raised / jnp.sum(raised, axis=1, keepdims=True)).astype(BF16)
            p_out[head, frames, :] = share
            mixed[frames, columns] = dot(share, pairs[:, values]).astype(BF16)
    work[...] = dot_cols(mixed[...], weights[:, base : base + local])
    split(idx, work, keep, send)


def conv_in_body(idx, x_ref, t1, t2, gains, weights, x_out, z_out, g_out, glu, first, last, work):
    join(idx, t1, t2, work)
    x = x_ref[...] + work[...]
    x_out[...] = x
    normal, unused = normalized(x)
    z = (normal * gains[2:3, :]).astype(BF16)
    z_out[...] = z
    rows, channels = glu.shape
    paired = dot(z, weights[:, : 2 * channels])
    g_out[...] = paired
    gated = (paired[:, :channels] * jax.nn.sigmoid(paired[:, channels:])).astype(BF16)
    glu[...] = gated
    first[...] = gated[:HALO, :]
    last[...] = gated[rows - HALO :, :]


def fill_padded(low, own, high, padded):
    rows = own.shape[0]
    padded[:HALO, :] = low[...].astype(F32)
    padded[HALO : HALO + rows, :] = own[...].astype(F32)
    padded[HALO + rows :, :] = high[...].astype(F32)


def conv_body(idx, glu, low, high, kernel, c_out, stats, padded):
    fill_padded(low, glu, high, padded)
    rows = glu.shape[0]
    taps = kernel.shape[0]
    shift = HALO - (taps - 1) // 2
    total = kernel[0:1, :] * padded[shift : shift + rows, :]
    for tap in range(1, taps):
        total = total + kernel[tap : tap + 1, :] * padded[shift + tap : shift + tap + rows, :]
    c_out[...] = total
    mean = jnp.mean(total, axis=0, keepdims=True)
    centred = total - mean
    stats[0:1, :] = mean
    stats[1:2, :] = jnp.sum(centred * centred, axis=0, keepdims=True)
    stats[2:, :] = jnp.zeros((stats.shape[0] - 2, stats.shape[1]), F32)


def batch_body(base, idx, c, stats, params, weights, q_out, act_out, keep, send, work):
    spread = stats[1:2, :]
    q = (c[...] - stats[0:1, :]) * spread
    q_out[...] = q
    a = q * params[0:1, :] + params[1:2, :]
    act = (a * jax.nn.sigmoid(a)).astype(BF16)
    act_out[...] = act
    work[...] = dot_cols(act, weights[:, base : base + act.shape[1]])
    split(idx, work, keep, send)


def feed_pullback(idx, grad, u, weights, base, f_out, du_out, keep, send, work):
    hidden = u.shape[1]
    f = (0.5 * grad).astype(BF16)
    f_out[...] = f
    value = u[...]
    logistic = jax.nn.sigmoid(value)
    back = dot(f, weights[:, base + hidden : base + 2 * hidden])
    du = (back * swish_slope(value, logistic)).astype(BF16)
    du_out[...] = du
    work[...] = dot_cols(du, weights[:, base : base + hidden])
    split(idx, work, keep, send)


def final_body(base, idx, x_ref, t1, t2, gains, cot, u, weights, y_out, d_out, gain_out, f_out, du_out, keep, send, work):
    join(idx, t1, t2, work)
    x = x_ref[...] + 0.5 * work[...]
    normal, unused = normalized(x)
    gain = gains[4:5, :]
    work[...] = normal * gain
    width = y_out.shape[1]
    y_out[...] = work[:, pl.ds(pl.multiple_of(idx[0] * width, width), width)].astype(BF16)
    grad, gain_grad = norm_pullback(cot[...].astype(F32), x, gain)
    gain_out[...] = gain_grad
    d_out[...] = grad
    feed_pullback(idx, grad, u, weights, base, f_out, du_out, keep, send, work)


def conv_back_body(base, idx, x_ref, d_ref, t1, t2, gains, q, params, weights, d_out, f_out, da_out, edges, gain_out, work):
    join(idx, t1, t2, work)
    grad, gain_grad = norm_pullback(work[...], x_ref[...], gains[3:4, :])
    gain_out[...] = gain_grad
    grad = d_ref[...] + grad
    d_out[...] = grad
    f = grad.astype(BF16)
    f_out[...] = f
    rows, channels = q.shape
    value = q[...]
    a = value * params[0:1, :] + params[1:2, :]
    da = dot(f, weights[:, base : base + channels]) * swish_slope(a, jax.nn.sigmoid(a))
    da_out[...] = da
    edges[0:1, :] = jnp.sum(da * value, axis=0, keepdims=True)
    edges[1:2, :] = jnp.sum(da, axis=0, keepdims=True)
    edges[2:8, :] = jnp.zeros((6, channels), F32)
    for at, part in enumerate((da[:HALO], value[:HALO], da[rows - HALO :], value[rows - HALO :])):
        edges[8 + at * HALO : 8 + (at + 1) * HALO, :] = part


def gate_back_body(ctx, counted, idx, da, q, own, near, far, stats, params, kernel, paired, weights, sums, dc_out, dg_out, keep, send, padded, work):
    rows, channels = q.shape
    sums[...] = own[:8, :] + far[:8, :]
    odd = idx[3] % 2 == 1
    low = jnp.where(odd, near[8 + 2 * HALO :, :], far[8 + 2 * HALO :, :])
    high = jnp.where(odd, far[8 : 8 + 2 * HALO, :], near[8 : 8 + 2 * HALO, :])
    factor = stats[1:2, :] * params[0:1, :]
    mean_scale = sums[0:1, :] / counted
    mean_shift = sums[1:2, :] / counted

    def centred(grad, normal):
        return (factor * (grad - mean_shift - normal * mean_scale)).astype(BF16)

    dc = centred(da[...], q[...])
    dc_out[...] = dc
    before = (idx[3] > 0).astype(F32)
    after = (idx[3] < ctx - 1).astype(F32)
    padded[:HALO, :] = centred(low[:HALO, :], low[HALO:, :]).astype(F32) * before
    padded[HALO : HALO + rows, :] = dc.astype(F32)
    padded[HALO + rows :, :] = centred(high[:HALO, :], high[HALO:, :]).astype(F32) * after
    taps = kernel.shape[0]
    top = HALO + (taps - 1) // 2
    total = kernel[0:1, :] * padded[top : top + rows, :]
    for tap in range(1, taps):
        total = total + kernel[tap : tap + 1, :] * padded[top - tap : top - tap + rows, :]
    logistic = jax.nn.sigmoid(paired[:, channels:])
    through = total * logistic
    dg_out[:, :channels] = through.astype(BF16)
    dg_out[:, channels:] = (through * paired[:, :channels] * (1.0 - logistic)).astype(BF16)
    work[...] = dot_cols(dg_out[...], weights[:, : 2 * channels])
    split(idx, work, keep, send)


def taps_body(idx, glu, low, high, dc, out, padded):
    fill_padded(low, glu, high, padded)
    rows = glu.shape[0]
    grad = dc[...].astype(F32)
    shift = HALO - (out.shape[0] - 1) // 2
    for tap in range(out.shape[0]):
        out[tap : tap + 1, :] = jnp.sum(
            grad * padded[shift + tap : shift + tap + rows, :], axis=0, keepdims=True
        )


def attend_back_body(heads, ctx, base, idx, x_ref, d_ref, t1, t2, gains, weights, p, qa, *refs):
    blocks = refs[:ctx]
    d_out, f_out, gain_out, ds_out, dqa = refs[ctx : ctx + 5]
    out_blocks = refs[ctx + 5 : 2 * ctx + 5]
    pairs, grads, do, work = refs[2 * ctx + 5 :]
    fill_pairs(idx, blocks, pairs)
    join(idx, t1, t2, work)
    grad, gain_grad = norm_pullback(work[...], x_ref[...], gains[2:3, :])
    gain_out[...] = gain_grad
    grad = d_ref[...] + grad
    d_out[...] = grad
    f = grad.astype(BF16)
    f_out[...] = f
    rows, local = qa.shape
    size = local // heads
    scale = size**-0.5
    do[...] = dot(f, weights[:, base : base + local]).astype(BF16)
    for head in range(heads):
        columns = slice(head * size, (head + 1) * size)
        values = slice(local + head * size, local + (head + 1) * size)
        for at in range(rows // BLOCK):
            frames = slice(at * BLOCK, (at + 1) * BLOCK)
            dp = dot_cols(do[frames, columns], pairs[:, values])
            share = p[head, frames, :].astype(F32)
            balance = jnp.sum(share * dp, axis=1, keepdims=True)
            ds = (share * (dp - balance)).astype(BF16)
            ds_out[head, frames, :] = ds
            dqa[frames, columns] = dot(ds, pairs[:, columns]) * scale
        grads[:, columns] = (dot_rows(ds_out[head], qa[:, columns]) * scale).astype(BF16)
        grads[:, values] = dot_rows(p[head], do[:, columns]).astype(BF16)
    for at, block in enumerate(out_blocks):
        source = jnp.bitwise_xor(idx[3], at)
        block[...] = grads[pl.ds(pl.multiple_of(source * rows, rows), rows), :]


def position_back_body(heads, idx, ds, qb, relative, dqb, dr_out, wide, total):
    rows, local = qb.shape
    size = local // heads
    length = ds.shape[2]
    width = length + BLOCK
    scale = size**-0.5
    down = lax.broadcasted_iota(jnp.int32, (BLOCK, BLOCK), 0)
    across = lax.broadcasted_iota(jnp.int32, (BLOCK, BLOCK), 1)
    flip = (down + across == BLOCK - 1).astype(BF16)
    total[...] = jnp.zeros(total.shape, F32)
    wide[:, length:] = jnp.zeros((BLOCK, BLOCK), F32)
    for head in range(heads):
        columns = slice(head * size, (head + 1) * size)
        for at in range(rows // BLOCK):
            frames = slice(at * BLOCK, (at + 1) * BLOCK)
            first = rows - BLOCK * (at + 1)
            wide[:, :length] = dot(flip, ds[head, frames, :])
            turned = pltpu.roll(wide[...], 0, 1, stride=1, stride_axis=0).astype(BF16)
            turned_b = dot(turned, relative[first : first + width, columns]) * scale
            dqb[frames, columns] = jnp.dot(
                flip.astype(F32), turned_b, precision=lax.Precision.HIGHEST, preferred_element_type=F32
            )
            flipped = dot(flip, qb[frames, columns]).astype(BF16)
            total[first : first + width, columns] += dot_rows(turned, flipped)
    dr_out[...] = (total[...] * scale).astype(BF16)


def attend_out_body(ctx, idx, dqa, dqb, *refs):
    blocks = refs[:ctx]
    weights, dp_out, bias_out, keep, send, work = refs[ctx:]
    local = dqa.shape[1]
    bias_out[0:1, :] = jnp.sum(dqa[...], axis=0, keepdims=True)
    bias_out[1:2, :] = jnp.sum(dqb[...], axis=0, keepdims=True)
    dp_out[:, :local] = (dqa[...] + dqb[...]).astype(BF16)
    total = blocks[0][...].astype(F32)
    for block in blocks[1:]:
        total = total + block[...].astype(F32)
    dp_out[:, local:] = total.astype(BF16)
    work[...] = dot_cols(dp_out[...], weights[:, : 3 * local])
    split(idx, work, keep, send)


def feed_back_body(idx, x_ref, d_ref, t1, t2, gains, u, weights, d_out, f_out, du_out, gain_out, keep, send, work):
    join(idx, t1, t2, work)
    grad, gain_grad = norm_pullback(work[...], x_ref[...], gains[1:2, :])
    gain_out[...] = gain_grad
    grad = d_ref[...] + grad
    d_out[...] = grad
    feed_pullback(idx, grad, u, weights, 0, f_out, du_out, keep, send, work)


def last_body(idx, x_ref, d_ref, t1, t2, gains, two, three, four, five, bias, kernel, out, small, work, each):
    join(idx, t1, t2, work)
    grad, gain_grad = norm_pullback(work[...], x_ref[...].astype(F32), gains[0:1, :])
    for at, row in enumerate((gain_grad, two[...], three[...], four[...], five[...])):
        each[at : at + 1, :] = row
    part = out.shape[1]
    own = pl.ds(pl.multiple_of(idx[0] * part, part), part)
    taps = kernel.shape[0]
    small[:5, :] = each[:5, own]
    small[5:7, :] = bias[...]
    small[7 : 7 + taps, :] = kernel[...]
    small[7 + taps :, :] = jnp.zeros((small.shape[0] - 7 - taps, part), F32)
    work[...] = d_ref[...] + grad
    width = out.shape[1]
    out[...] = work[:, pl.ds(pl.multiple_of(idx[0] * width, width), width)]


FRAMES = ("fsdp", "ctx")


def paired_mesh():
    return lax.axis_size("fsdp") == 2


def gathered(idx, shard, after=()):
    if not paired_mesh():
        return lax.all_gather(shard, FRAMES, axis=0, tiled=True), shard
    ctx = lax.axis_size("ctx")
    if after:
        shard = held(idx, shard, after)
    mine = [shard] + [swap(shard, "ctx", step) for step in range(1, ctx)]
    if after:
        mark = jnp.concatenate(mine, axis=0)
        theirs = [swap(mark, "fsdp", 1)]
    else:
        mark = jnp.concatenate(mine[1:], axis=0)
        theirs = [swap(shard, "fsdp", 1), swap(mark, "fsdp", 1)]
    rows, width = shard.shape
    outs = [((2 * ctx * rows, width), BF16)]
    return call(functools.partial(place_body, ctx), outs, idx, *mine, *theirs)[0], mark


def features_whole(value):
    far = swap(value, "tp", 2)
    return [value, swap(value, "tp", 1), far, swap(far, "tp", 1)]


def weight_grads(idx, pairs, ordered):
    depth = pairs[0][0].shape[1]
    width = sum(right.shape[1] for unused, right in pairs)
    flat = [array for pair in pairs for array in pair]
    ctx = lax.axis_size("ctx")
    return call(
        functools.partial(wgrad_body, len(pairs), ordered, ctx),
        [((depth, width), BF16)],
        idx,
        *flat,
        scratch=[pltpu.VMEM((8, 128) if ordered else (depth, width), BF16)],
    )[0]


def scattered(idx, pairs, layout):
    grads = weight_grads(idx, pairs, not paired_mesh())
    rows = grads.shape[0] // lax.axis_size(FRAMES)

    def formed(values):
        turns = {"rows": lambda v: v, "turned": lambda v: v.T, "middle": lambda v: v.swapaxes(0, 1)}
        return [turns[kind](value) for (kind, unused, unused), value in zip(layout, values)]

    if not paired_mesh():
        total = lax.psum_scatter(grads, FRAMES, scatter_dimension=0, tiled=True).astype(F32)

        def whole(after=()):
            values, column = [], 0
            for kind, count, width in layout:
                value = total[:, column : column + width]
                if kind == "middle":
                    value = value.reshape(rows, count, width // count).swapaxes(0, 1)
                values.append(value)
                column += width
            return formed(values)

        return grads, grads, lambda after=(): (grads, whole)
    ctx = lax.axis_size("ctx")
    half = grads.shape[0] // 2
    other = swap(grads[half:], "fsdp", 1)

    def along(after=()):
        total = added_after(idx, grads[:half], other, after)
        parts = [total[:rows]]
        for step in range(1, ctx):
            parts.append(swap(total[step * rows : (step + 1) * rows], "ctx", step))

        def finish(after=()):
            shapes = [
                ((count, rows, width // count) if kind == "middle" else (rows, width), F32)
                for kind, count, width in layout
            ]
            kinds = [(kind, width) for kind, unused, width in layout]
            body = functools.partial(finish_body, kinds, ctx)
            return formed(call(body, shapes, idx, *parts, after=after, results=True))

        return total, finish

    return grads, other, along


def hold_body(idx, value, out):
    out[...] = value[...]


def held(idx, value, after):
    return call(hold_body, [(value.shape, value.dtype)], idx, value, after=after)[0]


def over_frames(value, merge):
    for axis in ("fsdp", "ctx"):
        step = 1
        while step < lax.axis_size(axis):
            value = merge(value, swap(value, axis, step))
            step *= 2
    return value


def pooled(stats, rows):
    count = [rows]

    def merge(left, right):
        gap = left[0:1] - right[0:1]
        mean = 0.5 * (left[0:1] + right[0:1])
        squares = left[1:2] + right[1:2] + gap * gap * (0.5 * count[0])
        count[0] *= 2
        return jnp.concatenate([mean, squares, left[2:]], axis=0)

    stats = over_frames(stats, merge)
    spread = lax.rsqrt(stats[1:2] / count[0] + EPSILON)
    return jnp.concatenate([stats[0:1], spread, stats[2:]], axis=0)


def edges_summed(edges):
    step = 1
    while step < lax.axis_size("fsdp"):
        edges = jnp.concatenate([edges[:8] + swap(edges[:8], "fsdp", step), edges[8:]], axis=0)
        step *= 2
    near = swap(edges, "ctx", 1)
    own = jnp.concatenate([edges[:8] + near[:8], edges[8:]], axis=0)
    return own, near, swap(own, "ctx", 3)


def neighbours(first, last):
    count = lax.axis_size("ctx")
    up = [(i, i + 1) for i in range(count - 1)]
    down = [(i + 1, i) for i in range(count - 1)]
    return lax.ppermute(last, "ctx", up), lax.ppermute(first, "ctx", down)


def angle_tables(start, rows, width, features):
    step = 64
    column = jnp.arange(features, dtype=jnp.int32)
    rates = jnp.exp((column // 2).astype(F32) * (-2.0 * math.log(10000.0) / features))
    even = (column % 2 == 0)[None, :]
    near = (start + rows - 1 - step * jnp.arange(width // step, dtype=jnp.int32)).astype(F32)
    near = near[:, None] * rates[None, :]
    far = jnp.arange(step, dtype=jnp.int32).astype(F32)[:, None] * rates[None, :]
    sine, cosine = jnp.sin(near), jnp.cos(near)
    return (
        jnp.where(even, sine, cosine),
        jnp.where(even, -cosine, sine),
        jnp.cos(far),
        jnp.sin(far),
    )


def shards(
    tokens,
    first_expand,
    first_shrink,
    attend_input,
    position_map,
    position_bias,
    attend_output,
    gating_map,
    depth_kernel,
    batch_scale,
    batch_shift,
    mixing_map,
    second_expand,
    second_shrink,
    layer_gains,
    cotangent,
):
    rows, part = tokens.shape
    tp, ctx = lax.axis_size("tp"), lax.axis_size("ctx")
    features = part * tp
    shard = first_expand.shape[0]
    hidden = first_expand.shape[1]
    heads, size = position_bias.shape[1:]
    local = heads * size
    channels = depth_kernel.shape[1]
    length = rows * ctx
    width = length + rows
    tp_at = lax.axis_index("tp")
    ctx_at = lax.axis_index("ctx")
    idx = jnp.stack(
        [tp_at, tp_at % 2, lax.axis_index("fsdp"), ctx_at]
    ).astype(jnp.int32)

    one, one_mark = gathered(idx, jnp.concatenate([first_expand, first_shrink.T], axis=1))
    frames = call(
        pack_body, [((2 * rows + 16, part), BF16)], idx, tokens, cotangent, layer_gains
    )[0]
    x0, cot, gains = call(
        features_body,
        [((rows, features), BF16), ((rows, features), BF16), ((5, features), F32)],
        idx,
        *features_whole(frames),
    )
    bias = position_bias.reshape(2, local)
    params = jnp.stack([batch_scale, batch_shift])
    tables = angle_tables(ctx_at * rows, rows, width, features)
    thirds = [attend_input[:, at] for at in range(3)]
    two, two_mark = gathered(
        idx,
        jnp.concatenate(thirds + [position_map, attend_output.T], axis=1),
        [one_mark],
    )
    halves_in = [gating_map[:, at] for at in range(2)]
    three, three_mark = gathered(
        idx,
        jnp.concatenate(halves_in + [mixing_map.T, second_expand, second_shrink.T], axis=1),
        [two_mark],
    )
    at_pos, at_out = 3 * local, 4 * local
    at_mix, at_two = 2 * channels, 3 * channels

    stream = ((rows, features), F32)
    packed = ((rows, features), BF16)
    piece = ((rows // 2, features), BF16)
    gain_row = ((1, features), F32)
    work = pltpu.VMEM((rows, features), F32)
    inner_shape = (rows, hidden)

    z1, u1, h1, keep, send = call(
        functools.partial(feed_body, 0, 0, False),
        [packed, (inner_shape, F32), (inner_shape, BF16), piece, piece],
        idx,
        x0,
        gains,
        one,
        after=[two_mark],
        scratch=[work],
    )
    t1, t2 = tp_end(idx, tp_begin(keep, send), [three_mark, two])
    embed, relative = call(
        functools.partial(relative_body, at_pos),
        [((width, features), BF16), ((width, local), BF16)],
        idx,
        *tables,
        two,
    )
    per_head = ((rows, local), BF16)
    x1, z2, qa, qb, kv = call(
        attend_in_body,
        [stream, packed, per_head, per_head, ((rows, 2 * local), BF16)],
        idx,
        x0,
        t1,
        t2,
        gains,
        two,
        bias,
        scratch=[work],
    )
    pairs = [kv] + [swap(kv, "ctx", step) for step in range(1, ctx)]
    position = call(
        functools.partial(position_body, heads),
        [((heads, rows, length), F32)],
        idx,
        qb,
        relative,
        after=[three],
    )[0]
    whole_pairs = pltpu.VMEM((length, 2 * local), BF16)
    p, mixed, keep, send = call(
        functools.partial(attend_body, heads, ctx, at_out),
        [((heads, rows, length), BF16), per_head, piece, piece],
        idx,
        qa,
        *pairs,
        position,
        two,
        scratch=[whole_pairs, work],
    )
    t1, t2 = tp_sum(keep, send)
    edge = ((HALO, channels), BF16)
    x2, z3, paired, glu, first, last = call(
        conv_in_body,
        [
            stream,
            packed,
            ((rows, 2 * channels), F32),
            ((rows, channels), BF16),
            edge,
            edge,
        ],
        idx,
        x1,
        t1,
        t2,
        gains,
        three,
        scratch=[work],
    )
    low, high = neighbours(first, last)
    padded = pltpu.VMEM((rows + 2 * HALO, channels), F32)
    c, stats = call(
        conv_body,
        [((rows, channels), F32), ((8, channels), F32)],
        idx,
        glu,
        low,
        high,
        depth_kernel,
        scratch=[padded],
    )
    stats = pooled(stats, rows)
    q, act, keep, send = call(
        functools.partial(batch_body, at_mix),
        [((rows, channels), F32), ((rows, channels), BF16), piece, piece],
        idx,
        c,
        stats,
        params,
        three,
        scratch=[work],
    )
    t1, t2 = tp_sum(keep, send)
    x3, z4, u2, h2, keep, send = call(
        functools.partial(feed_body, 3, at_two, True),
        [stream, packed, (inner_shape, F32), (inner_shape, BF16), piece, piece],
        idx,
        x2,
        t1,
        t2,
        gains,
        three,
        scratch=[work],
    )
    t1, t2 = tp_sum(keep, send)
    outputs, d4, gain_five, f4, du2, keep, send = call(
        functools.partial(final_body, at_two),
        [
            ((rows, part), BF16),
            stream,
            gain_row,
            packed,
            (inner_shape, BF16),
            piece,
            piece,
        ],
        idx,
        x3,
        t1,
        t2,
        gains,
        cot,
        u2,
        three,
        scratch=[work],
    )
    total = tp_begin(keep, send)
    made_rear, other_rear, rear = scattered(
        idx, [(z4, du2), (f4, h2)], [("rows", 1, hidden), ("turned", 1, hidden)]
    )
    t1, t2 = tp_end(idx, total, [made_rear])
    d3, f3, da, edges, gain_four = call(
        functools.partial(conv_back_body, at_mix),
        [
            stream,
            packed,
            ((rows, channels), F32),
            ((8 + 4 * HALO, channels), F32),
            gain_row,
        ],
        idx,
        x3,
        d4,
        t1,
        t2,
        gains,
        q,
        params,
        three,
        scratch=[work],
    )
    own, near, far = edges_summed(edges)
    counted = rows * lax.axis_size(FRAMES)
    sums, dc, dg, keep, send = call(
        functools.partial(gate_back_body, ctx, counted),
        [
            ((8, channels), F32),
            ((rows, channels), BF16),
            ((rows, 2 * channels), BF16),
            piece,
            piece,
        ],
        idx,
        da,
        q,
        own,
        near,
        far,
        stats,
        params,
        depth_kernel,
        paired,
        three,
        after=[other_rear],
        scratch=[padded, work],
    )
    total = tp_begin(keep, send)
    kernel_grad = call(
        taps_body,
        [(depth_kernel.shape, F32)],
        idx,
        glu,
        low,
        high,
        dc,
        scratch=[padded],
    )[0]
    made_middle, other_middle, middle = scattered(
        idx,
        [(z3, dg), (f3, act)],
        [("middle", 2, 2 * channels), ("turned", 1, channels)],
    )
    rear_total, rear = rear([total])
    t1, t2 = tp_end(idx, total, [made_middle, kernel_grad, rear_total])
    pair_block = ((rows, 2 * local), BF16)
    results = call(
        functools.partial(attend_back_body, heads, ctx, at_out),
        [stream, packed, gain_row, ((heads, rows, length), BF16), ((rows, local), F32)]
        + [pair_block] * ctx,
        idx,
        x2,
        d3,
        t1,
        t2,
        gains,
        two,
        p,
        qa,
        *pairs,
        scratch=[whole_pairs, whole_pairs, pltpu.VMEM((rows, local), BF16), work],
    )
    d2, f2, gain_three, ds, dqa = results[:5]
    pair_grads = [results[5]] + [
        swap(block, "ctx", step + 1) for step, block in enumerate(results[6:])
    ]
    dqb, dr = call(
        functools.partial(position_back_body, heads),
        [((rows, local), F32), ((width, local), BF16)],
        idx,
        ds,
        qb,
        relative,
        scratch=[pltpu.VMEM((BLOCK, length + BLOCK), F32), pltpu.VMEM((width, local), F32)],
    )
    rear_expand, rear_shrink = rear([ds])
    dp, bias_grad, keep, send = call(
        functools.partial(attend_out_body, ctx),
        [((rows, 3 * local), BF16), ((2, local), F32), piece, piece],
        idx,
        dqa,
        dqb,
        *pair_grads,
        two,
        after=[rear_expand, other_middle],
        scratch=[work],
    )
    total = tp_begin(keep, send)
    made_inner, other_inner, inner = scattered(
        idx,
        [(z2, dp), (embed, dr), (f2, mixed)],
        [("middle", 3, 3 * local), ("rows", 1, local), ("turned", 1, local)],
    )
    middle_total, middle = middle([total])
    t1, t2 = tp_end(idx, total, [made_inner, middle_total])
    gate_grad, mix_grad = middle([total])
    d1, f1, du1, gain_two, keep, send = call(
        feed_back_body,
        [stream, ((rows, features), BF16), (inner_shape, BF16), gain_row, piece, piece],
        idx,
        x1,
        d2,
        t1,
        t2,
        gains,
        u1,
        one,
        after=[mix_grad],
        scratch=[work],
    )
    made_front, unused, front = scattered(
        idx, [(z1, du1), (f1, h1)], [("rows", 1, hidden), ("turned", 1, hidden)]
    )
    total = tp_begin(keep, send, idx, [made_front, other_inner])
    inner_total, inner = inner([total])
    t1, t2 = tp_end(idx, total, [inner_total])
    taps = depth_kernel.shape[0]
    tokens_grad, small = call(
        last_body,
        [((rows, part), F32), ((-(-(7 + taps) // 8) * 8, part), F32)],
        idx,
        x0,
        d1,
        t1,
        t2,
        gains,
        gain_two,
        gain_three,
        gain_four,
        gain_five,
        bias_grad,
        kernel_grad,
        scratch=[work, pltpu.VMEM((8, features), F32)],
    )
    steps = [
        (axis, step)
        for axis in ("fsdp", "ctx")
        for step in (1, 2, 4, 8)
        if step < lax.axis_size(axis)
    ]
    front_total, front = front([small])
    for axis, step in steps[:-1]:
        small = small + swap(small, axis, step)
    qkv_grad, map_grad, out_grad = inner([front_total])
    gains_grad, bias_grad, kernel_grad = call(
        finish_small_body,
        [((5, part), F32), ((2, heads, size), F32), ((taps, channels), F32)],
        idx,
        small,
        swap(small, *steps[-1]),
        results=True,
    )
    front_expand, front_shrink = front()
    return (
        outputs,
        tokens_grad,
        front_expand,
        front_shrink,
        qkv_grad,
        map_grad,
        bias_grad,
        out_grad,
        gate_grad,
        kernel_grad,
        sums[0],
        sums[1],
        mix_grad,
        rear_expand,
        rear_shrink,
        gains_grad,
    )


def solution(mesh):
    frames = ("fsdp", "ctx")
    rows, columns = P(frames, "tp"), P("tp", frames)
    three_dims, last_only, one_dim = P(frames, None, "tp"), P(None, "tp"), P("tp")
    heads = P(None, "tp", None)
    return jax.shard_map(
        shards,
        mesh=mesh,
        in_specs=(
            rows,
            rows,
            columns,
            three_dims,
            rows,
            heads,
            columns,
            three_dims,
            last_only,
            one_dim,
            one_dim,
            columns,
            rows,
            columns,
            last_only,
            rows,
        ),
        out_specs=(
            rows,
            rows,
            rows,
            columns,
            three_dims,
            rows,
            heads,
            columns,
            three_dims,
            last_only,
            one_dim,
            one_dim,
            columns,
            rows,
            columns,
            last_only,
        ),
        check_vma=False,
    )
```

```python
import functools
import math

import jax
import jax.numpy as jnp
from jax import lax
from jax.experimental import pallas as pl
from jax.experimental.pallas import tpu as pltpu
from jax.sharding import PartitionSpec as P

F32 = jnp.float32
BF16 = jnp.bfloat16
EPSILON = 1e-05
HALO = 16
BLOCK = 128
VMEM_BYTES = 16 * 1024 * 1024
COST = 1


def call(body, outs, *args, after=(), scratch=(), results=False, vmem=VMEM_BYTES):
    first, extra = len(args), len(after)

    def kernel(*refs):
        body(*refs[:first], *refs[first + extra :])

    return pl.pallas_call(
        kernel,
        out_shape=[jax.ShapeDtypeStruct(*out) for out in outs],
        in_specs=[pl.BlockSpec(memory_space=pltpu.SMEM)]
        + [pl.BlockSpec(memory_space=pltpu.VMEM)] * (first - 1)
        + [pl.BlockSpec(memory_space=pl.ANY)] * extra,
        out_specs=[pl.BlockSpec() if results else pl.BlockSpec(memory_space=pltpu.VMEM)]
        * len(outs),
        scratch_shapes=list(scratch),
        compiler_params=pltpu.CompilerParams(vmem_limit_bytes=vmem),
        cost_estimate=pl.CostEstimate(flops=COST, bytes_accessed=COST, transcendentals=0),
    )(*args, *after)


def dot(left, right):
    return jnp.dot(left, right, preferred_element_type=F32)


def dot_cols(left, right):
    return lax.dot_general(left, right, (((1,), (1,)), ((), ())), preferred_element_type=F32)


def dot_rows(left, right):
    return lax.dot_general(left, right, (((0,), (0,)), ((), ())), preferred_element_type=F32)


def normalized(stream):
    centred = stream - jnp.mean(stream, axis=1, keepdims=True)
    spread = lax.rsqrt(jnp.mean(centred * centred, axis=1, keepdims=True) + EPSILON)
    return centred * spread, spread


def norm_pullback(grad, stream, gain):
    normal, spread = normalized(stream)
    scaled = grad * gain
    first = jnp.mean(scaled, axis=1, keepdims=True)
    second = jnp.mean(scaled * normal, axis=1, keepdims=True)
    return spread * (scaled - first - normal * second), jnp.sum(
        grad * normal, axis=0, keepdims=True
    )


def swish_slope(value, logistic):
    return logistic * (1.0 + value * (1.0 - logistic))


def halves(idx, rows):
    half = rows // 2
    mine = pl.multiple_of(idx[1] * half, half)
    theirs = pl.multiple_of((1 - idx[1]) * half, half)
    return pl.ds(mine, half), pl.ds(theirs, half)


def split(idx, whole, keep, send):
    mine, theirs = halves(idx, whole.shape[0])
    keep[...] = whole[mine, :].astype(BF16)
    send[...] = whole[theirs, :].astype(BF16)


def join(idx, t_mine, t_theirs, whole):
    mine, theirs = halves(idx, whole.shape[0])
    whole[mine, :] = t_mine[...].astype(F32)
    whole[theirs, :] = t_theirs[...].astype(F32)


def xor_pairs(count, step):
    return [(i, i ^ step) for i in range(count)]


def swap(value, axis, step):
    return lax.ppermute(value, axis, xor_pairs(lax.axis_size(axis), step))


def added(left, right):
    return (left.astype(F32) + right.astype(F32)).astype(BF16)


def joined_body(count, idx, *refs):
    outs = refs[2 * count :]
    rows, column = outs[0].shape[0], 0
    for left, right in zip(refs[:count], refs[count : 2 * count]):
        total = (left[...].astype(F32) + right[...].astype(F32)).astype(BF16)
        width = total.shape[1]
        for at, out in enumerate(outs):
            out[:, column : column + width] = total[at * rows : (at + 1) * rows, :]
        column += width


def added_after(idx, left, right, after):
    body = functools.partial(joined_body, 1)
    return call(body, [(left.shape, left.dtype)], idx, left, right, after=after)[0]


def tp_begin(keep, send, idx=None, after=()):
    other = swap(send, "tp", 1)
    return added_after(idx, keep, other, after) if after else added(keep, other)


def tp_end(idx, total, after=()):
    other = swap(total, "tp", 2)
    total = added_after(idx, total, other, after) if after else added(total, other)
    return total, swap(total, "tp", 1)


def tp_sum(keep, send):
    return tp_end(None, tp_begin(keep, send))


def place_body(ctx, rows, idx, *refs):
    out = refs[-1]
    blocks = []
    for ref in refs[:-1]:
        for at in range(ref.shape[0] // rows):
            blocks.append(ref[at * rows : (at + 1) * rows, :])
    for at, block in enumerate(blocks):
        half = idx[2] if at < ctx else 1 - idx[2]
        target = half * ctx + jnp.bitwise_xor(idx[3], at % ctx)
        out[pl.ds(pl.multiple_of(target * rows, rows), rows), :] = block


def pack_body(idx, tokens, cot, gains, out):
    rows = tokens.shape[0]
    out[:rows, :] = tokens[...]
    out[rows : 2 * rows, :] = cot[...]
    rest = gains[...]
    pieces = []
    for unused in range(3):
        piece = rest.astype(BF16).astype(F32)
        pieces.append(piece)
        rest = rest - piece
    pieces.append(jnp.zeros((1, rest.shape[1]), F32))
    out[2 * rows :, :] = jnp.concatenate(pieces, axis=0).astype(BF16)


def features_body(idx, *refs):
    blocks = refs[:4]
    x_out, cot_out, gains_out = refs[4:]
    rows, features = x_out.shape
    part = features // 4
    for at in range(4):
        target = jnp.bitwise_xor(idx[0], at)
        columns = pl.ds(pl.multiple_of(target * part, part), part)
        x_out[:, columns] = blocks[at][:rows, :]
        cot_out[:, columns] = blocks[at][rows : 2 * rows, :]
        pieces = blocks[at][2 * rows :, :].astype(F32)
        gains_out[:, columns] = (pieces[0:5] + pieces[5:10]) + pieces[10:15]


def finish_body(layout, parts, idx, *refs):
    total = refs[0][...].astype(F32)
    for ref in refs[1:parts]:
        total = total + ref[...].astype(F32)
    column = 0
    for (kind, width), out in zip(layout, refs[parts:]):
        if kind == "middle":
            count = out.shape[0]
            each = width // count
            for at in range(count):
                out[at] = total[:, column + at * each : column + (at + 1) * each]
        else:
            out[...] = total[:, column : column + width]
        column += width


def finish_small_body(idx, left, right, gains_out, bias_out, kernel_out):
    total = left[...] + right[...]
    gains_out[...] = total[:5]
    heads, size = bias_out.shape[1:]
    for head in range(heads):
        bias_out[:, head, :] = total[5:7, head * size : (head + 1) * size]
    kernel_out[...] = total[7 : 7 + kernel_out.shape[0]]


def wgrad_body(pairs, ctx, idx, *refs):
    outs, scratch = refs[2 * pairs : -1], refs[-1]
    column = 0
    for at in range(pairs):
        left, right = refs[2 * at], refs[2 * at + 1]
        width = right.shape[1]
        scratch[:, column : column + width] = dot_rows(left[...], right[...]).astype(BF16)
        column += width
    if not ctx:
        outs[0][...] = scratch[...]
        return
    rows = scratch.shape[0] // (2 * ctx)
    for half, out in zip((idx[2], 1 - idx[2]), outs):
        for at in range(ctx):
            source = half * ctx + jnp.bitwise_xor(idx[3], at)
            out[at * rows : (at + 1) * rows, :] = scratch[
                pl.ds(pl.multiple_of(source * rows, rows), rows), :
            ]


def feed_body(gain_at, base, joined, idx, *refs):
    if joined:
        x_ref, t1, t2, gains, weights, x_out, z_out, u_out, h_out, keep, send, work = refs
        join(idx, t1, t2, work)
        x = x_ref[...] + work[...]
        x_out[...] = x
    else:
        x_ref, gains, weights, z_out, u_out, h_out, keep, send, work = refs
        x = x_ref[...].astype(F32)
    hidden = u_out.shape[1]
    normal, unused = normalized(x)
    z = (normal * gains[gain_at : gain_at + 1, :]).astype(BF16)
    z_out[...] = z
    u = dot(z, weights[:, base : base + hidden])
    u_out[...] = u
    h = (u * jax.nn.sigmoid(u)).astype(BF16)
    h_out[...] = h
    work[...] = dot_cols(h, weights[:, base + hidden : base + 2 * hidden])
    split(idx, work, keep, send)


def attend_in_body(idx, x_ref, t1, t2, gains, weights, bias, x_out, z_out, qa, qb, kv, work):
    join(idx, t1, t2, work)
    x = x_ref[...].astype(F32) + 0.5 * work[...]
    x_out[...] = x
    normal, unused = normalized(x)
    z = (normal * gains[1:2, :]).astype(BF16)
    z_out[...] = z
    local = bias.shape[1]
    project = dot(z, weights[:, : 3 * local])
    query = project[:, :local]
    qa[...] = (query + bias[0:1, :]).astype(BF16)
    qb[...] = (query + bias[1:2, :]).astype(BF16)
    kv[...] = project[:, local:].astype(BF16)


def relative_body(base, idx, near_p, near_q, far_c, far_s, weights, embed, relative):
    step = far_c.shape[0]
    cos, sin = far_c[...], far_s[...]
    for at in range(embed.shape[0] // step):
        value = near_p[at : at + 1, :] * cos + near_q[at : at + 1, :] * sin
        embed[at * step : (at + 1) * step, :] = value.astype(BF16)
    relative[...] = dot(embed[...], weights[:, base : base + relative.shape[1]]).astype(BF16)


def position_body(heads, idx, qb, relative, out):
    rows, local = qb.shape
    size = local // heads
    length = out.shape[2]
    width = length + BLOCK
    for head in range(heads):
        columns = slice(head * size, (head + 1) * size)
        for at in range(rows // BLOCK):
            frames = slice(at * BLOCK, (at + 1) * BLOCK)
            first = rows - BLOCK * (at + 1)
            wide = dot_cols(qb[frames, columns], relative[first : first + width, columns])
            turned = pltpu.roll(wide, width - (BLOCK - 1), 1, stride=1, stride_axis=0)
            out[head, frames, :] = turned[:, :length]


def fill_pairs(idx, blocks, whole):
    rows = blocks[0].shape[0]
    for at, block in enumerate(blocks):
        target = jnp.bitwise_xor(idx[3], at)
        whole[pl.ds(pl.multiple_of(target * rows, rows), rows), :] = block[...]


def attend_body(heads, ctx, base, idx, qa, *refs):
    blocks = refs[:ctx]
    position, weights, p_out, mixed, keep, send, pairs, work = refs[ctx:]
    fill_pairs(idx, blocks, pairs)
    rows, local = qa.shape
    size = local // heads
    scale = size**-0.5
    for head in range(heads):
        columns = slice(head * size, (head + 1) * size)
        values = slice(local + head * size, local + (head + 1) * size)
        for at in range(rows // BLOCK):
            frames = slice(at * BLOCK, (at + 1) * BLOCK)
            scores = (dot_cols(qa[frames, columns], pairs[:, columns]) + position[head, frames, :]) * scale
            raised = jnp.exp(scores - jnp.max(scores, axis=1, keepdims=True))
            share = (raised / jnp.sum(raised, axis=1, keepdims=True)).astype(BF16)
            p_out[head, frames, :] = share
            mixed[frames, columns] = dot(share, pairs[:, values]).astype(BF16)
    work[...] = dot_cols(mixed[...], weights[:, base : base + local])
    split(idx, work, keep, send)


def conv_in_body(idx, x_ref, t1, t2, gains, weights, x_out, z_out, g_out, glu, first, last, work):
    join(idx, t1, t2, work)
    x = x_ref[...] + work[...]
    x_out[...] = x
    normal, unused = normalized(x)
    z = (normal * gains[2:3, :]).astype(BF16)
    z_out[...] = z
    rows, channels = glu.shape
    paired = dot(z, weights[:, : 2 * channels])
    g_out[...] = paired
    gated = (paired[:, :channels] * jax.nn.sigmoid(paired[:, channels:])).astype(BF16)
    glu[...] = gated
    first[...] = gated[:HALO, :]
    last[...] = gated[rows - HALO :, :]


def fill_padded(low, own, high, padded):
    rows = own.shape[0]
    padded[:HALO, :] = low[...].astype(F32)
    padded[HALO : HALO + rows, :] = own[...].astype(F32)
    padded[HALO + rows :, :] = high[...].astype(F32)


def conv_body(idx, glu, low, high, kernel, c_out, stats, padded):
    fill_padded(low, glu, high, padded)
    rows = glu.shape[0]
    taps = kernel.shape[0]
    shift = HALO - (taps - 1) // 2
    total = kernel[0:1, :] * padded[shift : shift + rows, :]
    for tap in range(1, taps):
        total = total + kernel[tap : tap + 1, :] * padded[shift + tap : shift + tap + rows, :]
    c_out[...] = total
    mean = jnp.mean(total, axis=0, keepdims=True)
    centred = total - mean
    stats[0:1, :] = mean
    stats[1:2, :] = jnp.sum(centred * centred, axis=0, keepdims=True)
    stats[2:, :] = jnp.zeros((stats.shape[0] - 2, stats.shape[1]), F32)


def batch_body(base, idx, c, stats, params, weights, q_out, act_out, keep, send, work):
    spread = stats[1:2, :]
    q = (c[...] - stats[0:1, :]) * spread
    q_out[...] = q
    a = q * params[0:1, :] + params[1:2, :]
    act = (a * jax.nn.sigmoid(a)).astype(BF16)
    act_out[...] = act
    work[...] = dot_cols(act, weights[:, base : base + act.shape[1]])
    split(idx, work, keep, send)


def feed_pullback(idx, grad, u, weights, base, f_out, du_out, keep, send, work):
    hidden = u.shape[1]
    f = (0.5 * grad).astype(BF16)
    f_out[...] = f
    value = u[...]
    logistic = jax.nn.sigmoid(value)
    back = dot(f, weights[:, base + hidden : base + 2 * hidden])
    du = (back * swish_slope(value, logistic)).astype(BF16)
    du_out[...] = du
    work[...] = dot_cols(du, weights[:, base : base + hidden])
    split(idx, work, keep, send)


def final_body(base, idx, x_ref, t1, t2, gains, cot, u, weights, y_out, d_out, gain_out, f_out, du_out, keep, send, work):
    join(idx, t1, t2, work)
    x = x_ref[...] + 0.5 * work[...]
    normal, unused = normalized(x)
    gain = gains[4:5, :]
    work[...] = normal * gain
    width = y_out.shape[1]
    y_out[...] = work[:, pl.ds(pl.multiple_of(idx[0] * width, width), width)].astype(BF16)
    grad, gain_grad = norm_pullback(cot[...].astype(F32), x, gain)
    gain_out[...] = gain_grad
    d_out[...] = grad
    feed_pullback(idx, grad, u, weights, base, f_out, du_out, keep, send, work)


def conv_back_body(base, idx, x_ref, d_ref, t1, t2, gains, q, params, weights, d_out, f_out, da_out, edges, gain_out, work):
    join(idx, t1, t2, work)
    grad, gain_grad = norm_pullback(work[...], x_ref[...], gains[3:4, :])
    gain_out[...] = gain_grad
    grad = d_ref[...] + grad
    d_out[...] = grad
    f = grad.astype(BF16)
    f_out[...] = f
    rows, channels = q.shape
    value = q[...]
    a = value * params[0:1, :] + params[1:2, :]
    da = dot(f, weights[:, base : base + channels]) * swish_slope(a, jax.nn.sigmoid(a))
    da_out[...] = da
    edges[0:1, :] = jnp.sum(da * value, axis=0, keepdims=True)
    edges[1:2, :] = jnp.sum(da, axis=0, keepdims=True)
    edges[2:8, :] = jnp.zeros((6, channels), F32)
    for at, part in enumerate((da[:HALO], value[:HALO], da[rows - HALO :], value[rows - HALO :])):
        edges[8 + at * HALO : 8 + (at + 1) * HALO, :] = part


def gate_back_body(ctx, counted, idx, da, q, sums, near, far, stats, params, kernel, paired, weights, dc_out, dg_out, keep, send, padded, work):
    rows, channels = q.shape
    odd = idx[3] % 2 == 1
    low = jnp.where(odd, near[8 + 2 * HALO :, :], far[8 + 2 * HALO :, :])
    high = jnp.where(odd, far[8 : 8 + 2 * HALO, :], near[8 : 8 + 2 * HALO, :])
    factor = stats[1:2, :] * params[0:1, :]
    mean_scale = sums[0:1, :] / counted
    mean_shift = sums[1:2, :] / counted

    def centred(grad, normal):
        return (factor * (grad - mean_shift - normal * mean_scale)).astype(BF16)

    dc = centred(da[...], q[...])
    dc_out[...] = dc
    before = (idx[3] > 0).astype(F32)
    after = (idx[3] < ctx - 1).astype(F32)
    padded[:HALO, :] = centred(low[:HALO, :], low[HALO:, :]).astype(F32) * before
    padded[HALO : HALO + rows, :] = dc.astype(F32)
    padded[HALO + rows :, :] = centred(high[:HALO, :], high[HALO:, :]).astype(F32) * after
    taps = kernel.shape[0]
    top = HALO + (taps - 1) // 2
    total = kernel[0:1, :] * padded[top : top + rows, :]
    for tap in range(1, taps):
        total = total + kernel[tap : tap + 1, :] * padded[top - tap : top - tap + rows, :]
    logistic = jax.nn.sigmoid(paired[:, channels:])
    through = total * logistic
    dg_out[:, :channels] = through.astype(BF16)
    dg_out[:, channels:] = (through * paired[:, :channels] * (1.0 - logistic)).astype(BF16)
    work[...] = dot_cols(dg_out[...], weights[:, : 2 * channels])
    split(idx, work, keep, send)


def taps_body(idx, glu, low, high, dc, out, padded):
    fill_padded(low, glu, high, padded)
    rows = glu.shape[0]
    grad = dc[...].astype(F32)
    shift = HALO - (out.shape[0] - 1) // 2
    for tap in range(out.shape[0]):
        out[tap : tap + 1, :] = jnp.sum(
            grad * padded[shift + tap : shift + tap + rows, :], axis=0, keepdims=True
        )


def attend_back_body(heads, ctx, base, idx, x_ref, d_ref, t1, t2, gains, weights, p, qa, *refs):
    blocks = refs[:ctx]
    d_out, f_out, gain_out, ds_out, dqa = refs[ctx : ctx + 5]
    out_blocks = refs[ctx + 5 : 2 * ctx + 5]
    pairs, grads, do, work = refs[2 * ctx + 5 :]
    fill_pairs(idx, blocks, pairs)
    join(idx, t1, t2, work)
    grad, gain_grad = norm_pullback(work[...], x_ref[...], gains[2:3, :])
    gain_out[...] = gain_grad
    grad = d_ref[...] + grad
    d_out[...] = grad
    f = grad.astype(BF16)
    f_out[...] = f
    rows, local = qa.shape
    size = local // heads
    scale = size**-0.5
    do[...] = dot(f, weights[:, base : base + local]).astype(BF16)
    for head in range(heads):
        columns = slice(head * size, (head + 1) * size)
        values = slice(local + head * size, local + (head + 1) * size)
        for at in range(rows // BLOCK):
            frames = slice(at * BLOCK, (at + 1) * BLOCK)
            dp = dot_cols(do[frames, columns], pairs[:, values])
            share = p[head, frames, :].astype(F32)
            balance = jnp.sum(share * dp, axis=1, keepdims=True)
            ds = (share * (dp - balance)).astype(BF16)
            ds_out[head, frames, :] = ds
            dqa[frames, columns] = dot(ds, pairs[:, columns]) * scale
        grads[:, columns] = (dot_rows(ds_out[head], qa[:, columns]) * scale).astype(BF16)
        grads[:, values] = dot_rows(p[head], do[:, columns]).astype(BF16)
    for at, block in enumerate(out_blocks):
        source = jnp.bitwise_xor(idx[3], at)
        block[...] = grads[pl.ds(pl.multiple_of(source * rows, rows), rows), :]


def position_back_body(heads, idx, ds, qb, relative, dqb, dr_out, wide, total):
    rows, local = qb.shape
    size = local // heads
    length = ds.shape[2]
    width = length + BLOCK
    scale = size**-0.5
    down = lax.broadcasted_iota(jnp.int32, (BLOCK, BLOCK), 0)
    across = lax.broadcasted_iota(jnp.int32, (BLOCK, BLOCK), 1)
    flip = (down + across == BLOCK - 1).astype(BF16)
    total[...] = jnp.zeros(total.shape, F32)
    wide[:, length:] = jnp.zeros((BLOCK, BLOCK), F32)
    for head in range(heads):
        columns = slice(head * size, (head + 1) * size)
        for at in range(rows // BLOCK):
            frames = slice(at * BLOCK, (at + 1) * BLOCK)
            first = rows - BLOCK * (at + 1)
            wide[:, :length] = dot(flip, ds[head, frames, :])
            turned = pltpu.roll(wide[...], 0, 1, stride=1, stride_axis=0).astype(BF16)
            turned_b = dot(turned, relative[first : first + width, columns]) * scale
            dqb[frames, columns] = jnp.dot(
                flip.astype(F32), turned_b, precision=lax.Precision.HIGHEST, preferred_element_type=F32
            )
            flipped = dot(flip, qb[frames, columns]).astype(BF16)
            total[first : first + width, columns] += dot_rows(turned, flipped)
    dr_out[...] = (total[...] * scale).astype(BF16)


def attend_out_body(ctx, idx, dqa, dqb, *refs):
    blocks = refs[:ctx]
    weights, dp_out, bias_out, keep, send, work = refs[ctx:]
    local = dqa.shape[1]
    bias_out[0:1, :] = jnp.sum(dqa[...], axis=0, keepdims=True)
    bias_out[1:2, :] = jnp.sum(dqb[...], axis=0, keepdims=True)
    dp_out[:, :local] = (dqa[...] + dqb[...]).astype(BF16)
    total = blocks[0][...].astype(F32)
    for block in blocks[1:]:
        total = total + block[...].astype(F32)
    dp_out[:, local:] = total.astype(BF16)
    work[...] = dot_cols(dp_out[...], weights[:, : 3 * local])
    split(idx, work, keep, send)


def feed_back_body(idx, x_ref, d_ref, t1, t2, gains, u, weights, d_out, f_out, du_out, gain_out, keep, send, work):
    join(idx, t1, t2, work)
    grad, gain_grad = norm_pullback(work[...], x_ref[...], gains[1:2, :])
    gain_out[...] = gain_grad
    grad = d_ref[...] + grad
    d_out[...] = grad
    feed_pullback(idx, grad, u, weights, 0, f_out, du_out, keep, send, work)


def last_body(idx, x_ref, d_ref, t1, t2, gains, two, three, four, five, bias, kernel, out, small, work, each):
    join(idx, t1, t2, work)
    grad, gain_grad = norm_pullback(work[...], x_ref[...].astype(F32), gains[0:1, :])
    for at, row in enumerate((gain_grad, two[...], three[...], four[...], five[...])):
        each[at : at + 1, :] = row
    part = out.shape[1]
    own = pl.ds(pl.multiple_of(idx[0] * part, part), part)
    taps = kernel.shape[0]
    small[:5, :] = each[:5, own]
    small[5:7, :] = bias[...]
    small[7 : 7 + taps, :] = kernel[...]
    small[7 + taps :, :] = jnp.zeros((small.shape[0] - 7 - taps, part), F32)
    work[...] = d_ref[...] + grad
    width = out.shape[1]
    out[...] = work[:, pl.ds(pl.multiple_of(idx[0] * width, width), width)]


FRAMES = ("fsdp", "ctx")


def paired_mesh():
    return lax.axis_size("fsdp") == 2


def gathered(idx, shard, after=(), stepwise=False):
    if not paired_mesh():
        whole = lax.all_gather(shard, FRAMES, axis=0, tiled=True)
        return whole, shard
    ctx = lax.axis_size("ctx")
    rows, width = shard.shape
    if after:
        shard = held(idx, shard, after)
    if not stepwise:
        mine = [shard] + [swap(shard, "ctx", step) for step in range(1, ctx)]
        mark = jnp.concatenate(mine, axis=0)
    else:
        near = jnp.concatenate([shard, swap(shard, "ctx", 1)], axis=0)
        mark = jnp.concatenate([near, swap(near, "ctx", 2)], axis=0)

    def ended(after=()):
        block = held(idx, mark, after) if after else mark
        outs = [((2 * ctx * rows, width), BF16)]
        body = functools.partial(place_body, ctx, rows)
        return call(body, outs, idx, block, swap(block, "fsdp", 1))[0]

    return (ended if stepwise else ended()), mark


def features_whole(value):
    near, far = swap(value, "tp", 1), swap(value, "tp", 2)
    return [value, near, far, swap(far, "tp", 1)]


def products(idx, pairs):
    depth = pairs[0][0].shape[1]
    width = sum(right.shape[1] for unused, right in pairs)
    flat = [array for pair in pairs for array in pair]
    ctx = lax.axis_size("ctx") if paired_mesh() else 0
    outs = [((depth // 2, width), BF16)] * 2 if ctx else [((depth, width), BF16)]
    body = functools.partial(wgrad_body, len(pairs), ctx)
    return call(body, outs, idx, *flat, scratch=[pltpu.VMEM((depth, width), BF16)])


def across(idx, made, after=()):
    if not paired_mesh():
        return made[0]
    return swap(held(idx, made[1], after) if after else made[1], "fsdp", 1)


def along(idx, made, others, after=()):
    if not paired_mesh():
        grads = jnp.concatenate([part[0] for part in made], axis=1)
        return grads, [lax.psum_scatter(grads, FRAMES, scatter_dimension=0, tiled=True)]
    ctx = lax.axis_size("ctx")
    rows = made[0][0].shape[0] // ctx
    width = sum(part[0].shape[1] for part in made)
    body = functools.partial(joined_body, len(made))
    mine = [part[0] for part in made]
    blocks = call(body, [((rows, width), BF16)] * ctx, idx, *mine, *others, after=after)
    return blocks[0], [blocks[0]] + [swap(blocks[at], "ctx", at) for at in range(1, ctx)]


def finish(idx, parts, layout, after=()):
    rows, values, column = parts[0].shape[0], [], 0
    if paired_mesh():
        shapes = [
            ((count, rows, width // count) if kind == "middle" else (rows, width), F32)
            for kind, count, width in layout
        ]
        kinds = [(kind, width) for kind, unused, width in layout]
        body = functools.partial(finish_body, kinds, len(parts))
        values = call(body, shapes, idx, *parts, after=after, results=True)
    else:
        total = parts[0].astype(F32)
        for kind, count, width in layout:
            value = total[:, column : column + width]
            if kind == "middle":
                value = value.reshape(rows, count, width // count).swapaxes(0, 1)
            values.append(value)
            column += width
    turns = {"rows": lambda v: v, "turned": lambda v: v.T, "middle": lambda v: v.swapaxes(0, 1)}
    return [turns[kind](value) for (kind, unused, unused), value in zip(layout, values)]


def hold_body(idx, value, out):
    out[...] = value[...]


def held(idx, value, after):
    return call(hold_body, [(value.shape, value.dtype)], idx, value, after=after)[0]


def over_frames(value, merge):
    near, far, across = (swap(value, "ctx", step) for step in (1, 2, 3))
    value = merge(merge(value, near), merge(far, across))
    step = 1
    while step < lax.axis_size("fsdp"):
        value = merge(value, swap(value, "fsdp", step))
        step *= 2
    return value


def pooled(stats, rows):
    stats = jnp.concatenate([stats[:2], jnp.full_like(stats[:1], rows), stats[3:]], axis=0)

    def merge(left, right):
        gap = left[0:1] - right[0:1]
        mean = 0.5 * (left[0:1] + right[0:1])
        squares = left[1:2] + right[1:2] + gap * gap * (0.5 * left[2:3])
        return jnp.concatenate([mean, squares, 2.0 * left[2:3], left[3:]], axis=0)

    stats = over_frames(stats, merge)
    spread = lax.rsqrt(stats[1:2] / stats[2:3] + EPSILON)
    return jnp.concatenate([stats[0:1], spread, stats[2:]], axis=0)


def edges_summed(edges):
    near, far = swap(edges, "ctx", 1), swap(edges, "ctx", 3)
    sums = (edges[:8] + near[:8]) + (swap(edges[:8], "ctx", 2) + far[:8])
    step = 1
    while step < lax.axis_size("fsdp"):
        sums = sums + swap(sums, "fsdp", step)
        step *= 2
    return sums, near, far


def neighbours(first, last):
    count = lax.axis_size("ctx")
    up = [(i, i + 1) for i in range(count - 1)]
    down = [(i + 1, i) for i in range(count - 1)]
    return lax.ppermute(last, "ctx", up), lax.ppermute(first, "ctx", down)


def angle_tables(start, rows, width, features):
    step = 64
    column = jnp.arange(features, dtype=jnp.int32)
    rates = jnp.exp((column // 2).astype(F32) * (-2.0 * math.log(10000.0) / features))
    even = (column % 2 == 0)[None, :]
    near = (start + rows - 1 - step * jnp.arange(width // step, dtype=jnp.int32)).astype(F32)
    near = near[:, None] * rates[None, :]
    far = jnp.arange(step, dtype=jnp.int32).astype(F32)[:, None] * rates[None, :]
    sine, cosine = jnp.sin(near), jnp.cos(near)
    return (
        jnp.where(even, sine, cosine),
        jnp.where(even, -cosine, sine),
        jnp.cos(far),
        jnp.sin(far),
    )


def shards(
    tokens,
    first_expand,
    first_shrink,
    attend_input,
    position_map,
    position_bias,
    attend_output,
    gating_map,
    depth_kernel,
    batch_scale,
    batch_shift,
    mixing_map,
    second_expand,
    second_shrink,
    layer_gains,
    cotangent,
):
    rows, part = tokens.shape
    tp, ctx = lax.axis_size("tp"), lax.axis_size("ctx")
    features = part * tp
    shard = first_expand.shape[0]
    hidden = first_expand.shape[1]
    heads, size = position_bias.shape[1:]
    local = heads * size
    channels = depth_kernel.shape[1]
    length = rows * ctx
    width = length + rows
    tp_at = lax.axis_index("tp")
    ctx_at = lax.axis_index("ctx")
    idx = jnp.stack(
        [tp_at, tp_at % 2, lax.axis_index("fsdp"), ctx_at]
    ).astype(jnp.int32)

    packed_frames = call(
        pack_body, [((2 * rows + 16, part), BF16)], idx, tokens, cotangent, layer_gains
    )[0]
    blocks_whole = features_whole(packed_frames)
    one, one_mark = gathered(idx, jnp.concatenate([first_expand, first_shrink.T], axis=1))
    x0, cot, gains = call(
        features_body,
        [((rows, features), BF16), ((rows, features), BF16), ((5, features), F32)],
        idx,
        *blocks_whole,
    )
    bias = position_bias.reshape(2, local)
    params = jnp.stack([batch_scale, batch_shift])
    tables = angle_tables(ctx_at * rows, rows, width, features)
    thirds = [attend_input[:, at] for at in range(3)]
    two, two_mark = gathered(
        idx,
        jnp.concatenate(thirds + [position_map, attend_output.T], axis=1),
        [one_mark, blocks_whole[1], blocks_whole[2]],
    )
    halves_in = [gating_map[:, at] for at in range(2)]
    three, three_mark = gathered(
        idx,
        jnp.concatenate(halves_in + [mixing_map.T, second_expand, second_shrink.T], axis=1),
        [one_mark],
        stepwise=True,
    )
    at_pos, at_out = 3 * local, 4 * local
    at_mix, at_two = 2 * channels, 3 * channels

    stream = ((rows, features), F32)
    packed = ((rows, features), BF16)
    piece = ((rows // 2, features), BF16)
    gain_row = ((1, features), F32)
    work = pltpu.VMEM((rows, features), F32)
    inner_shape = (rows, hidden)

    z1, u1, h1, keep, send = call(
        functools.partial(feed_body, 0, 0, False),
        [packed, (inner_shape, F32), (inner_shape, BF16), piece, piece],
        idx,
        x0,
        gains,
        one,
        scratch=[work],
    )
    t1, t2 = tp_end(idx, tp_begin(keep, send, idx, [two_mark]), [two])
    embed, relative = call(
        functools.partial(relative_body, at_pos),
        [((width, features), BF16), ((width, local), BF16)],
        idx,
        *tables,
        two,
    )
    per_head = ((rows, local), BF16)
    x1, z2, qa, qb, kv = call(
        attend_in_body,
        [stream, packed, per_head, per_head, ((rows, 2 * local), BF16)],
        idx,
        x0,
        t1,
        t2,
        gains,
        two,
        bias,
        after=[three_mark],
        scratch=[work],
    )
    if callable(three):
        three = three([kv])
    pairs = [kv] + [swap(kv, "ctx", step) for step in range(1, ctx)]
    position = call(
        functools.partial(position_body, heads),
        [((heads, rows, length), F32)],
        idx,
        qb,
        relative,
    )[0]
    whole_pairs = pltpu.VMEM((length, 2 * local), BF16)
    p, mixed, keep, send = call(
        functools.partial(attend_body, heads, ctx, at_out),
        [((heads, rows, length), BF16), per_head, piece, piece],
        idx,
        qa,
        *pairs,
        position,
        two,
        scratch=[whole_pairs, work],
    )
    t1, t2 = tp_end(idx, tp_begin(keep, send, idx, [three]))
    edge = ((HALO, channels), BF16)
    x2, z3, paired, glu, first, last = call(
        conv_in_body,
        [
            stream,
            packed,
            ((rows, 2 * channels), F32),
            ((rows, channels), BF16),
            edge,
            edge,
        ],
        idx,
        x1,
        t1,
        t2,
        gains,
        three,
        scratch=[work],
    )
    low, high = neighbours(first, last)
    padded = pltpu.VMEM((rows + 2 * HALO, channels), F32)
    c, stats = call(
        conv_body,
        [((rows, channels), F32), ((8, channels), F32)],
        idx,
        glu,
        low,
        high,
        depth_kernel,
        scratch=[padded],
    )
    stats = pooled(stats, rows)
    q, act, keep, send = call(
        functools.partial(batch_body, at_mix),
        [((rows, channels), F32), ((rows, channels), BF16), piece, piece],
        idx,
        c,
        stats,
        params,
        three,
        scratch=[work],
    )
    t1, t2 = tp_sum(keep, send)
    x3, z4, u2, h2, keep, send = call(
        functools.partial(feed_body, 3, at_two, True),
        [stream, packed, (inner_shape, F32), (inner_shape, BF16), piece, piece],
        idx,
        x2,
        t1,
        t2,
        gains,
        three,
        scratch=[work],
    )
    t1, t2 = tp_sum(keep, send)
    outputs, d4, gain_five, f4, du2, keep, send = call(
        functools.partial(final_body, at_two),
        [
            ((rows, part), BF16),
            stream,
            gain_row,
            packed,
            (inner_shape, BF16),
            piece,
            piece,
        ],
        idx,
        x3,
        t1,
        t2,
        gains,
        cot,
        u2,
        three,
        scratch=[work],
    )
    total = tp_begin(keep, send)
    rear = products(idx, [(z4, du2), (f4, h2)])
    t1, t2 = tp_end(idx, total, [rear[0]])
    d3, f3, da, edges, gain_four = call(
        functools.partial(conv_back_body, at_mix),
        [
            stream,
            packed,
            ((rows, channels), F32),
            ((8 + 4 * HALO, channels), F32),
            gain_row,
        ],
        idx,
        x3,
        d4,
        t1,
        t2,
        gains,
        q,
        params,
        three,
        scratch=[work],
    )
    sums, near, far = edges_summed(edges)
    rear_other = across(idx, rear)
    counted = rows * lax.axis_size(FRAMES)
    dc, dg, keep, send = call(
        functools.partial(gate_back_body, ctx, counted),
        [
            ((rows, channels), BF16),
            ((rows, 2 * channels), BF16),
            piece,
            piece,
        ],
        idx,
        da,
        q,
        sums,
        near,
        far,
        stats,
        params,
        depth_kernel,
        paired,
        three,
        after=[rear_other],
        scratch=[padded, work],
    )
    total = tp_begin(keep, send)
    kernel_grad = call(
        taps_body,
        [(depth_kernel.shape, F32)],
        idx,
        glu,
        low,
        high,
        dc,
        scratch=[padded],
    )[0]
    middle = products(idx, [(z3, dg), (f3, act)])
    rear_total, rear_parts = along(idx, [rear], [rear_other], [total])
    t1, t2 = tp_end(idx, total, [middle[0], kernel_grad, rear_total])
    pair_block = ((rows, 2 * local), BF16)
    results = call(
        functools.partial(attend_back_body, heads, ctx, at_out),
        [stream, packed, gain_row, ((heads, rows, length), BF16), ((rows, local), F32)]
        + [pair_block] * ctx,
        idx,
        x2,
        d3,
        t1,
        t2,
        gains,
        two,
        p,
        qa,
        *pairs,
        scratch=[whole_pairs, whole_pairs, pltpu.VMEM((rows, local), BF16), work],
    )
    d2, f2, gain_three, ds, dqa = results[:5]
    pair_grads = [results[5]] + [
        swap(block, "ctx", step + 1) for step, block in enumerate(results[6:])
    ]
    dqb, dr = call(
        functools.partial(position_back_body, heads),
        [((rows, local), F32), ((width, local), BF16)],
        idx,
        ds,
        qb,
        relative,
        scratch=[pltpu.VMEM((BLOCK, length + BLOCK), F32), pltpu.VMEM((width, local), F32)],
    )
    middle_other = across(idx, middle, [ds])
    rear_expand, rear_shrink = finish(
        idx, rear_parts, [("rows", 1, hidden), ("turned", 1, hidden)], [dr]
    )
    dp, bias_grad, keep, send = call(
        functools.partial(attend_out_body, ctx),
        [((rows, 3 * local), BF16), ((2, local), F32), piece, piece],
        idx,
        dqa,
        dqb,
        *pair_grads,
        two,
        after=[rear_expand, middle_other],
        scratch=[work],
    )
    total = tp_begin(keep, send)
    inner = products(idx, [(z2, dp), (embed, dr), (f2, mixed)])
    t1, t2 = tp_end(idx, total, [inner[0]])
    inner_other = across(idx, inner)
    d1, f1, du1, gain_two, keep, send = call(
        feed_back_body,
        [stream, ((rows, features), BF16), (inner_shape, BF16), gain_row, piece, piece],
        idx,
        x1,
        d2,
        t1,
        t2,
        gains,
        u1,
        one,
        scratch=[work],
    )
    front = products(idx, [(z1, du1), (f1, h1)])
    total = tp_begin(keep, send, idx, [front[0]])
    front_other = across(idx, front)
    inner_total, inner_parts = along(idx, [inner, middle], [inner_other, middle_other], [total])
    t1, t2 = tp_end(idx, total, [inner_total])
    taps = depth_kernel.shape[0]
    tokens_grad, small = call(
        last_body,
        [((rows, part), F32), ((-(-(7 + taps) // 8) * 8, part), F32)],
        idx,
        x0,
        d1,
        t1,
        t2,
        gains,
        gain_two,
        gain_three,
        gain_four,
        gain_five,
        bias_grad,
        kernel_grad,
        scratch=[work, pltpu.VMEM((8, features), F32)],
    )
    steps = [
        (axis, step)
        for axis in ("fsdp", "ctx")
        for step in (1, 2, 4, 8)
        if step < lax.axis_size(axis)
    ]
    small = small + swap(small, *steps[0])
    front_total, front_parts = along(idx, [front], [front_other], [small])
    for axis, step in steps[1:-1]:
        small = small + swap(small, axis, step)
    qkv_grad, map_grad, out_grad, gate_grad, mix_grad = finish(
        idx,
        inner_parts,
        [
            ("middle", 3, 3 * local),
            ("rows", 1, local),
            ("turned", 1, local),
            ("middle", 2, 2 * channels),
            ("turned", 1, channels),
        ],
        [front_total],
    )
    gains_grad, bias_grad, kernel_grad = call(
        finish_small_body,
        [((5, part), F32), ((2, heads, size), F32), ((taps, channels), F32)],
        idx,
        small,
        swap(small, *steps[-1]),
        results=True,
    )
    front_expand, front_shrink = finish(
        idx, front_parts, [("rows", 1, hidden), ("turned", 1, hidden)]
    )
    return (
        outputs,
        tokens_grad,
        front_expand,
        front_shrink,
        qkv_grad,
        map_grad,
        bias_grad,
        out_grad,
        gate_grad,
        kernel_grad,
        sums[0],
        sums[1],
        mix_grad,
        rear_expand,
        rear_shrink,
        gains_grad,
    )


def solution(mesh):
    frames = ("fsdp", "ctx")
    rows, columns = P(frames, "tp"), P("tp", frames)
    three_dims, last_only, one_dim = P(frames, None, "tp"), P(None, "tp"), P("tp")
    heads = P(None, "tp", None)
    return jax.shard_map(
        shards,
        mesh=mesh,
        in_specs=(
            rows,
            rows,
            columns,
            three_dims,
            rows,
            heads,
            columns,
            three_dims,
            last_only,
            one_dim,
            one_dim,
            columns,
            rows,
            columns,
            last_only,
            rows,
        ),
        out_specs=(
            rows,
            rows,
            rows,
            columns,
            three_dims,
            rows,
            heads,
            columns,
            three_dims,
            last_only,
            one_dim,
            one_dim,
            columns,
            rows,
            columns,
            last_only,
        ),
        check_vma=False,
    )
```

```python
import functools
import math

import jax
import jax.numpy as jnp
from jax import lax
from jax.experimental import pallas as pl
from jax.experimental.pallas import tpu as pltpu
from jax.sharding import PartitionSpec as P

F32 = jnp.float32
BF16 = jnp.bfloat16
EPSILON = 1e-05
HALO = 16
BLOCK = 128
VMEM_BYTES = 16 * 1024 * 1024
COST = 1


def call(body, outs, *args, after=(), scratch=(), results=False, vmem=VMEM_BYTES):
    first, extra = len(args), len(after)

    def kernel(*refs):
        body(*refs[:first], *refs[first + extra :])

    return pl.pallas_call(
        kernel,
        out_shape=[jax.ShapeDtypeStruct(*out) for out in outs],
        in_specs=[pl.BlockSpec(memory_space=pltpu.SMEM)]
        + [pl.BlockSpec(memory_space=pltpu.VMEM)] * (first - 1)
        + [pl.BlockSpec(memory_space=pl.ANY)] * extra,
        out_specs=[pl.BlockSpec() if results else pl.BlockSpec(memory_space=pltpu.VMEM)]
        * len(outs),
        scratch_shapes=list(scratch),
        compiler_params=pltpu.CompilerParams(vmem_limit_bytes=vmem),
        cost_estimate=pl.CostEstimate(flops=COST, bytes_accessed=COST, transcendentals=0),
    )(*args, *after)


def dot(left, right):
    return jnp.dot(left, right, preferred_element_type=F32)


def dot_cols(left, right):
    return lax.dot_general(left, right, (((1,), (1,)), ((), ())), preferred_element_type=F32)


def dot_rows(left, right):
    return lax.dot_general(left, right, (((0,), (0,)), ((), ())), preferred_element_type=F32)


def normalized(stream):
    centred = stream - jnp.mean(stream, axis=1, keepdims=True)
    spread = lax.rsqrt(jnp.mean(centred * centred, axis=1, keepdims=True) + EPSILON)
    return centred * spread, spread


def norm_pullback(grad, stream, gain):
    normal, spread = normalized(stream)
    scaled = grad * gain
    first = jnp.mean(scaled, axis=1, keepdims=True)
    second = jnp.mean(scaled * normal, axis=1, keepdims=True)
    return spread * (scaled - first - normal * second), jnp.sum(
        grad * normal, axis=0, keepdims=True
    )


def swish_slope(value, logistic):
    return logistic * (1.0 + value * (1.0 - logistic))


def halves(idx, rows):
    half = rows // 2
    mine = pl.multiple_of(idx[1] * half, half)
    theirs = pl.multiple_of((1 - idx[1]) * half, half)
    return pl.ds(mine, half), pl.ds(theirs, half)


def split(idx, whole, keep, send):
    mine, theirs = halves(idx, whole.shape[0])
    keep[...] = whole[mine, :].astype(BF16)
    send[...] = whole[theirs, :].astype(BF16)


def join(idx, t_mine, t_theirs, whole):
    mine, theirs = halves(idx, whole.shape[0])
    whole[mine, :] = t_mine[...].astype(F32)
    whole[theirs, :] = t_theirs[...].astype(F32)


def xor_pairs(count, step):
    return [(i, i ^ step) for i in range(count)]


def swap(value, axis, step):
    return lax.ppermute(value, axis, xor_pairs(lax.axis_size(axis), step))


def added(left, right):
    return (left.astype(F32) + right.astype(F32)).astype(BF16)


def joined_body(count, idx, *refs):
    outs = refs[2 * count :]
    rows, column = outs[0].shape[0], 0
    for left, right in zip(refs[:count], refs[count : 2 * count]):
        total = (left[...].astype(F32) + right[...].astype(F32)).astype(BF16)
        width = total.shape[1]
        for at, out in enumerate(outs):
            out[:, column : column + width] = total[at * rows : (at + 1) * rows, :]
        column += width


def added_after(idx, left, right, after):
    body = functools.partial(joined_body, 1)
    return call(body, [(left.shape, left.dtype)], idx, left, right, after=after)[0]


def tp_begin(keep, send, idx=None, after=()):
    other = swap(send, "tp", 1)
    return added_after(idx, keep, other, after) if after else added(keep, other)


def tp_end(idx, total, after=()):
    other = swap(total, "tp", 2)
    total = added_after(idx, total, other, after) if after else added(total, other)
    return total, swap(total, "tp", 1)


def tp_sum(keep, send):
    return tp_end(None, tp_begin(keep, send))


def place_body(ctx, rows, idx, *refs):
    out = refs[-1]
    blocks = []
    for ref in refs[:-1]:
        for at in range(ref.shape[0] // rows):
            blocks.append(ref[at * rows : (at + 1) * rows, :])
    for at, block in enumerate(blocks):
        half = idx[2] if at < ctx else 1 - idx[2]
        target = half * ctx + jnp.bitwise_xor(idx[3], at % ctx)
        out[pl.ds(pl.multiple_of(target * rows, rows), rows), :] = block


def pack_body(idx, tokens, cot, gains, out):
    rows = tokens.shape[0]
    out[:rows, :] = tokens[...]
    out[rows : 2 * rows, :] = cot[...]
    rest = gains[...]
    pieces = []
    for unused in range(3):
        piece = rest.astype(BF16).astype(F32)
        pieces.append(piece)
        rest = rest - piece
    pieces.append(jnp.zeros((1, rest.shape[1]), F32))
    out[2 * rows :, :] = jnp.concatenate(pieces, axis=0).astype(BF16)


def features_body(idx, *refs):
    blocks = refs[:4]
    x_out, cot_out, gains_out = refs[4:]
    rows, features = x_out.shape
    part = features // 4
    for at in range(4):
        target = jnp.bitwise_xor(idx[0], at)
        columns = pl.ds(pl.multiple_of(target * part, part), part)
        x_out[:, columns] = blocks[at][:rows, :]
        cot_out[:, columns] = blocks[at][rows : 2 * rows, :]
        pieces = blocks[at][2 * rows :, :].astype(F32)
        gains_out[:, columns] = (pieces[0:5] + pieces[5:10]) + pieces[10:15]


def finish_body(layout, parts, idx, *refs):
    total = refs[0][...].astype(F32)
    for ref in refs[1:parts]:
        total = total + ref[...].astype(F32)
    column = 0
    for (kind, width), out in zip(layout, refs[parts:]):
        if kind == "middle":
            count = out.shape[0]
            each = width // count
            for at in range(count):
                out[at] = total[:, column + at * each : column + (at + 1) * each]
        else:
            out[...] = total[:, column : column + width]
        column += width


def finish_small_body(idx, left, right, gains_out, bias_out, kernel_out):
    total = left[...] + right[...]
    gains_out[...] = total[:5]
    heads, size = bias_out.shape[1:]
    for head in range(heads):
        bias_out[:, head, :] = total[5:7, head * size : (head + 1) * size]
    kernel_out[...] = total[7 : 7 + kernel_out.shape[0]]


def wgrad_body(pairs, ctx, idx, *refs):
    outs, scratch = refs[2 * pairs : -1], refs[-1]
    column = 0
    for at in range(pairs):
        left, right = refs[2 * at], refs[2 * at + 1]
        width = right.shape[1]
        scratch[:, column : column + width] = dot_rows(left[...], right[...]).astype(BF16)
        column += width
    if not ctx:
        outs[0][...] = scratch[...]
        return
    rows = scratch.shape[0] // (2 * ctx)
    for half, out in zip((idx[2], 1 - idx[2]), outs):
        for at in range(ctx):
            source = half * ctx + jnp.bitwise_xor(idx[3], at)
            out[at * rows : (at + 1) * rows, :] = scratch[
                pl.ds(pl.multiple_of(source * rows, rows), rows), :
            ]


def feed_body(gain_at, base, joined, idx, *refs):
    if joined:
        x_ref, t1, t2, gains, weights, x_out, z_out, u_out, h_out, keep, send, work = refs
        join(idx, t1, t2, work)
        x = x_ref[...] + work[...]
        x_out[...] = x
    else:
        x_ref, gains, weights, z_out, u_out, h_out, keep, send, work = refs
        x = x_ref[...].astype(F32)
    hidden = u_out.shape[1]
    normal, unused = normalized(x)
    z = (normal * gains[gain_at : gain_at + 1, :]).astype(BF16)
    z_out[...] = z
    u = dot(z, weights[:, base : base + hidden])
    u_out[...] = u
    h = (u * jax.nn.sigmoid(u)).astype(BF16)
    h_out[...] = h
    work[...] = dot_cols(h, weights[:, base + hidden : base + 2 * hidden])
    split(idx, work, keep, send)


def attend_in_body(idx, x_ref, t1, t2, gains, weights, bias, x_out, z_out, qa, qb, kv, work):
    join(idx, t1, t2, work)
    x = x_ref[...].astype(F32) + 0.5 * work[...]
    x_out[...] = x
    normal, unused = normalized(x)
    z = (normal * gains[1:2, :]).astype(BF16)
    z_out[...] = z
    local = bias.shape[1]
    project = dot(z, weights[:, : 3 * local])
    query = project[:, :local]
    qa[...] = (query + bias[0:1, :]).astype(BF16)
    qb[...] = (query + bias[1:2, :]).astype(BF16)
    kv[...] = project[:, local:].astype(BF16)


def relative_body(base, idx, near_p, near_q, far_c, far_s, weights, embed, relative):
    step = far_c.shape[0]
    cos, sin = far_c[...], far_s[...]
    for at in range(embed.shape[0] // step):
        value = near_p[at : at + 1, :] * cos + near_q[at : at + 1, :] * sin
        embed[at * step : (at + 1) * step, :] = value.astype(BF16)
    relative[...] = dot(embed[...], weights[:, base : base + relative.shape[1]]).astype(BF16)


def position_body(heads, idx, qb, relative, out):
    rows, local = qb.shape
    size = local // heads
    length = out.shape[2]
    width = length + BLOCK
    for head in range(heads):
        columns = slice(head * size, (head + 1) * size)
        for at in range(rows // BLOCK):
            frames = slice(at * BLOCK, (at + 1) * BLOCK)
            first = rows - BLOCK * (at + 1)
            wide = dot_cols(qb[frames, columns], relative[first : first + width, columns])
            turned = pltpu.roll(wide, width - (BLOCK - 1), 1, stride=1, stride_axis=0)
            out[head, frames, :] = turned[:, :length]


def fill_pairs(idx, blocks, whole):
    rows = blocks[0].shape[0]
    for at, block in enumerate(blocks):
        target = jnp.bitwise_xor(idx[3], at)
        whole[pl.ds(pl.multiple_of(target * rows, rows), rows), :] = block[...]


def attend_body(heads, ctx, base, idx, qa, *refs):
    blocks = refs[:ctx]
    position, weights, p_out, mixed, keep, send, pairs, work = refs[ctx:]
    fill_pairs(idx, blocks, pairs)
    rows, local = qa.shape
    size = local // heads
    scale = size**-0.5
    for head in range(heads):
        columns = slice(head * size, (head + 1) * size)
        values = slice(local + head * size, local + (head + 1) * size)
        for at in range(rows // BLOCK):
            frames = slice(at * BLOCK, (at + 1) * BLOCK)
            scores = (dot_cols(qa[frames, columns], pairs[:, columns]) + position[head, frames, :]) * scale
            raised = jnp.exp(scores - jnp.max(scores, axis=1, keepdims=True))
            share = (raised / jnp.sum(raised, axis=1, keepdims=True)).astype(BF16)
            p_out[head, frames, :] = share
            mixed[frames, columns] = dot(share, pairs[:, values]).astype(BF16)
    work[...] = dot_cols(mixed[...], weights[:, base : base + local])
    split(idx, work, keep, send)


def conv_in_body(idx, x_ref, t1, t2, gains, weights, x_out, z_out, g_out, glu, first, last, work):
    join(idx, t1, t2, work)
    x = x_ref[...] + work[...]
    x_out[...] = x
    normal, unused = normalized(x)
    z = (normal * gains[2:3, :]).astype(BF16)
    z_out[...] = z
    rows, channels = glu.shape
    paired = dot(z, weights[:, : 2 * channels])
    g_out[...] = paired
    gated = (paired[:, :channels] * jax.nn.sigmoid(paired[:, channels:])).astype(BF16)
    glu[...] = gated
    first[...] = gated[:HALO, :]
    last[...] = gated[rows - HALO :, :]


def fill_padded(low, own, high, padded):
    rows = own.shape[0]
    padded[:HALO, :] = low[...].astype(F32)
    padded[HALO : HALO + rows, :] = own[...].astype(F32)
    padded[HALO + rows :, :] = high[...].astype(F32)


def conv_body(idx, glu, low, high, kernel, c_out, stats, padded):
    fill_padded(low, glu, high, padded)
    rows = glu.shape[0]
    taps = kernel.shape[0]
    shift = HALO - (taps - 1) // 2
    total = kernel[0:1, :] * padded[shift : shift + rows, :]
    for tap in range(1, taps):
        total = total + kernel[tap : tap + 1, :] * padded[shift + tap : shift + tap + rows, :]
    c_out[...] = total
    mean = jnp.mean(total, axis=0, keepdims=True)
    centred = total - mean
    stats[0:1, :] = mean
    stats[1:2, :] = jnp.sum(centred * centred, axis=0, keepdims=True)
    stats[2:, :] = jnp.zeros((stats.shape[0] - 2, stats.shape[1]), F32)


def batch_body(base, idx, c, stats, params, weights, q_out, act_out, keep, send, work):
    spread = stats[1:2, :]
    q = (c[...] - stats[0:1, :]) * spread
    q_out[...] = q
    a = q * params[0:1, :] + params[1:2, :]
    act = (a * jax.nn.sigmoid(a)).astype(BF16)
    act_out[...] = act
    work[...] = dot_cols(act, weights[:, base : base + act.shape[1]])
    split(idx, work, keep, send)


def feed_pullback(idx, grad, u, weights, base, f_out, du_out, keep, send, work):
    hidden = u.shape[1]
    f = (0.5 * grad).astype(BF16)
    f_out[...] = f
    value = u[...]
    logistic = jax.nn.sigmoid(value)
    back = dot(f, weights[:, base + hidden : base + 2 * hidden])
    du = (back * swish_slope(value, logistic)).astype(BF16)
    du_out[...] = du
    work[...] = dot_cols(du, weights[:, base : base + hidden])
    split(idx, work, keep, send)


def final_body(base, idx, x_ref, t1, t2, gains, cot, u, weights, y_out, d_out, gain_out, f_out, du_out, keep, send, work):
    join(idx, t1, t2, work)
    x = x_ref[...] + 0.5 * work[...]
    normal, unused = normalized(x)
    gain = gains[4:5, :]
    work[...] = normal * gain
    width = y_out.shape[1]
    y_out[...] = work[:, pl.ds(pl.multiple_of(idx[0] * width, width), width)].astype(BF16)
    grad, gain_grad = norm_pullback(cot[...].astype(F32), x, gain)
    gain_out[...] = gain_grad
    d_out[...] = grad
    feed_pullback(idx, grad, u, weights, base, f_out, du_out, keep, send, work)


def conv_back_body(base, idx, x_ref, d_ref, t1, t2, gains, q, params, weights, d_out, f_out, da_out, edges, gain_out, work):
    join(idx, t1, t2, work)
    grad, gain_grad = norm_pullback(work[...], x_ref[...], gains[3:4, :])
    gain_out[...] = gain_grad
    grad = d_ref[...] + grad
    d_out[...] = grad
    f = grad.astype(BF16)
    f_out[...] = f
    rows, channels = q.shape
    value = q[...]
    a = value * params[0:1, :] + params[1:2, :]
    da = dot(f, weights[:, base : base + channels]) * swish_slope(a, jax.nn.sigmoid(a))
    da_out[...] = da
    edges[0:1, :] = jnp.sum(da * value, axis=0, keepdims=True)
    edges[1:2, :] = jnp.sum(da, axis=0, keepdims=True)
    edges[2:8, :] = jnp.zeros((6, channels), F32)
    for at, part in enumerate((da[:HALO], value[:HALO], da[rows - HALO :], value[rows - HALO :])):
        edges[8 + at * HALO : 8 + (at + 1) * HALO, :] = part


def gate_back_body(ctx, counted, idx, da, q, sums, near, far, stats, params, kernel, paired, weights, dc_out, dg_out, keep, send, padded, work):
    rows, channels = q.shape
    odd = idx[3] % 2 == 1
    low = jnp.where(odd, near[8 + 2 * HALO :, :], far[8 + 2 * HALO :, :])
    high = jnp.where(odd, far[8 : 8 + 2 * HALO, :], near[8 : 8 + 2 * HALO, :])
    factor = stats[1:2, :] * params[0:1, :]
    mean_scale = sums[0:1, :] / counted
    mean_shift = sums[1:2, :] / counted

    def centred(grad, normal):
        return (factor * (grad - mean_shift - normal * mean_scale)).astype(BF16)

    dc = centred(da[...], q[...])
    dc_out[...] = dc
    before = (idx[3] > 0).astype(F32)
    after = (idx[3] < ctx - 1).astype(F32)
    padded[:HALO, :] = centred(low[:HALO, :], low[HALO:, :]).astype(F32) * before
    padded[HALO : HALO + rows, :] = dc.astype(F32)
    padded[HALO + rows :, :] = centred(high[:HALO, :], high[HALO:, :]).astype(F32) * after
    taps = kernel.shape[0]
    top = HALO + (taps - 1) // 2
    total = kernel[0:1, :] * padded[top : top + rows, :]
    for tap in range(1, taps):
        total = total + kernel[tap : tap + 1, :] * padded[top - tap : top - tap + rows, :]
    logistic = jax.nn.sigmoid(paired[:, channels:])
    through = total * logistic
    dg_out[:, :channels] = through.astype(BF16)
    dg_out[:, channels:] = (through * paired[:, :channels] * (1.0 - logistic)).astype(BF16)
    work[...] = dot_cols(dg_out[...], weights[:, : 2 * channels])
    split(idx, work, keep, send)


def taps_body(idx, glu, low, high, dc, out, padded):
    fill_padded(low, glu, high, padded)
    rows = glu.shape[0]
    grad = dc[...].astype(F32)
    shift = HALO - (out.shape[0] - 1) // 2
    for tap in range(out.shape[0]):
        out[tap : tap + 1, :] = jnp.sum(
            grad * padded[shift + tap : shift + tap + rows, :], axis=0, keepdims=True
        )


def attend_back_body(heads, ctx, base, idx, x_ref, d_ref, t1, t2, gains, weights, p, qa, *refs):
    blocks = refs[:ctx]
    d_out, f_out, gain_out, ds_out, dqa = refs[ctx : ctx + 5]
    out_blocks = refs[ctx + 5 : 2 * ctx + 5]
    pairs, grads, do, work = refs[2 * ctx + 5 :]
    fill_pairs(idx, blocks, pairs)
    join(idx, t1, t2, work)
    grad, gain_grad = norm_pullback(work[...], x_ref[...], gains[2:3, :])
    gain_out[...] = gain_grad
    grad = d_ref[...] + grad
    d_out[...] = grad
    f = grad.astype(BF16)
    f_out[...] = f
    rows, local = qa.shape
    size = local // heads
    scale = size**-0.5
    do[...] = dot(f, weights[:, base : base + local]).astype(BF16)
    for head in range(heads):
        columns = slice(head * size, (head + 1) * size)
        values = slice(local + head * size, local + (head + 1) * size)
        for at in range(rows // BLOCK):
            frames = slice(at * BLOCK, (at + 1) * BLOCK)
            dp = dot_cols(do[frames, columns], pairs[:, values])
            share = p[head, frames, :].astype(F32)
            balance = jnp.sum(share * dp, axis=1, keepdims=True)
            ds = (share * (dp - balance)).astype(BF16)
            ds_out[head, frames, :] = ds
            dqa[frames, columns] = dot(ds, pairs[:, columns]) * scale
        grads[:, columns] = (dot_rows(ds_out[head], qa[:, columns]) * scale).astype(BF16)
        grads[:, values] = dot_rows(p[head], do[:, columns]).astype(BF16)
    for at, block in enumerate(out_blocks):
        source = jnp.bitwise_xor(idx[3], at)
        block[...] = grads[pl.ds(pl.multiple_of(source * rows, rows), rows), :]


def position_back_body(heads, idx, ds, qb, relative, dqb, dr_out, wide, total):
    rows, local = qb.shape
    size = local // heads
    length = ds.shape[2]
    width = length + BLOCK
    scale = size**-0.5
    down = lax.broadcasted_iota(jnp.int32, (BLOCK, BLOCK), 0)
    across = lax.broadcasted_iota(jnp.int32, (BLOCK, BLOCK), 1)
    flip = (down + across == BLOCK - 1).astype(BF16)
    total[...] = jnp.zeros(total.shape, F32)
    wide[:, length:] = jnp.zeros((BLOCK, BLOCK), F32)
    for head in range(heads):
        columns = slice(head * size, (head + 1) * size)
        for at in range(rows // BLOCK):
            frames = slice(at * BLOCK, (at + 1) * BLOCK)
            first = rows - BLOCK * (at + 1)
            wide[:, :length] = dot(flip, ds[head, frames, :])
            turned = pltpu.roll(wide[...], 0, 1, stride=1, stride_axis=0).astype(BF16)
            turned_b = dot(turned, relative[first : first + width, columns]) * scale
            dqb[frames, columns] = jnp.dot(
                flip.astype(F32), turned_b, precision=lax.Precision.HIGHEST, preferred_element_type=F32
            )
            flipped = dot(flip, qb[frames, columns]).astype(BF16)
            total[first : first + width, columns] += dot_rows(turned, flipped)
    dr_out[...] = (total[...] * scale).astype(BF16)


def attend_out_body(ctx, idx, dqa, dqb, *refs):
    blocks = refs[:ctx]
    weights, dp_out, bias_out, keep, send, work = refs[ctx:]
    local = dqa.shape[1]
    bias_out[0:1, :] = jnp.sum(dqa[...], axis=0, keepdims=True)
    bias_out[1:2, :] = jnp.sum(dqb[...], axis=0, keepdims=True)
    dp_out[:, :local] = (dqa[...] + dqb[...]).astype(BF16)
    total = blocks[0][...].astype(F32)
    for block in blocks[1:]:
        total = total + block[...].astype(F32)
    dp_out[:, local:] = total.astype(BF16)
    work[...] = dot_cols(dp_out[...], weights[:, : 3 * local])
    split(idx, work, keep, send)


def feed_back_body(idx, x_ref, d_ref, t1, t2, gains, u, weights, d_out, f_out, du_out, gain_out, keep, send, work):
    join(idx, t1, t2, work)
    grad, gain_grad = norm_pullback(work[...], x_ref[...], gains[1:2, :])
    gain_out[...] = gain_grad
    grad = d_ref[...] + grad
    d_out[...] = grad
    feed_pullback(idx, grad, u, weights, 0, f_out, du_out, keep, send, work)


def last_body(idx, x_ref, d_ref, t1, t2, gains, two, three, four, five, bias, kernel, out, small, work, each):
    join(idx, t1, t2, work)
    grad, gain_grad = norm_pullback(work[...], x_ref[...].astype(F32), gains[0:1, :])
    for at, row in enumerate((gain_grad, two[...], three[...], four[...], five[...])):
        each[at : at + 1, :] = row
    part = out.shape[1]
    own = pl.ds(pl.multiple_of(idx[0] * part, part), part)
    taps = kernel.shape[0]
    small[:5, :] = each[:5, own]
    small[5:7, :] = bias[...]
    small[7 : 7 + taps, :] = kernel[...]
    small[7 + taps :, :] = jnp.zeros((small.shape[0] - 7 - taps, part), F32)
    work[...] = d_ref[...] + grad
    width = out.shape[1]
    out[...] = work[:, pl.ds(pl.multiple_of(idx[0] * width, width), width)]


FRAMES = ("fsdp", "ctx")


def paired_mesh():
    return lax.axis_size("fsdp") == 2


def gathered(idx, shard, after=(), stepwise=False):
    if not paired_mesh():
        whole = lax.all_gather(shard, FRAMES, axis=0, tiled=True)
        return whole, shard
    ctx = lax.axis_size("ctx")
    rows, width = shard.shape
    if after:
        shard = held(idx, shard, after)
    if not stepwise:
        mine = [shard] + [swap(shard, "ctx", step) for step in range(1, ctx)]
        mark = jnp.concatenate(mine, axis=0)
    else:
        near = jnp.concatenate([shard, swap(shard, "ctx", 1)], axis=0)
        mark = jnp.concatenate([near, swap(near, "ctx", 2)], axis=0)

    def ended(after=()):
        block = held(idx, mark, after) if after else mark
        outs = [((2 * ctx * rows, width), BF16)]
        body = functools.partial(place_body, ctx, rows)
        return call(body, outs, idx, block, swap(block, "fsdp", 1))[0]

    return (ended if stepwise else ended()), mark


def features_whole(value):
    near, far = swap(value, "tp", 1), swap(value, "tp", 2)
    return [value, near, far, swap(far, "tp", 1)]


def products(idx, pairs):
    depth = pairs[0][0].shape[1]
    width = sum(right.shape[1] for unused, right in pairs)
    flat = [array for pair in pairs for array in pair]
    ctx = lax.axis_size("ctx") if paired_mesh() else 0
    outs = [((depth // 2, width), BF16)] * 2 if ctx else [((depth, width), BF16)]
    body = functools.partial(wgrad_body, len(pairs), ctx)
    return call(body, outs, idx, *flat, scratch=[pltpu.VMEM((depth, width), BF16)])


def across(idx, made, after=()):
    if not paired_mesh():
        return made[0]
    return swap(held(idx, made[1], after) if after else made[1], "fsdp", 1)


def along(idx, made, others, after=()):
    if not paired_mesh():
        grads = jnp.concatenate([part[0] for part in made], axis=1)
        return grads, [lax.psum_scatter(grads, FRAMES, scatter_dimension=0, tiled=True)]
    ctx = lax.axis_size("ctx")
    rows = made[0][0].shape[0] // ctx
    width = sum(part[0].shape[1] for part in made)
    body = functools.partial(joined_body, len(made))
    mine = [part[0] for part in made]
    blocks = call(body, [((rows, width), BF16)] * ctx, idx, *mine, *others, after=after)
    return blocks[0], [blocks[0]] + [swap(blocks[at], "ctx", at) for at in range(1, ctx)]


def along_halves(idx, made, other, after=()):
    if not paired_mesh():
        parts = along(idx, [made], [other])
        return parts[0], lambda after=(): parts
    keep, send = halved(idx, made[0], other, after)
    came = swap(send, "ctx", 2)

    def rest(after=()):
        block, send = halved(idx, keep, came, after)
        return block, [block, swap(send, "ctx", 1)]

    return keep, rest


def halved(idx, left, right, after=()):
    part = ((left.shape[0] // 2, left.shape[1]), left.dtype)
    return call(functools.partial(joined_body, 1), [part] * 2, idx, left, right, after=after)


def finish(idx, parts, layout, after=()):
    rows, values, column = parts[0].shape[0], [], 0
    if paired_mesh():
        shapes = [
            ((count, rows, width // count) if kind == "middle" else (rows, width), F32)
            for kind, count, width in layout
        ]
        kinds = [(kind, width) for kind, unused, width in layout]
        body = functools.partial(finish_body, kinds, len(parts))
        values = call(body, shapes, idx, *parts, after=after, results=True)
    else:
        total = parts[0].astype(F32)
        for kind, count, width in layout:
            value = total[:, column : column + width]
            if kind == "middle":
                value = value.reshape(rows, count, width // count).swapaxes(0, 1)
            values.append(value)
            column += width
    turns = {"rows": lambda v: v, "turned": lambda v: v.T, "middle": lambda v: v.swapaxes(0, 1)}
    return [turns[kind](value) for (kind, unused, unused), value in zip(layout, values)]


def hold_body(idx, value, out):
    out[...] = value[...]


def held(idx, value, after):
    return call(hold_body, [(value.shape, value.dtype)], idx, value, after=after)[0]


def over_frames(value, merge):
    near, far, across = (swap(value, "ctx", step) for step in (1, 2, 3))
    value = merge(merge(value, near), merge(far, across))
    step = 1
    while step < lax.axis_size("fsdp"):
        value = merge(value, swap(value, "fsdp", step))
        step *= 2
    return value


def pooled(stats, rows):
    stats = jnp.concatenate([stats[:2], jnp.full_like(stats[:1], rows), stats[3:]], axis=0)

    def merge(left, right):
        gap = left[0:1] - right[0:1]
        mean = 0.5 * (left[0:1] + right[0:1])
        squares = left[1:2] + right[1:2] + gap * gap * (0.5 * left[2:3])
        return jnp.concatenate([mean, squares, 2.0 * left[2:3], left[3:]], axis=0)

    stats = over_frames(stats, merge)
    spread = lax.rsqrt(stats[1:2] / stats[2:3] + EPSILON)
    return jnp.concatenate([stats[0:1], spread, stats[2:]], axis=0)


def edges_summed(edges):
    near, far = swap(edges, "ctx", 1), swap(edges, "ctx", 3)
    sums = (edges[:8] + near[:8]) + (swap(edges[:8], "ctx", 2) + far[:8])
    step = 1
    while step < lax.axis_size("fsdp"):
        sums = sums + swap(sums, "fsdp", step)
        step *= 2
    return sums, near, far


def neighbours(first, last):
    count = lax.axis_size("ctx")
    up = [(i, i + 1) for i in range(count - 1)]
    down = [(i + 1, i) for i in range(count - 1)]
    return lax.ppermute(last, "ctx", up), lax.ppermute(first, "ctx", down)


def angle_tables(start, rows, width, features):
    step = 64
    column = jnp.arange(features, dtype=jnp.int32)
    rates = jnp.exp((column // 2).astype(F32) * (-2.0 * math.log(10000.0) / features))
    even = (column % 2 == 0)[None, :]
    near = (start + rows - 1 - step * jnp.arange(width // step, dtype=jnp.int32)).astype(F32)
    near = near[:, None] * rates[None, :]
    far = jnp.arange(step, dtype=jnp.int32).astype(F32)[:, None] * rates[None, :]
    sine, cosine = jnp.sin(near), jnp.cos(near)
    return (
        jnp.where(even, sine, cosine),
        jnp.where(even, -cosine, sine),
        jnp.cos(far),
        jnp.sin(far),
    )


def shards(
    tokens,
    first_expand,
    first_shrink,
    attend_input,
    position_map,
    position_bias,
    attend_output,
    gating_map,
    depth_kernel,
    batch_scale,
    batch_shift,
    mixing_map,
    second_expand,
    second_shrink,
    layer_gains,
    cotangent,
):
    rows, part = tokens.shape
    tp, ctx = lax.axis_size("tp"), lax.axis_size("ctx")
    features = part * tp
    shard = first_expand.shape[0]
    hidden = first_expand.shape[1]
    heads, size = position_bias.shape[1:]
    local = heads * size
    channels = depth_kernel.shape[1]
    length = rows * ctx
    width = length + rows
    tp_at = lax.axis_index("tp")
    ctx_at = lax.axis_index("ctx")
    idx = jnp.stack(
        [tp_at, tp_at % 2, lax.axis_index("fsdp"), ctx_at]
    ).astype(jnp.int32)

    packed_frames = call(
        pack_body, [((2 * rows + 16, part), BF16)], idx, tokens, cotangent, layer_gains
    )[0]
    blocks_whole = features_whole(packed_frames)
    one, one_mark = gathered(idx, jnp.concatenate([first_expand, first_shrink.T], axis=1))
    x0, cot, gains = call(
        features_body,
        [((rows, features), BF16), ((rows, features), BF16), ((5, features), F32)],
        idx,
        *blocks_whole,
    )
    bias = position_bias.reshape(2, local)
    params = jnp.stack([batch_scale, batch_shift])
    tables = angle_tables(ctx_at * rows, rows, width, features)
    thirds = [attend_input[:, at] for at in range(3)]
    two, two_mark = gathered(
        idx,
        jnp.concatenate(thirds + [position_map, attend_output.T], axis=1),
        [one_mark, blocks_whole[1], blocks_whole[2]],
    )
    halves_in = [gating_map[:, at] for at in range(2)]
    three, three_mark = gathered(
        idx,
        jnp.concatenate(halves_in + [mixing_map.T, second_expand, second_shrink.T], axis=1),
        [one_mark],
        stepwise=True,
    )
    at_pos, at_out = 3 * local, 4 * local
    at_mix, at_two = 2 * channels, 3 * channels

    stream = ((rows, features), F32)
    packed = ((rows, features), BF16)
    piece = ((rows // 2, features), BF16)
    gain_row = ((1, features), F32)
    work = pltpu.VMEM((rows, features), F32)
    inner_shape = (rows, hidden)

    z1, u1, h1, keep, send = call(
        functools.partial(feed_body, 0, 0, False),
        [packed, (inner_shape, F32), (inner_shape, BF16), piece, piece],
        idx,
        x0,
        gains,
        one,
        scratch=[work],
    )
    t1, t2 = tp_end(idx, tp_begin(keep, send, idx, [two_mark]), [two])
    embed, relative = call(
        functools.partial(relative_body, at_pos),
        [((width, features), BF16), ((width, local), BF16)],
        idx,
        *tables,
        two,
    )
    per_head = ((rows, local), BF16)
    x1, z2, qa, qb, kv = call(
        attend_in_body,
        [stream, packed, per_head, per_head, ((rows, 2 * local), BF16)],
        idx,
        x0,
        t1,
        t2,
        gains,
        two,
        bias,
        after=[three_mark],
        scratch=[work],
    )
    if callable(three):
        three = three([kv])
    pairs = [kv] + [swap(kv, "ctx", step) for step in range(1, ctx)]
    position = call(
        functools.partial(position_body, heads),
        [((heads, rows, length), F32)],
        idx,
        qb,
        relative,
    )[0]
    whole_pairs = pltpu.VMEM((length, 2 * local), BF16)
    p, mixed, keep, send = call(
        functools.partial(attend_body, heads, ctx, at_out),
        [((heads, rows, length), BF16), per_head, piece, piece],
        idx,
        qa,
        *pairs,
        position,
        two,
        scratch=[whole_pairs, work],
    )
    t1, t2 = tp_end(idx, tp_begin(keep, send, idx, [three]))
    edge = ((HALO, channels), BF16)
    x2, z3, paired, glu, first, last = call(
        conv_in_body,
        [
            stream,
            packed,
            ((rows, 2 * channels), F32),
            ((rows, channels), BF16),
            edge,
            edge,
        ],
        idx,
        x1,
        t1,
        t2,
        gains,
        three,
        scratch=[work],
    )
    low, high = neighbours(first, last)
    padded = pltpu.VMEM((rows + 2 * HALO, channels), F32)
    c, stats = call(
        conv_body,
        [((rows, channels), F32), ((8, channels), F32)],
        idx,
        glu,
        low,
        high,
        depth_kernel,
        scratch=[padded],
    )
    stats = pooled(stats, rows)
    q, act, keep, send = call(
        functools.partial(batch_body, at_mix),
        [((rows, channels), F32), ((rows, channels), BF16), piece, piece],
        idx,
        c,
        stats,
        params,
        three,
        scratch=[work],
    )
    t1, t2 = tp_sum(keep, send)
    x3, z4, u2, h2, keep, send = call(
        functools.partial(feed_body, 3, at_two, True),
        [stream, packed, (inner_shape, F32), (inner_shape, BF16), piece, piece],
        idx,
        x2,
        t1,
        t2,
        gains,
        three,
        scratch=[work],
    )
    t1, t2 = tp_sum(keep, send)
    outputs, d4, gain_five, f4, du2, keep, send = call(
        functools.partial(final_body, at_two),
        [
            ((rows, part), BF16),
            stream,
            gain_row,
            packed,
            (inner_shape, BF16),
            piece,
            piece,
        ],
        idx,
        x3,
        t1,
        t2,
        gains,
        cot,
        u2,
        three,
        scratch=[work],
    )
    total = tp_begin(keep, send)
    rear = products(idx, [(z4, du2), (f4, h2)])
    t1, t2 = tp_end(idx, total, [rear[0]])
    d3, f3, da, edges, gain_four = call(
        functools.partial(conv_back_body, at_mix),
        [
            stream,
            packed,
            ((rows, channels), F32),
            ((8 + 4 * HALO, channels), F32),
            gain_row,
        ],
        idx,
        x3,
        d4,
        t1,
        t2,
        gains,
        q,
        params,
        three,
        scratch=[work],
    )
    sums, near, far = edges_summed(edges)
    rear_other = across(idx, rear)
    counted = rows * lax.axis_size(FRAMES)
    dc, dg, keep, send = call(
        functools.partial(gate_back_body, ctx, counted),
        [
            ((rows, channels), BF16),
            ((rows, 2 * channels), BF16),
            piece,
            piece,
        ],
        idx,
        da,
        q,
        sums,
        near,
        far,
        stats,
        params,
        depth_kernel,
        paired,
        three,
        after=[rear_other],
        scratch=[padded, work],
    )
    total = tp_begin(keep, send)
    kernel_grad = call(
        taps_body,
        [(depth_kernel.shape, F32)],
        idx,
        glu,
        low,
        high,
        dc,
        scratch=[padded],
    )[0]
    middle = products(idx, [(z3, dg), (f3, act)])
    t1, t2 = tp_end(idx, total, [middle[0], kernel_grad])
    pair_block = ((rows, 2 * local), BF16)
    results = call(
        functools.partial(attend_back_body, heads, ctx, at_out),
        [stream, packed, gain_row, ((heads, rows, length), BF16), ((rows, local), F32)]
        + [pair_block] * ctx,
        idx,
        x2,
        d3,
        t1,
        t2,
        gains,
        two,
        p,
        qa,
        *pairs,
        scratch=[whole_pairs, whole_pairs, pltpu.VMEM((rows, local), BF16), work],
    )
    d2, f2, gain_three, ds, dqa = results[:5]
    pair_grads = [results[5]] + [
        swap(block, "ctx", step + 1) for step, block in enumerate(results[6:])
    ]
    dqb, dr = call(
        functools.partial(position_back_body, heads),
        [((rows, local), F32), ((width, local), BF16)],
        idx,
        ds,
        qb,
        relative,
        scratch=[pltpu.VMEM((BLOCK, length + BLOCK), F32), pltpu.VMEM((width, local), F32)],
    )
    middle_other = across(idx, middle, [ds])
    dp, bias_grad, keep, send = call(
        functools.partial(attend_out_body, ctx),
        [((rows, 3 * local), BF16), ((2, local), F32), piece, piece],
        idx,
        dqa,
        dqb,
        *pair_grads,
        two,
        after=[middle_other],
        scratch=[work],
    )
    total = tp_begin(keep, send)
    inner = products(idx, [(z2, dp), (embed, dr), (f2, mixed)])
    rear_total, rear_rest = along_halves(idx, rear, rear_other, [total])
    t1, t2 = tp_end(idx, total, [inner[0], rear_total])
    inner_other = across(idx, inner)
    d1, f1, du1, gain_two, keep, send = call(
        feed_back_body,
        [stream, ((rows, features), BF16), (inner_shape, BF16), gain_row, piece, piece],
        idx,
        x1,
        d2,
        t1,
        t2,
        gains,
        u1,
        one,
        scratch=[work],
    )
    front = products(idx, [(z1, du1), (f1, h1)])
    total = tp_begin(keep, send, idx, [front[0]])
    front_other = across(idx, front)
    inner_total, inner_parts = along(idx, [inner, middle], [inner_other, middle_other], [total])
    rear_total, rear_parts = rear_rest([inner_total])
    t1, t2 = tp_end(idx, total, [rear_total])
    taps = depth_kernel.shape[0]
    tokens_grad, small = call(
        last_body,
        [((rows, part), F32), ((-(-(7 + taps) // 8) * 8, part), F32)],
        idx,
        x0,
        d1,
        t1,
        t2,
        gains,
        gain_two,
        gain_three,
        gain_four,
        gain_five,
        bias_grad,
        kernel_grad,
        scratch=[work, pltpu.VMEM((8, features), F32)],
    )
    steps = [
        (axis, step)
        for axis in ("fsdp", "ctx")
        for step in (1, 2, 4, 8)
        if step < lax.axis_size(axis)
    ]
    small = small + swap(small, *steps[0])
    front_total, front_parts = along(idx, [front], [front_other], [small])
    for axis, step in steps[1:-1]:
        small = small + swap(small, axis, step)
    rear_expand, rear_shrink = finish(
        idx, rear_parts, [("rows", 1, hidden), ("turned", 1, hidden)], [front_total]
    )
    qkv_grad, map_grad, out_grad, gate_grad, mix_grad = finish(
        idx,
        inner_parts,
        [
            ("middle", 3, 3 * local),
            ("rows", 1, local),
            ("turned", 1, local),
            ("middle", 2, 2 * channels),
            ("turned", 1, channels),
        ],
        [front_total],
    )
    gains_grad, bias_grad, kernel_grad = call(
        finish_small_body,
        [((5, part), F32), ((2, heads, size), F32), ((taps, channels), F32)],
        idx,
        small,
        swap(small, *steps[-1]),
        results=True,
    )
    front_expand, front_shrink = finish(
        idx, front_parts, [("rows", 1, hidden), ("turned", 1, hidden)]
    )
    return (
        outputs,
        tokens_grad,
        front_expand,
        front_shrink,
        qkv_grad,
        map_grad,
        bias_grad,
        out_grad,
        gate_grad,
        kernel_grad,
        sums[0],
        sums[1],
        mix_grad,
        rear_expand,
        rear_shrink,
        gains_grad,
    )


def solution(mesh):
    frames = ("fsdp", "ctx")
    rows, columns = P(frames, "tp"), P("tp", frames)
    three_dims, last_only, one_dim = P(frames, None, "tp"), P(None, "tp"), P("tp")
    heads = P(None, "tp", None)
    return jax.shard_map(
        shards,
        mesh=mesh,
        in_specs=(
            rows,
            rows,
            columns,
            three_dims,
            rows,
            heads,
            columns,
            three_dims,
            last_only,
            one_dim,
            one_dim,
            columns,
            rows,
            columns,
            last_only,
            rows,
        ),
        out_specs=(
            rows,
            rows,
            rows,
            columns,
            three_dims,
            rows,
            heads,
            columns,
            three_dims,
            last_only,
            one_dim,
            one_dim,
            columns,
            rows,
            columns,
            last_only,
        ),
        check_vma=False,
    )
```

```python
import functools
import math

import jax
import jax.numpy as jnp
from jax import lax
from jax.experimental import pallas as pl
from jax.experimental.pallas import tpu as pltpu
from jax.sharding import PartitionSpec as P

F32 = jnp.float32
BF16 = jnp.bfloat16
EPSILON = 1e-05
HALO = 16
BLOCK = 128
VMEM_BYTES = 16 * 1024 * 1024
COST = 1


def call(body, outs, *args, after=(), scratch=(), results=False, vmem=VMEM_BYTES):
    first, extra = len(args), len(after)

    def kernel(*refs):
        body(*refs[:first], *refs[first + extra :])

    return pl.pallas_call(
        kernel,
        out_shape=[jax.ShapeDtypeStruct(*out) for out in outs],
        in_specs=[pl.BlockSpec(memory_space=pltpu.SMEM)]
        + [pl.BlockSpec(memory_space=pltpu.VMEM)] * (first - 1)
        + [pl.BlockSpec(memory_space=pl.ANY)] * extra,
        out_specs=[pl.BlockSpec() if results else pl.BlockSpec(memory_space=pltpu.VMEM)]
        * len(outs),
        scratch_shapes=list(scratch),
        compiler_params=pltpu.CompilerParams(vmem_limit_bytes=vmem),
        cost_estimate=pl.CostEstimate(flops=COST, bytes_accessed=COST, transcendentals=0),
    )(*args, *after)


def dot(left, right):
    return jnp.dot(left, right, preferred_element_type=F32)


def dot_cols(left, right):
    return lax.dot_general(left, right, (((1,), (1,)), ((), ())), preferred_element_type=F32)


def dot_rows(left, right):
    return lax.dot_general(left, right, (((0,), (0,)), ((), ())), preferred_element_type=F32)


def normalized(stream):
    centred = stream - jnp.mean(stream, axis=1, keepdims=True)
    spread = lax.rsqrt(jnp.mean(centred * centred, axis=1, keepdims=True) + EPSILON)
    return centred * spread, spread


def norm_pullback(grad, stream, gain):
    normal, spread = normalized(stream)
    scaled = grad * gain
    first = jnp.mean(scaled, axis=1, keepdims=True)
    second = jnp.mean(scaled * normal, axis=1, keepdims=True)
    return spread * (scaled - first - normal * second), jnp.sum(
        grad * normal, axis=0, keepdims=True
    )


def swish_slope(value, logistic):
    return logistic * (1.0 + value * (1.0 - logistic))


def halves(idx, rows):
    half = rows // 2
    mine = pl.multiple_of(idx[1] * half, half)
    theirs = pl.multiple_of((1 - idx[1]) * half, half)
    return pl.ds(mine, half), pl.ds(theirs, half)


def split(idx, whole, keep, send):
    mine, theirs = halves(idx, whole.shape[0])
    keep[...] = whole[mine, :].astype(BF16)
    send[...] = whole[theirs, :].astype(BF16)


def join(idx, t_mine, t_theirs, whole):
    mine, theirs = halves(idx, whole.shape[0])
    whole[mine, :] = t_mine[...].astype(F32)
    whole[theirs, :] = t_theirs[...].astype(F32)


def xor_pairs(count, step):
    return [(i, i ^ step) for i in range(count)]


def swap(value, axis, step):
    return lax.ppermute(value, axis, xor_pairs(lax.axis_size(axis), step))


def added(left, right):
    return (left.astype(F32) + right.astype(F32)).astype(BF16)


def joined_body(count, idx, *refs):
    outs = refs[2 * count :]
    rows, column = outs[0].shape[0], 0
    for left, right in zip(refs[:count], refs[count : 2 * count]):
        total = (left[...].astype(F32) + right[...].astype(F32)).astype(BF16)
        width = total.shape[1]
        for at, out in enumerate(outs):
            out[:, column : column + width] = total[at * rows : (at + 1) * rows, :]
        column += width


def added_after(idx, left, right, after):
    body = functools.partial(joined_body, 1)
    return call(body, [(left.shape, left.dtype)], idx, left, right, after=after)[0]


def tp_begin(keep, send, idx=None, after=()):
    other = swap(send, "tp", 1)
    return added_after(idx, keep, other, after) if after else added(keep, other)


def tp_end(idx, total, after=()):
    other = swap(total, "tp", 2)
    total = added_after(idx, total, other, after) if after else added(total, other)
    return total, swap(total, "tp", 1)


def tp_sum(keep, send):
    return tp_end(None, tp_begin(keep, send))


def place_body(ctx, rows, idx, *refs):
    out = refs[-1]
    blocks = []
    for ref in refs[:-1]:
        for at in range(ref.shape[0] // rows):
            blocks.append(ref[at * rows : (at + 1) * rows, :])
    for at, block in enumerate(blocks):
        half = idx[2] if at < ctx else 1 - idx[2]
        target = half * ctx + jnp.bitwise_xor(idx[3], at % ctx)
        out[pl.ds(pl.multiple_of(target * rows, rows), rows), :] = block


def pack_body(idx, tokens, cot, gains, out):
    rows = tokens.shape[0]
    out[:rows, :] = tokens[...]
    out[rows : 2 * rows, :] = cot[...]
    rest = gains[...]
    pieces = []
    for unused in range(3):
        piece = rest.astype(BF16).astype(F32)
        pieces.append(piece)
        rest = rest - piece
    pieces.append(jnp.zeros((1, rest.shape[1]), F32))
    out[2 * rows :, :] = jnp.concatenate(pieces, axis=0).astype(BF16)


def features_body(idx, *refs):
    blocks = refs[:4]
    x_out, cot_out, gains_out = refs[4:]
    rows, features = x_out.shape
    part = features // 4
    for at in range(4):
        target = jnp.bitwise_xor(idx[0], at)
        columns = pl.ds(pl.multiple_of(target * part, part), part)
        x_out[:, columns] = blocks[at][:rows, :]
        cot_out[:, columns] = blocks[at][rows : 2 * rows, :]
        pieces = blocks[at][2 * rows :, :].astype(F32)
        gains_out[:, columns] = (pieces[0:5] + pieces[5:10]) + pieces[10:15]


def finish_body(layout, parts, idx, *refs):
    total = refs[0][...].astype(F32)
    for ref in refs[1:parts]:
        total = total + ref[...].astype(F32)
    column = 0
    for (kind, width), out in zip(layout, refs[parts:]):
        if kind == "middle":
            count = out.shape[0]
            each = width // count
            for at in range(count):
                out[at] = total[:, column + at * each : column + (at + 1) * each]
        else:
            out[...] = total[:, column : column + width]
        column += width


def finish_small_body(idx, left, right, gains_out, bias_out, kernel_out):
    total = left[...] + right[...]
    gains_out[...] = total[:5]
    heads, size = bias_out.shape[1:]
    for head in range(heads):
        bias_out[:, head, :] = total[5:7, head * size : (head + 1) * size]
    kernel_out[...] = total[7 : 7 + kernel_out.shape[0]]


def wgrad_body(pairs, ctx, idx, *refs):
    outs, scratch = refs[2 * pairs : -1], refs[-1]
    column = 0
    for at in range(pairs):
        left, right = refs[2 * at], refs[2 * at + 1]
        width = right.shape[1]
        scratch[:, column : column + width] = dot_rows(left[...], right[...]).astype(BF16)
        column += width
    if not ctx:
        outs[0][...] = scratch[...]
        return
    rows = scratch.shape[0] // (2 * ctx)
    for half, out in zip((idx[2], 1 - idx[2]), outs):
        for at in range(ctx):
            source = half * ctx + jnp.bitwise_xor(idx[3], at)
            out[at * rows : (at + 1) * rows, :] = scratch[
                pl.ds(pl.multiple_of(source * rows, rows), rows), :
            ]


def feed_body(gain_at, base, joined, idx, *refs):
    if joined:
        x_ref, t1, t2, gains, weights, x_out, z_out, u_out, h_out, keep, send, work = refs
        join(idx, t1, t2, work)
        x = x_ref[...] + work[...]
        x_out[...] = x
    else:
        x_ref, gains, weights, z_out, u_out, h_out, keep, send, work = refs
        x = x_ref[...].astype(F32)
    hidden = u_out.shape[1]
    normal, unused = normalized(x)
    z = (normal * gains[gain_at : gain_at + 1, :]).astype(BF16)
    z_out[...] = z
    u = dot(z, weights[:, base : base + hidden])
    u_out[...] = u
    h = (u * jax.nn.sigmoid(u)).astype(BF16)
    h_out[...] = h
    work[...] = dot_cols(h, weights[:, base + hidden : base + 2 * hidden])
    split(idx, work, keep, send)


def attend_in_body(idx, x_ref, t1, t2, gains, weights, bias, x_out, z_out, qa, qb, kv, work):
    join(idx, t1, t2, work)
    x = x_ref[...].astype(F32) + 0.5 * work[...]
    x_out[...] = x
    normal, unused = normalized(x)
    z = (normal * gains[1:2, :]).astype(BF16)
    z_out[...] = z
    local = bias.shape[1]
    project = dot(z, weights[:, : 3 * local])
    query = project[:, :local]
    qa[...] = (query + bias[0:1, :]).astype(BF16)
    qb[...] = (query + bias[1:2, :]).astype(BF16)
    kv[...] = project[:, local:].astype(BF16)


def relative_body(base, idx, near_p, near_q, far_c, far_s, weights, embed, relative):
    step = far_c.shape[0]
    cos, sin = far_c[...], far_s[...]
    for at in range(embed.shape[0] // step):
        value = near_p[at : at + 1, :] * cos + near_q[at : at + 1, :] * sin
        embed[at * step : (at + 1) * step, :] = value.astype(BF16)
    relative[...] = dot(embed[...], weights[:, base : base + relative.shape[1]]).astype(BF16)


def position_body(heads, idx, qb, relative, out):
    rows, local = qb.shape
    size = local // heads
    length = out.shape[2]
    width = length + BLOCK
    for head in range(heads):
        columns = slice(head * size, (head + 1) * size)
        for at in range(rows // BLOCK):
            frames = slice(at * BLOCK, (at + 1) * BLOCK)
            first = rows - BLOCK * (at + 1)
            wide = dot_cols(qb[frames, columns], relative[first : first + width, columns])
            turned = pltpu.roll(wide, width - (BLOCK - 1), 1, stride=1, stride_axis=0)
            out[head, frames, :] = turned[:, :length]


def fill_pairs(idx, blocks, whole):
    rows = blocks[0].shape[0]
    for at, block in enumerate(blocks):
        target = jnp.bitwise_xor(idx[3], at)
        whole[pl.ds(pl.multiple_of(target * rows, rows), rows), :] = block[...]


def attend_body(heads, ctx, base, idx, qa, *refs):
    blocks = refs[:ctx]
    position, weights, p_out, mixed, keep, send, pairs, work = refs[ctx:]
    fill_pairs(idx, blocks, pairs)
    rows, local = qa.shape
    size = local // heads
    scale = size**-0.5
    for head in range(heads):
        columns = slice(head * size, (head + 1) * size)
        values = slice(local + head * size, local + (head + 1) * size)
        for at in range(rows // BLOCK):
            frames = slice(at * BLOCK, (at + 1) * BLOCK)
            scores = (dot_cols(qa[frames, columns], pairs[:, columns]) + position[head, frames, :]) * scale
            raised = jnp.exp(scores - jnp.max(scores, axis=1, keepdims=True))
            share = (raised * (1.0 / jnp.sum(raised, axis=1, keepdims=True))).astype(BF16)
            p_out[head, frames, :] = share
            mixed[frames, columns] = dot(share, pairs[:, values]).astype(BF16)
    work[...] = dot_cols(mixed[...], weights[:, base : base + local])
    split(idx, work, keep, send)


def conv_in_body(idx, x_ref, t1, t2, gains, weights, x_out, z_out, g_out, glu, first, last, work):
    join(idx, t1, t2, work)
    x = x_ref[...] + work[...]
    x_out[...] = x
    normal, unused = normalized(x)
    z = (normal * gains[2:3, :]).astype(BF16)
    z_out[...] = z
    rows, channels = glu.shape
    paired = dot(z, weights[:, : 2 * channels])
    g_out[...] = paired
    gated = (paired[:, :channels] * jax.nn.sigmoid(paired[:, channels:])).astype(BF16)
    glu[...] = gated
    first[...] = gated[:HALO, :]
    last[...] = gated[rows - HALO :, :]


def fill_padded(low, own, high, padded):
    rows = own.shape[0]
    padded[:HALO, :] = low[...].astype(F32)
    padded[HALO : HALO + rows, :] = own[...].astype(F32)
    padded[HALO + rows :, :] = high[...].astype(F32)


def conv_body(idx, glu, low, high, kernel, c_out, stats, padded):
    fill_padded(low, glu, high, padded)
    rows = glu.shape[0]
    taps = kernel.shape[0]
    shift = HALO - (taps - 1) // 2
    total = kernel[0:1, :] * padded[shift : shift + rows, :]
    for tap in range(1, taps):
        total = total + kernel[tap : tap + 1, :] * padded[shift + tap : shift + tap + rows, :]
    c_out[...] = total
    mean = jnp.mean(total, axis=0, keepdims=True)
    centred = total - mean
    stats[0:1, :] = mean
    stats[1:2, :] = jnp.sum(centred * centred, axis=0, keepdims=True)
    stats[2:, :] = jnp.zeros((stats.shape[0] - 2, stats.shape[1]), F32)


def batch_body(base, idx, c, stats, params, weights, q_out, act_out, keep, send, work):
    spread = stats[1:2, :]
    q = (c[...] - stats[0:1, :]) * spread
    q_out[...] = q
    a = q * params[0:1, :] + params[1:2, :]
    act = (a * jax.nn.sigmoid(a)).astype(BF16)
    act_out[...] = act
    work[...] = dot_cols(act, weights[:, base : base + act.shape[1]])
    split(idx, work, keep, send)


def feed_pullback(idx, grad, u, weights, base, f_out, du_out, keep, send, work):
    hidden = u.shape[1]
    f = (0.5 * grad).astype(BF16)
    f_out[...] = f
    value = u[...]
    logistic = jax.nn.sigmoid(value)
    back = dot(f, weights[:, base + hidden : base + 2 * hidden])
    du = (back * swish_slope(value, logistic)).astype(BF16)
    du_out[...] = du
    work[...] = dot_cols(du, weights[:, base : base + hidden])
    split(idx, work, keep, send)


def final_body(base, idx, x_ref, t1, t2, gains, cot, u, weights, y_out, d_out, gain_out, f_out, du_out, keep, send, work):
    join(idx, t1, t2, work)
    x = x_ref[...] + 0.5 * work[...]
    normal, unused = normalized(x)
    gain = gains[4:5, :]
    work[...] = normal * gain
    width = y_out.shape[1]
    y_out[...] = work[:, pl.ds(pl.multiple_of(idx[0] * width, width), width)].astype(BF16)
    grad, gain_grad = norm_pullback(cot[...].astype(F32), x, gain)
    gain_out[...] = gain_grad
    d_out[...] = grad
    feed_pullback(idx, grad, u, weights, base, f_out, du_out, keep, send, work)


def conv_back_body(base, idx, x_ref, d_ref, t1, t2, gains, q, params, weights, d_out, f_out, da_out, edges, gain_out, work):
    join(idx, t1, t2, work)
    grad, gain_grad = norm_pullback(work[...], x_ref[...], gains[3:4, :])
    gain_out[...] = gain_grad
    grad = d_ref[...] + grad
    d_out[...] = grad
    f = grad.astype(BF16)
    f_out[...] = f
    rows, channels = q.shape
    value = q[...]
    a = value * params[0:1, :] + params[1:2, :]
    da = dot(f, weights[:, base : base + channels]) * swish_slope(a, jax.nn.sigmoid(a))
    da_out[...] = da
    edges[0:1, :] = jnp.sum(da * value, axis=0, keepdims=True)
    edges[1:2, :] = jnp.sum(da, axis=0, keepdims=True)
    edges[2:8, :] = jnp.zeros((6, channels), F32)
    for at, part in enumerate((da[:HALO], value[:HALO], da[rows - HALO :], value[rows - HALO :])):
        edges[8 + at * HALO : 8 + (at + 1) * HALO, :] = part


def gate_back_body(ctx, counted, idx, da, q, sums, near, far, stats, params, kernel, paired, weights, dc_out, dg_out, keep, send, padded, work):
    rows, channels = q.shape
    odd = idx[3] % 2 == 1
    low = jnp.where(odd, near[8 + 2 * HALO :, :], far[8 + 2 * HALO :, :])
    high = jnp.where(odd, far[8 : 8 + 2 * HALO, :], near[8 : 8 + 2 * HALO, :])
    factor = stats[1:2, :] * params[0:1, :]
    mean_scale = sums[0:1, :] / counted
    mean_shift = sums[1:2, :] / counted

    def centred(grad, normal):
        return (factor * (grad - mean_shift - normal * mean_scale)).astype(BF16)

    dc = centred(da[...], q[...])
    dc_out[...] = dc
    before = (idx[3] > 0).astype(F32)
    after = (idx[3] < ctx - 1).astype(F32)
    padded[:HALO, :] = centred(low[:HALO, :], low[HALO:, :]).astype(F32) * before
    padded[HALO : HALO + rows, :] = dc.astype(F32)
    padded[HALO + rows :, :] = centred(high[:HALO, :], high[HALO:, :]).astype(F32) * after
    taps = kernel.shape[0]
    top = HALO + (taps - 1) // 2
    total = kernel[0:1, :] * padded[top : top + rows, :]
    for tap in range(1, taps):
        total = total + kernel[tap : tap + 1, :] * padded[top - tap : top - tap + rows, :]
    logistic = jax.nn.sigmoid(paired[:, channels:])
    through = total * logistic
    dg_out[:, :channels] = through.astype(BF16)
    dg_out[:, channels:] = (through * paired[:, :channels] * (1.0 - logistic)).astype(BF16)
    work[...] = dot_cols(dg_out[...], weights[:, : 2 * channels])
    split(idx, work, keep, send)


def taps_body(idx, glu, low, high, dc, out, padded):
    fill_padded(low, glu, high, padded)
    rows = glu.shape[0]
    grad = dc[...].astype(F32)
    shift = HALO - (out.shape[0] - 1) // 2
    for tap in range(out.shape[0]):
        out[tap : tap + 1, :] = jnp.sum(
            grad * padded[shift + tap : shift + tap + rows, :], axis=0, keepdims=True
        )


def attend_back_body(heads, ctx, base, idx, x_ref, d_ref, t1, t2, gains, weights, p, qa, *refs):
    blocks = refs[:ctx]
    d_out, f_out, gain_out, ds_out, dqa = refs[ctx : ctx + 5]
    out_blocks = refs[ctx + 5 : 2 * ctx + 5]
    pairs, grads, do, work = refs[2 * ctx + 5 :]
    fill_pairs(idx, blocks, pairs)
    join(idx, t1, t2, work)
    grad, gain_grad = norm_pullback(work[...], x_ref[...], gains[2:3, :])
    gain_out[...] = gain_grad
    grad = d_ref[...] + grad
    d_out[...] = grad
    f = grad.astype(BF16)
    f_out[...] = f
    rows, local = qa.shape
    size = local // heads
    scale = size**-0.5
    do[...] = dot(f, weights[:, base : base + local]).astype(BF16)
    for head in range(heads):
        columns = slice(head * size, (head + 1) * size)
        values = slice(local + head * size, local + (head + 1) * size)
        for at in range(rows // BLOCK):
            frames = slice(at * BLOCK, (at + 1) * BLOCK)
            dp = dot_cols(do[frames, columns], pairs[:, values])
            share = p[head, frames, :].astype(F32)
            balance = jnp.sum(share * dp, axis=1, keepdims=True)
            ds = (share * (dp - balance)).astype(BF16)
            ds_out[head, frames, :] = ds
            dqa[frames, columns] = dot(ds, pairs[:, columns]) * scale
        grads[:, columns] = (dot_rows(ds_out[head], qa[:, columns]) * scale).astype(BF16)
        grads[:, values] = dot_rows(p[head], do[:, columns]).astype(BF16)
    for at, block in enumerate(out_blocks):
        source = jnp.bitwise_xor(idx[3], at)
        block[...] = grads[pl.ds(pl.multiple_of(source * rows, rows), rows), :]


def position_back_body(heads, idx, ds, qb, relative, dqb, dr_out, wide, total):
    rows, local = qb.shape
    size = local // heads
    length = ds.shape[2]
    width = length + BLOCK
    scale = size**-0.5
    down = lax.broadcasted_iota(jnp.int32, (BLOCK, BLOCK), 0)
    across = lax.broadcasted_iota(jnp.int32, (BLOCK, BLOCK), 1)
    flip = (down + across == BLOCK - 1).astype(BF16)
    total[...] = jnp.zeros(total.shape, F32)
    wide[:, length:] = jnp.zeros((BLOCK, BLOCK), F32)
    for head in range(heads):
        columns = slice(head * size, (head + 1) * size)
        for at in range(rows // BLOCK):
            frames = slice(at * BLOCK, (at + 1) * BLOCK)
            first = rows - BLOCK * (at + 1)
            wide[:, :length] = dot(flip, ds[head, frames, :])
            turned = pltpu.roll(wide[...], 0, 1, stride=1, stride_axis=0).astype(BF16)
            turned_b = dot(turned, relative[first : first + width, columns]) * scale
            dqb[frames, columns] = jnp.dot(
                flip.astype(F32), turned_b, precision=lax.Precision.HIGHEST, preferred_element_type=F32
            )
            flipped = dot(flip, qb[frames, columns]).astype(BF16)
            total[first : first + width, columns] += dot_rows(turned, flipped)
    dr_out[...] = (total[...] * scale).astype(BF16)


def attend_out_body(ctx, idx, dqa, dqb, *refs):
    blocks = refs[:ctx]
    weights, dp_out, bias_out, keep, send, work = refs[ctx:]
    local = dqa.shape[1]
    bias_out[0:1, :] = jnp.sum(dqa[...], axis=0, keepdims=True)
    bias_out[1:2, :] = jnp.sum(dqb[...], axis=0, keepdims=True)
    dp_out[:, :local] = (dqa[...] + dqb[...]).astype(BF16)
    total = blocks[0][...].astype(F32)
    for block in blocks[1:]:
        total = total + block[...].astype(F32)
    dp_out[:, local:] = total.astype(BF16)
    work[...] = dot_cols(dp_out[...], weights[:, : 3 * local])
    split(idx, work, keep, send)


def feed_back_body(idx, x_ref, d_ref, t1, t2, gains, u, weights, d_out, f_out, du_out, gain_out, keep, send, work):
    join(idx, t1, t2, work)
    grad, gain_grad = norm_pullback(work[...], x_ref[...], gains[1:2, :])
    gain_out[...] = gain_grad
    grad = d_ref[...] + grad
    d_out[...] = grad
    feed_pullback(idx, grad, u, weights, 0, f_out, du_out, keep, send, work)


def last_body(idx, x_ref, d_ref, t1, t2, gains, two, three, four, five, bias, kernel, out, small, work, each):
    join(idx, t1, t2, work)
    grad, gain_grad = norm_pullback(work[...], x_ref[...].astype(F32), gains[0:1, :])
    for at, row in enumerate((gain_grad, two[...], three[...], four[...], five[...])):
        each[at : at + 1, :] = row
    part = out.shape[1]
    own = pl.ds(pl.multiple_of(idx[0] * part, part), part)
    taps = kernel.shape[0]
    small[:5, :] = each[:5, own]
    small[5:7, :] = bias[...]
    small[7 : 7 + taps, :] = kernel[...]
    small[7 + taps :, :] = jnp.zeros((small.shape[0] - 7 - taps, part), F32)
    work[...] = d_ref[...] + grad
    width = out.shape[1]
    out[...] = work[:, pl.ds(pl.multiple_of(idx[0] * width, width), width)]


FRAMES = ("fsdp", "ctx")


def paired_mesh():
    return lax.axis_size("fsdp") == 2


def gathered(idx, shard, after=(), stepwise=False):
    if not paired_mesh():
        whole = lax.all_gather(shard, FRAMES, axis=0, tiled=True)
        return whole, shard
    ctx = lax.axis_size("ctx")
    rows, width = shard.shape
    if after:
        shard = held(idx, shard, after)
    if not stepwise:
        mine = [shard] + [swap(shard, "ctx", step) for step in range(1, ctx)]
        mark = jnp.concatenate(mine, axis=0)
    else:
        near = jnp.concatenate([shard, swap(shard, "ctx", 1)], axis=0)
        mark = jnp.concatenate([near, swap(near, "ctx", 2)], axis=0)

    def ended(after=()):
        block = held(idx, mark, after) if after else mark
        outs = [((2 * ctx * rows, width), BF16)]
        body = functools.partial(place_body, ctx, rows)
        return call(body, outs, idx, block, swap(block, "fsdp", 1))[0]

    return (ended if stepwise else ended()), mark


def features_whole(value):
    near, far = swap(value, "tp", 1), swap(value, "tp", 2)
    return [value, near, far, swap(far, "tp", 1)]


def products(idx, pairs):
    depth = pairs[0][0].shape[1]
    width = sum(right.shape[1] for unused, right in pairs)
    flat = [array for pair in pairs for array in pair]
    ctx = lax.axis_size("ctx") if paired_mesh() else 0
    outs = [((depth // 2, width), BF16)] * 2 if ctx else [((depth, width), BF16)]
    body = functools.partial(wgrad_body, len(pairs), ctx)
    return call(body, outs, idx, *flat, scratch=[pltpu.VMEM((depth, width), BF16)])


def across(idx, made, after=()):
    if not paired_mesh():
        return made[0]
    return swap(held(idx, made[1], after) if after else made[1], "fsdp", 1)


def along(idx, made, others, after=()):
    if not paired_mesh():
        grads = jnp.concatenate([part[0] for part in made], axis=1)
        return grads, [lax.psum_scatter(grads, FRAMES, scatter_dimension=0, tiled=True)]
    ctx = lax.axis_size("ctx")
    rows = made[0][0].shape[0] // ctx
    width = sum(part[0].shape[1] for part in made)
    body = functools.partial(joined_body, len(made))
    mine = [part[0] for part in made]
    blocks = call(body, [((rows, width), BF16)] * ctx, idx, *mine, *others, after=after)
    return blocks[0], [blocks[0]] + [swap(blocks[at], "ctx", at) for at in range(1, ctx)]


def along_halves(idx, made, other, after=()):
    if not paired_mesh():
        parts = along(idx, [made], [other])
        return parts[0], lambda after=(): parts
    keep, send = halved(idx, made[0], other, after)
    came = swap(send, "ctx", 2)

    def rest(after=()):
        block, send = halved(idx, keep, came, after)
        return block, [block, swap(send, "ctx", 1)]

    return keep, rest


def halved(idx, left, right, after=()):
    part = ((left.shape[0] // 2, left.shape[1]), left.dtype)
    return call(functools.partial(joined_body, 1), [part] * 2, idx, left, right, after=after)


def finish(idx, parts, layout, after=()):
    rows, values, column = parts[0].shape[0], [], 0
    if paired_mesh():
        shapes = [
            ((count, rows, width // count) if kind == "middle" else (rows, width), F32)
            for kind, count, width in layout
        ]
        kinds = [(kind, width) for kind, unused, width in layout]
        body = functools.partial(finish_body, kinds, len(parts))
        values = call(body, shapes, idx, *parts, after=after, results=True)
    else:
        total = parts[0].astype(F32)
        for kind, count, width in layout:
            value = total[:, column : column + width]
            if kind == "middle":
                value = value.reshape(rows, count, width // count).swapaxes(0, 1)
            values.append(value)
            column += width
    turns = {"rows": lambda v: v, "turned": lambda v: v.T, "middle": lambda v: v.swapaxes(0, 1)}
    return [turns[kind](value) for (kind, unused, unused), value in zip(layout, values)]


def hold_body(idx, value, out):
    out[...] = value[...]


def held(idx, value, after):
    return call(hold_body, [(value.shape, value.dtype)], idx, value, after=after)[0]


def over_frames(value, merge):
    near, far, across = (swap(value, "ctx", step) for step in (1, 2, 3))
    value = merge(merge(value, near), merge(far, across))
    step = 1
    while step < lax.axis_size("fsdp"):
        value = merge(value, swap(value, "fsdp", step))
        step *= 2
    return value


def pooled(stats, rows):
    stats = jnp.concatenate([stats[:2], jnp.full_like(stats[:1], rows), stats[3:]], axis=0)

    def merge(left, right):
        gap = left[0:1] - right[0:1]
        mean = 0.5 * (left[0:1] + right[0:1])
        squares = left[1:2] + right[1:2] + gap * gap * (0.5 * left[2:3])
        return jnp.concatenate([mean, squares, 2.0 * left[2:3], left[3:]], axis=0)

    stats = over_frames(stats, merge)
    spread = lax.rsqrt(stats[1:2] / stats[2:3] + EPSILON)
    return jnp.concatenate([stats[0:1], spread, stats[2:]], axis=0)


def edges_summed(edges):
    near, far = swap(edges, "ctx", 1), swap(edges, "ctx", 3)
    sums = (edges[:8] + near[:8]) + (swap(edges[:8], "ctx", 2) + far[:8])
    step = 1
    while step < lax.axis_size("fsdp"):
        sums = sums + swap(sums, "fsdp", step)
        step *= 2
    return sums, near, far


def neighbours(first, last):
    count = lax.axis_size("ctx")
    up = [(i, i + 1) for i in range(count - 1)]
    down = [(i + 1, i) for i in range(count - 1)]
    return lax.ppermute(last, "ctx", up), lax.ppermute(first, "ctx", down)


def angle_tables(start, rows, width, features):
    step = 64
    column = jnp.arange(features, dtype=jnp.int32)
    rates = jnp.exp((column // 2).astype(F32) * (-2.0 * math.log(10000.0) / features))
    even = (column % 2 == 0)[None, :]
    near = (start + rows - 1 - step * jnp.arange(width // step, dtype=jnp.int32)).astype(F32)
    near = near[:, None] * rates[None, :]
    far = jnp.arange(step, dtype=jnp.int32).astype(F32)[:, None] * rates[None, :]
    sine, cosine = jnp.sin(near), jnp.cos(near)
    return (
        jnp.where(even, sine, cosine),
        jnp.where(even, -cosine, sine),
        jnp.cos(far),
        jnp.sin(far),
    )


def shards(
    tokens,
    first_expand,
    first_shrink,
    attend_input,
    position_map,
    position_bias,
    attend_output,
    gating_map,
    depth_kernel,
    batch_scale,
    batch_shift,
    mixing_map,
    second_expand,
    second_shrink,
    layer_gains,
    cotangent,
):
    rows, part = tokens.shape
    tp, ctx = lax.axis_size("tp"), lax.axis_size("ctx")
    features = part * tp
    shard = first_expand.shape[0]
    hidden = first_expand.shape[1]
    heads, size = position_bias.shape[1:]
    local = heads * size
    channels = depth_kernel.shape[1]
    length = rows * ctx
    width = length + rows
    tp_at = lax.axis_index("tp")
    ctx_at = lax.axis_index("ctx")
    idx = jnp.stack(
        [tp_at, tp_at % 2, lax.axis_index("fsdp"), ctx_at]
    ).astype(jnp.int32)

    packed_frames = call(
        pack_body, [((2 * rows + 16, part), BF16)], idx, tokens, cotangent, layer_gains
    )[0]
    blocks_whole = features_whole(packed_frames)
    one, one_mark = gathered(idx, jnp.concatenate([first_expand, first_shrink.T], axis=1))
    x0, cot, gains = call(
        features_body,
        [((rows, features), BF16), ((rows, features), BF16), ((5, features), F32)],
        idx,
        *blocks_whole,
    )
    bias = position_bias.reshape(2, local)
    params = jnp.stack([batch_scale, batch_shift])
    tables = angle_tables(ctx_at * rows, rows, width, features)
    thirds = [attend_input[:, at] for at in range(3)]
    two, two_mark = gathered(
        idx,
        jnp.concatenate(thirds + [position_map, attend_output.T], axis=1),
        [one_mark, blocks_whole[1], blocks_whole[2]],
    )
    halves_in = [gating_map[:, at] for at in range(2)]
    three, three_mark = gathered(
        idx,
        jnp.concatenate(halves_in + [mixing_map.T, second_expand, second_shrink.T], axis=1),
        [one_mark],
        stepwise=True,
    )
    at_pos, at_out = 3 * local, 4 * local
    at_mix, at_two = 2 * channels, 3 * channels

    stream = ((rows, features), F32)
    packed = ((rows, features), BF16)
    piece = ((rows // 2, features), BF16)
    gain_row = ((1, features), F32)
    work = pltpu.VMEM((rows, features), F32)
    inner_shape = (rows, hidden)

    z1, u1, h1, keep, send = call(
        functools.partial(feed_body, 0, 0, False),
        [packed, (inner_shape, F32), (inner_shape, BF16), piece, piece],
        idx,
        x0,
        gains,
        one,
        scratch=[work],
    )
    t1, t2 = tp_end(idx, tp_begin(keep, send, idx, [two_mark]), [two])
    embed, relative = call(
        functools.partial(relative_body, at_pos),
        [((width, features), BF16), ((width, local), BF16)],
        idx,
        *tables,
        two,
    )
    per_head = ((rows, local), BF16)
    x1, z2, qa, qb, kv = call(
        attend_in_body,
        [stream, packed, per_head, per_head, ((rows, 2 * local), BF16)],
        idx,
        x0,
        t1,
        t2,
        gains,
        two,
        bias,
        after=[three_mark],
        scratch=[work],
    )
    if callable(three):
        three = three([kv])
    pairs = [kv] + [swap(kv, "ctx", step) for step in range(1, ctx)]
    position = call(
        functools.partial(position_body, heads),
        [((heads, rows, length), F32)],
        idx,
        qb,
        relative,
    )[0]
    whole_pairs = pltpu.VMEM((length, 2 * local), BF16)
    p, mixed, keep, send = call(
        functools.partial(attend_body, heads, ctx, at_out),
        [((heads, rows, length), BF16), per_head, piece, piece],
        idx,
        qa,
        *pairs,
        position,
        two,
        scratch=[whole_pairs, work],
    )
    t1, t2 = tp_end(idx, tp_begin(keep, send, idx, [three]))
    edge = ((HALO, channels), BF16)
    x2, z3, paired, glu, first, last = call(
        conv_in_body,
        [
            stream,
            packed,
            ((rows, 2 * channels), F32),
            ((rows, channels), BF16),
            edge,
            edge,
        ],
        idx,
        x1,
        t1,
        t2,
        gains,
        three,
        scratch=[work],
    )
    low, high = neighbours(first, last)
    padded = pltpu.VMEM((rows + 2 * HALO, channels), F32)
    c, stats = call(
        conv_body,
        [((rows, channels), F32), ((8, channels), F32)],
        idx,
        glu,
        low,
        high,
        depth_kernel,
        scratch=[padded],
    )
    stats = pooled(stats, rows)
    q, act, keep, send = call(
        functools.partial(batch_body, at_mix),
        [((rows, channels), F32), ((rows, channels), BF16), piece, piece],
        idx,
        c,
        stats,
        params,
        three,
        scratch=[work],
    )
    t1, t2 = tp_sum(keep, send)
    x3, z4, u2, h2, keep, send = call(
        functools.partial(feed_body, 3, at_two, True),
        [stream, packed, (inner_shape, F32), (inner_shape, BF16), piece, piece],
        idx,
        x2,
        t1,
        t2,
        gains,
        three,
        scratch=[work],
    )
    t1, t2 = tp_sum(keep, send)
    outputs, d4, gain_five, f4, du2, keep, send = call(
        functools.partial(final_body, at_two),
        [
            ((rows, part), BF16),
            stream,
            gain_row,
            packed,
            (inner_shape, BF16),
            piece,
            piece,
        ],
        idx,
        x3,
        t1,
        t2,
        gains,
        cot,
        u2,
        three,
        scratch=[work],
    )
    total = tp_begin(keep, send)
    rear = products(idx, [(z4, du2), (f4, h2)])
    t1, t2 = tp_end(idx, total, [rear[0]])
    d3, f3, da, edges, gain_four = call(
        functools.partial(conv_back_body, at_mix),
        [
            stream,
            packed,
            ((rows, channels), F32),
            ((8 + 4 * HALO, channels), F32),
            gain_row,
        ],
        idx,
        x3,
        d4,
        t1,
        t2,
        gains,
        q,
        params,
        three,
        scratch=[work],
    )
    sums, near, far = edges_summed(edges)
    rear_other = across(idx, rear)
    counted = rows * lax.axis_size(FRAMES)
    dc, dg, keep, send = call(
        functools.partial(gate_back_body, ctx, counted),
        [
            ((rows, channels), BF16),
            ((rows, 2 * channels), BF16),
            piece,
            piece,
        ],
        idx,
        da,
        q,
        sums,
        near,
        far,
        stats,
        params,
        depth_kernel,
        paired,
        three,
        after=[rear_other],
        scratch=[padded, work],
    )
    total = tp_begin(keep, send)
    kernel_grad = call(
        taps_body,
        [(depth_kernel.shape, F32)],
        idx,
        glu,
        low,
        high,
        dc,
        scratch=[padded],
    )[0]
    middle = products(idx, [(z3, dg), (f3, act)])
    t1, t2 = tp_end(idx, total, [middle[0], kernel_grad])
    pair_block = ((rows, 2 * local), BF16)
    results = call(
        functools.partial(attend_back_body, heads, ctx, at_out),
        [stream, packed, gain_row, ((heads, rows, length), BF16), ((rows, local), F32)]
        + [pair_block] * ctx,
        idx,
        x2,
        d3,
        t1,
        t2,
        gains,
        two,
        p,
        qa,
        *pairs,
        scratch=[whole_pairs, whole_pairs, pltpu.VMEM((rows, local), BF16), work],
    )
    d2, f2, gain_three, ds, dqa = results[:5]
    pair_grads = [results[5]] + [
        swap(block, "ctx", step + 1) for step, block in enumerate(results[6:])
    ]
    dqb, dr = call(
        functools.partial(position_back_body, heads),
        [((rows, local), F32), ((width, local), BF16)],
        idx,
        ds,
        qb,
        relative,
        scratch=[pltpu.VMEM((BLOCK, length + BLOCK), F32), pltpu.VMEM((width, local), F32)],
    )
    middle_other = across(idx, middle, [ds])
    dp, bias_grad, keep, send = call(
        functools.partial(attend_out_body, ctx),
        [((rows, 3 * local), BF16), ((2, local), F32), piece, piece],
        idx,
        dqa,
        dqb,
        *pair_grads,
        two,
        after=[middle_other],
        scratch=[work],
    )
    total = tp_begin(keep, send)
    inner = products(idx, [(z2, dp), (embed, dr), (f2, mixed)])
    rear_total, rear_rest = along_halves(idx, rear, rear_other, [total])
    t1, t2 = tp_end(idx, total, [inner[0], rear_total])
    inner_other = across(idx, inner)
    d1, f1, du1, gain_two, keep, send = call(
        feed_back_body,
        [stream, ((rows, features), BF16), (inner_shape, BF16), gain_row, piece, piece],
        idx,
        x1,
        d2,
        t1,
        t2,
        gains,
        u1,
        one,
        scratch=[work],
    )
    front = products(idx, [(z1, du1), (f1, h1)])
    total = tp_begin(keep, send, idx, [front[0]])
    front_other = across(idx, front)
    inner_total, inner_parts = along(idx, [inner, middle], [inner_other, middle_other], [total])
    rear_total, rear_parts = rear_rest([inner_total])
    t1, t2 = tp_end(idx, total, [inner_total])
    taps = depth_kernel.shape[0]
    tokens_grad, small = call(
        last_body,
        [((rows, part), F32), ((-(-(7 + taps) // 8) * 8, part), F32)],
        idx,
        x0,
        d1,
        t1,
        t2,
        gains,
        gain_two,
        gain_three,
        gain_four,
        gain_five,
        bias_grad,
        kernel_grad,
        after=[rear_total],
        scratch=[work, pltpu.VMEM((8, features), F32)],
    )
    steps = [
        (axis, step)
        for axis in ("fsdp", "ctx")
        for step in (1, 2, 4, 8)
        if step < lax.axis_size(axis)
    ]
    small = small + swap(small, *steps[0])
    front_total, front_parts = along(idx, [front], [front_other], [small])
    for axis, step in steps[1:-1]:
        small = small + swap(small, axis, step)
    rear_expand, rear_shrink = finish(
        idx, rear_parts, [("rows", 1, hidden), ("turned", 1, hidden)], [front_total]
    )
    qkv_grad, map_grad, out_grad, gate_grad, mix_grad = finish(
        idx,
        inner_parts,
        [
            ("middle", 3, 3 * local),
            ("rows", 1, local),
            ("turned", 1, local),
            ("middle", 2, 2 * channels),
            ("turned", 1, channels),
        ],
        [front_total],
    )
    gains_grad, bias_grad, kernel_grad = call(
        finish_small_body,
        [((5, part), F32), ((2, heads, size), F32), ((taps, channels), F32)],
        idx,
        small,
        swap(small, *steps[-1]),
        results=True,
    )
    front_expand, front_shrink = finish(
        idx, front_parts, [("rows", 1, hidden), ("turned", 1, hidden)]
    )
    return (
        outputs,
        tokens_grad,
        front_expand,
        front_shrink,
        qkv_grad,
        map_grad,
        bias_grad,
        out_grad,
        gate_grad,
        kernel_grad,
        sums[0],
        sums[1],
        mix_grad,
        rear_expand,
        rear_shrink,
        gains_grad,
    )


def solution(mesh):
    frames = ("fsdp", "ctx")
    rows, columns = P(frames, "tp"), P("tp", frames)
    three_dims, last_only, one_dim = P(frames, None, "tp"), P(None, "tp"), P("tp")
    heads = P(None, "tp", None)
    return jax.shard_map(
        shards,
        mesh=mesh,
        in_specs=(
            rows,
            rows,
            columns,
            three_dims,
            rows,
            heads,
            columns,
            three_dims,
            last_only,
            one_dim,
            one_dim,
            columns,
            rows,
            columns,
            last_only,
            rows,
        ),
        out_specs=(
            rows,
            rows,
            rows,
            columns,
            three_dims,
            rows,
            heads,
            columns,
            three_dims,
            last_only,
            one_dim,
            one_dim,
            columns,
            rows,
            columns,
            last_only,
        ),
        check_vma=False,
    )
```
